128 devices in a mesh: lat: 8 (over x, z_lo), lon: 16 (over z_hi, y, core).
Axes of the slice: x: 4, y: 4, z: 4 (z_hi: 2, z_lo: 2; z = z_hi * 2 + z_lo), core: 2. Of those that a mesh axis runs over, the one named last changes fastest.
Arguments:
- initial_state: bfloat16 [192, 384, 512], P('lat', 'lon'), may hold values from -6 to 6
- norm_gain: float32 [512], replicated, may hold values from 0.1 to 1.9
- input_weight: bfloat16 [512, 1536], replicated, may hold values from -2 to 2
- output_weight: bfloat16 [512, 512], replicated, may hold values from -0.25 to 0.25
- obs_in_weight: bfloat16 [512, 1024], replicated, may hold values from -0.25 to 0.25
- obs_out_weight: bfloat16 [1024, 256], replicated, may hold values from -0.1875 to 0.1875
- observed: bfloat16 [65536, 256], P(('lat', 'lon')), may hold values from -6 to 6
- error_scale: float32 [256], replicated, may hold values from 0.5 to 2
- foot_tile: int32 [65536, 1], P(('lat', 'lon')), may hold values from 0 to 127; in each aligned block of 512 rows (0 to 511, 512 to 1023, ...) at most 8 rows name the same one
- foot_cell: int32 [65536], P(('lat', 'lon')), may hold values from 0 to 575
- foot_count: int32 [128], P(('lat', 'lon')), may hold values from 1 to 512, 49152 in all
Outputs:
- gradient: float32 [192, 384, 512], P('lat', 'lon')
- misfit: float32 [65536], P(('lat', 'lon'))
The draws below stay inside these ranges and needn't reach their ends.
Inputs may be any that keep to these rules, and one draw needn't show every extreme that they name: `foot_tile`: among the 512 footprints of one device at most 8 name the same tile. `foot_count`: the live footprints are the first slots of a device; the counts sum to 49152, and some device has all 512 live.
All inputs are finite; a program needn't handle non-finite values.
Results may differ from the reference program's by a relative error of at most 0.02.
The reference program's roundings to bfloat16 on the way count: a program that leaves them out, or rounds other values in their place, can miss the bound.
Values may be sent and summed in bfloat16 or wider, within the bound.
A program may use at most 128 MiB of HBM per device.

```python
import math
import jax
import jax.numpy as jnp
import numpy as np
from jax import lax

D = 512
HEADS = 8
WIN = 12
CH = 256
OBS_HID = 1024
CLAT = 24
CLON = 24
FP_DEV = 512
NLAT = 192
NLON = 384
NFOOT = 65536
CAP = 8
LIVE = 49152
N_LON = 16
DEVICES = 128


def draw_input_weight(key, part):
    key = jax.random.fold_in(key, 11)
    base_key = jax.random.fold_in(key, 1)
    base = jax.random.truncated_normal(base_key, -4.0, 4.0, (D, 3 * D), jnp.float32) / math.sqrt(D)
    return jnp.clip(base, -2.0, 2.0).astype(jnp.bfloat16)


def with_ends(entries, stream_key, low, largest):
    longest = entries.shape.index(max(entries.shape))
    spots = []
    for shift in (0, 1):
        where = [jax.random.randint(jax.random.fold_in(stream_key, axis), (), 0, length) for axis, length in enumerate(entries.shape)]
        where[longest] = (where[longest] + shift) % entries.shape[longest]
        spots.append(tuple(where))
    return entries.at[spots[0]].set(low).at[spots[1]].set(largest)


def levels(rng, dims, cuts, least, largest):
    level = 1.0
    for position, blocks in cuts:
        draws = jax.random.uniform(jax.random.fold_in(jax.random.fold_in(rng, 6), position), (blocks,), jnp.float32, least / len(cuts), largest / len(cuts))
        level = level * jnp.repeat(jnp.exp(draws), dims[position] // blocks).reshape((-1,) + (1,) * (len(dims) - 1 - position))
    return level


def length_profile(count, total, limit, skew):
    portions = [(1 << 20) // math.isqrt(rank ** skew) + 1 for rank in range(2, count + 1)]
    surplus, counts = total - limit - (count - 1), [1] * (count - 1)
    while surplus > 0:
        free = [i for i in range(count - 1) if counts[i] < limit]
        mass, remaining = sum([portions[i] for i in free]), surplus
        for i in free:
            more = min(limit - counts[i], max(1, remaining * portions[i] // mass), surplus)
            counts[i] = counts[i] + more
            surplus = surplus - more
    return np.array([limit] + counts)


def uneven_parts(own_key, number_of, total, reach, skew):
    if number_of == 2:
        one = jax.random.randint(own_key, (), max(1, total - reach), min(reach, total - 1) + 1)
        return jnp.stack([one, total - one])
    tallies = jnp.asarray(length_profile(number_of, total, reach, skew), jnp.int32)
    twos = (number_of - 1) // 2
    giver, taker = tallies[1:1 + 2 * twos:2], tallies[2:2 + 2 * twos:2]
    margin = jnp.minimum(giver - 1, reach - taker)
    passed = jax.random.randint(jax.random.fold_in(own_key, 1), (twos,), 0, 1 << 20) % (margin + 1)
    tallies = tallies.at[1:1 + 2 * twos:2].set(giver - passed).at[2:2 + 2 * twos:2].set(taker + passed)
    return tallies[jax.random.permutation(jax.random.fold_in(own_key, 2), number_of)]


def assign_block(rng, own, number, rows, amount, top, most, lean):
    sequence = jax.random.permutation(rng, amount)
    packed, ordinary = load_shares(amount, rows * top, most, lean, True), load_shares(amount, rows * top, most, lean, False)
    places = jnp.arange(amount)

    def named(sizes, offset_by):
        used = int((sizes > 0).sum())
        fixed = max(1, used // 4)
        moved = fixed + (places - fixed + offset_by * (used - fixed)) % max(1, amount - fixed)
        return jnp.zeros((amount,), jnp.int32).at[sequence[jnp.where(places < fixed, places, moved)]].set(jnp.asarray(sizes, jnp.int32))

    sizes = jnp.where(number % 4 == 0, named(packed, number // 4), named(ordinary, number - number // 4 - 1))
    mixed = jax.random.permutation(jax.random.fold_in(own, 3), amount)
    giver, receiver = mixed[0:amount // 2 * 2:2], mixed[1:amount // 2 * 2:2]
    margin = jnp.minimum(sizes[giver] - 1, most - sizes[receiver]) // 2
    margin = jnp.where((giver == sequence[0]) | (receiver == sequence[0]) | (sizes[receiver] == 0), 0, jnp.maximum(margin, 0))
    moved = jax.random.randint(jax.random.fold_in(own, 4), (amount // 2,), 0, 1 << 20) % (margin + 1)
    sizes = sizes.at[giver].add(-moved).at[receiver].add(moved)
    items = jnp.searchsorted(jnp.cumsum(sizes), jnp.arange(rows * top), side="right").astype(jnp.int32)
    listing = items.reshape(top, rows).T
    listing = listing[jax.random.permutation(jax.random.fold_in(own, 1), rows)]
    offset_by = jax.random.randint(jax.random.fold_in(own, 2), (rows, 1), 0, top)
    return jnp.take_along_axis(listing, (jnp.arange(top)[None, :] + offset_by) % top, axis=1)


def load_shares(count, total, most, lean, full):
    weights = [(1 << 20) // math.isqrt(grade ** lean) + 1 for grade in range(1, count + 1)]
    largest = most if full else min(most, max(-(-total // count), total * weights[0] // sum(weights)))
    least = 1 if total - largest >= count - 1 else 0
    holding, rest = [largest] + [least] * (count - 1), total - largest - least * (count - 1)
    while rest > 0:
        candidates = [i for i in range(1, count) if holding[i] < largest] or [i for i in range(1, count) if holding[i] < most]
        pool, left = sum([weights[i] for i in candidates]), rest
        for i in candidates:
            extra = min(most - holding[i], max(1, left * weights[i] // pool), rest)
            holding[i] = holding[i] + extra
            rest = rest - extra
    return np.array(holding)


def normal_values(own_key, shape, spread, bound, cuts=(), kind=jnp.bfloat16):
    result = spread * jax.random.normal(own_key, shape, jnp.float32)
    if cuts:
        result = result * levels(own_key, shape, cuts, -0.22, 0.18)
    return jnp.clip(result, -bound, bound).astype(kind)


def setup_inputs(seed: int = 0) -> dict:
    splits = jax.random.split(jax.random.key(seed), 12)
    initial_state = normal_values(splits[0], (NLAT, NLON, D), 1.0, 6.0, ((0, 8), (1, 16)))
    norm_gain = jnp.clip(1.0 + 0.18 * jax.random.normal(splits[1], (D,), jnp.float32), 0.1, 1.9)
    input_weight = draw_input_weight(jax.random.fold_in(splits[11], 71), 0)
    output_weight = normal_values(splits[3], (D, D), D ** -0.5, 0.25)
    obs_in_weight = normal_values(splits[4], (D, OBS_HID), D ** -0.5, 0.25)
    obs_out_weight = normal_values(splits[5], (OBS_HID, CH), OBS_HID ** -0.5, 0.1875)
    observed = normal_values(splits[6], (NFOOT, CH), 1.0, 6.0, ((0, 128),))
    error_scale = jnp.clip(jnp.exp(jax.random.uniform(splits[7], (CH,), jnp.float32, math.log(0.5), math.log(2.0))), 0.5, 2.0)
    foot_tile_keys = jax.random.split(jax.random.fold_in(splits[8], 1), NFOOT // FP_DEV)
    foot_tile_turns = jax.random.permutation(jax.random.fold_in(splits[8], 3), NFOOT // FP_DEV)
    foot_tile = jax.vmap(lambda own, number: assign_block(jax.random.fold_in(splits[8], 2), own, number, FP_DEV, DEVICES, 1, CAP, 2))(foot_tile_keys, foot_tile_turns).reshape((NFOOT, 1))
    foot_cell = with_ends(jax.random.randint(splits[9], (NFOOT,), 0, CLAT * CLON), jax.random.fold_in(splits[9], 1), 0, (CLAT * CLON) - 1).astype(jnp.int32)
    foot_count = uneven_parts(splits[10], DEVICES, LIVE, FP_DEV, 2).astype(jnp.int32)
    return {"initial_state": initial_state, "norm_gain": norm_gain, "input_weight": input_weight, "output_weight": output_weight, "obs_in_weight": obs_in_weight, "obs_out_weight": obs_out_weight, "observed": observed, "error_scale": error_scale, "foot_tile": foot_tile, "foot_cell": foot_cell, "foot_count": foot_count}


norm_eps = 1e-06

def split_heads(window_block, parts):
    rows, cols, chans = window_block.shape
    nwin = cols // rows
    depth = chans // (parts * HEADS)
    shaped = window_block.reshape(rows, nwin, rows, parts, HEADS, depth)
    return shaped.transpose(1, 3, 4, 0, 2, 5).reshape(nwin, parts, HEADS, rows * rows, depth)

def merge_heads(windows, rows):
    nwin, parts, heads, length, depth = windows.shape
    shaped = windows.reshape(nwin, parts, heads, rows, rows, depth)
    return shaped.transpose(3, 0, 4, 1, 2, 5).reshape(rows, nwin * rows, parts * heads * depth)

def softmax_weights(queries, keys, row_valid):
    depth = queries.shape[-1]
    scores = jnp.einsum('nhqe,nhke->nhqk', queries, keys) / math.sqrt(depth)
    key_valid = jnp.repeat(row_valid, WIN)
    scores = jnp.where(key_valid[None, None, None, :], scores, jnp.float32(-1e+30))
    top = lax.optimization_barrier(jnp.max(scores, axis=-1, keepdims=True))
    expo = jnp.exp(scores - top)
    return expo / lax.optimization_barrier(jnp.sum(expo, axis=-1, keepdims=True))

def round_probs(probs):
    held = lax.optimization_barrier(probs.astype(jnp.bfloat16))
    return held.astype(jnp.float32)

def band_forward(pieces):
    window_block, row_valid = pieces
    split = split_heads(window_block, 3).astype(jnp.float32)
    queries, keys, values = (split[:, 0], split[:, 1], split[:, 2])
    probs = softmax_weights(queries, keys, row_valid)
    attended = jnp.einsum('nhqk,nhke->nhqe', round_probs(probs), values).astype(jnp.bfloat16)
    return merge_heads(attended[:, None], WIN)

def band_backward(pieces):
    window_block, grad_block, row_valid = pieces
    split = split_heads(window_block, 3).astype(jnp.float32)
    queries, keys, values = (split[:, 0], split[:, 1], split[:, 2])
    upstream = split_heads(grad_block, 1)[:, 0].astype(jnp.float32)
    depth = queries.shape[-1]
    probs = softmax_weights(queries, keys, row_valid)
    value_grad = jnp.einsum('nhqk,nhqe->nhke', round_probs(probs), upstream)
    prob_grad = jnp.einsum('nhqe,nhke->nhqk', upstream, values)
    inner = lax.optimization_barrier(jnp.sum(probs * prob_grad, axis=-1, keepdims=True))
    score_grad = (probs * (prob_grad - inner) / math.sqrt(depth)).astype(jnp.bfloat16)
    held = lax.optimization_barrier(score_grad).astype(jnp.float32)
    query_grad = jnp.einsum('nhqk,nhke->nhqe', held, keys)
    key_grad = jnp.einsum('nhqk,nhqe->nhke', held, queries)
    stacked = jnp.stack([query_grad.astype(jnp.bfloat16), key_grad.astype(jnp.bfloat16), value_grad.astype(jnp.bfloat16)], axis=1)
    return merge_heads(stacked, WIN)

def observe(features, obs_values, live, error_scale, obs_in_weight, obs_out_weight):
    pre = jnp.dot(features, obs_in_weight, preferred_element_type=jnp.float32)
    sigmoid_pre = jax.nn.sigmoid(pre)
    hidden = (pre * sigmoid_pre).astype(jnp.bfloat16)
    predicted = jnp.dot(hidden, obs_out_weight, preferred_element_type=jnp.float32)
    scaled_res = (predicted - obs_values.astype(jnp.float32)) / error_scale
    misfit = 0.5 * live * lax.optimization_barrier(jnp.sum(scaled_res * scaled_res, axis=-1))
    pred_grad = (live[:, None] * scaled_res / error_scale).astype(jnp.bfloat16)
    hidden_grad = jnp.dot(pred_grad, obs_out_weight.T, preferred_element_type=jnp.float32)
    pre_grad = (hidden_grad * sigmoid_pre * (1.0 + pre * (1.0 - sigmoid_pre))).astype(jnp.bfloat16)
    foot_grad = jnp.dot(pre_grad, obs_in_weight.T, preferred_element_type=jnp.float32).astype(jnp.bfloat16)
    return (misfit, foot_grad)

def reference(initial_state, norm_gain, input_weight, output_weight, obs_in_weight, obs_out_weight, observed, error_scale, foot_tile, foot_cell, foot_count):
    grid_rows, grid_cols, channels = initial_state.shape
    cell_total = grid_rows * grid_cols
    half_win = WIN // 2
    band_count = (grid_rows + 2 * half_win) // WIN
    state_f32 = initial_state.astype(jnp.float32).reshape(cell_total, channels)
    inv_rms = lax.rsqrt(lax.optimization_barrier(jnp.mean(state_f32 * state_f32, axis=-1, keepdims=True)) + norm_eps)
    normed = (state_f32 * inv_rms * norm_gain).astype(jnp.bfloat16)
    projected = jnp.dot(normed, input_weight, preferred_element_type=jnp.float32).astype(jnp.bfloat16)
    projected = projected.reshape(grid_rows, grid_cols, 3 * channels)

    def to_windows(field):
        padded = jnp.pad(field, ((half_win, half_win), (0, 0), (0, 0)))
        rolled = jnp.roll(padded, half_win, axis=1)
        return rolled.reshape(band_count, WIN, grid_cols, field.shape[2])

    def from_windows(bands):
        whole = bands.reshape(band_count * WIN, grid_cols, bands.shape[3])[half_win:half_win + grid_rows]
        return jnp.roll(whole, -half_win, axis=1)
    row_index = jnp.arange(grid_rows + 2 * half_win, dtype=jnp.int32)
    row_valid = ((row_index >= half_win) & (row_index < half_win + grid_rows)).reshape(band_count, WIN)
    proj_bands = to_windows(projected)
    attended = from_windows(lax.map(band_forward, (proj_bands, row_valid))).reshape(cell_total, channels)
    block_out = (state_f32 + jnp.dot(attended, output_weight, preferred_element_type=jnp.float32)).astype(jnp.bfloat16)
    foot_total = observed.shape[0]
    source_dev = foot_tile[:, 0]
    lat_tile = source_dev // N_LON
    lon_tile = source_dev % N_LON
    grid_index = ((lat_tile * CLAT + foot_cell // CLON) * grid_cols + lon_tile * CLON + foot_cell % CLON).astype(jnp.int32)
    features = block_out[grid_index]
    slot_index = jnp.arange(foot_total, dtype=jnp.int32)
    owner_dev = slot_index // FP_DEV
    live = (slot_index % FP_DEV < foot_count[owner_dev]).astype(jnp.float32)
    misfit, foot_grad = observe(features, observed, live, error_scale, obs_in_weight, obs_out_weight)
    state_grad = jnp.zeros((cell_total, channels), jnp.float32).at[grid_index].add(foot_grad.astype(jnp.float32))
    attended_grad = jnp.dot(state_grad.astype(jnp.bfloat16), output_weight.T, preferred_element_type=jnp.float32).astype(jnp.bfloat16)
    grad_bands = to_windows(attended_grad.reshape(grid_rows, grid_cols, channels))
    proj_grad = from_windows(lax.map(band_backward, (proj_bands, grad_bands, row_valid)))
    normed_grad = jnp.dot(proj_grad.reshape(cell_total, 3 * channels), input_weight.T, preferred_element_type=jnp.float32)
    scaled = norm_gain * normed_grad
    inner = lax.optimization_barrier(jnp.mean(state_f32 * scaled, axis=-1, keepdims=True))
    gradient = state_grad + inv_rms * scaled - state_f32 * inv_rms * inv_rms * inv_rms * inner
    return (gradient.reshape(grid_rows, grid_cols, channels), misfit)
```

```python
import functools

import jax
import jax.numpy as jnp
import numpy as np
from jax import lax
from jax.experimental import pallas as pl
from jax.experimental.pallas import tpu as pltpu
from jax.sharding import PartitionSpec as P

HEADS = 8
WIN = 12
HALF = WIN // 2
SIDE = 2 * WIN
CELLS = SIDE * SIDE
AREA = WIN * WIN
STRIP = HALF * SIDE
MAIN = 128
LATE = AREA - MAIN
SRC = 384
NORM_EPS = 1e-06
MESH = pl.DeviceIdType.MESH
BF = jnp.bfloat16
F32 = jnp.float32

WINDOWS = ((1, 0), (0, 1), (0, 0), (1, 1))
REACH = 3 * STRIP
ACROSS = SIDE - HALF
SIDES, CORNER = 112, 48
LEFT, TOP, TL = 0, SIDES, 2 * SIDES
MARGIN = 2 * SIDES + CORNER
PIECES = ((LEFT, SIDES, 0, 1), (TOP, SIDES, 1, 0), (TL, CORNER, 1, 1))
SOURCES = (
    ((True, 144, 288), (False, LEFT + 32, 80), (True, 0, 16)),
    ((True, 0, 272), (False, TOP, SIDES)),
    ((True, 0, 176), (False, TOP, SIDES), (False, LEFT, 48), (False, TL, CORNER)),
    ((True, 144, 288), (True, 0, 96)),
)
TARGETS = (
    (0, STRIP, (1, 2)),
    (STRIP, 2 * STRIP, (0, 3)),
    (REACH + LEFT, SIDES, (0, 2)),
    (REACH + TOP, SIDES, (1, 2)),
    (REACH + TL, CORNER, (2,)),
)


def place_of(row, col):
    if row >= 0 and col >= 0:
        return True, row * SIDE + col
    if col >= 0:
        return False, TOP + (row + HALF) * ACROSS + col
    if row >= 0:
        return False, LEFT + row * HALF + col + HALF
    return False, TL + (row + HALF) * HALF + col + HALF


def selectors():
    pack = np.zeros((MARGIN, CELLS), np.float32)
    for a in range(HALF):
        for b in range(ACROSS):
            pack[LEFT + b * HALF + a, b * SIDE + ACROSS + a] = 1
            pack[TOP + a * ACROSS + b, (ACROSS + a) * SIDE + b] = 1
        for b in range(HALF):
            pack[TL + a * HALF + b, (ACROSS + a) * SIDE + ACROSS + b] = 1
    gather = np.zeros((4, AREA, SRC), np.float32)
    spread = np.zeros((4, REACH + MARGIN, AREA), np.float32)
    spread_q = np.zeros((4, REACH + MARGIN, 2 * MAIN), np.float32)
    for w, (i, j) in enumerate(WINDOWS):
        where = {}
        at = 0
        for own, first, rows in SOURCES[w]:
            for row in range(rows):
                where.setdefault((own, first + row), at + row)
            at += rows
        for a in range(WIN):
            for b in range(WIN):
                own, spot = place_of(WIN * i - HALF + a, WIN * j - HALF + b)
                cell = a * WIN + b
                gather[w, cell, where[own, spot]] = 1
                to = spot if own else REACH + spot
                spread[w, to, cell] = 1
                for h in range(HEADS if cell >= MAIN else 1):
                    spread_q[w, to, cell + h * LATE] = 1
    return pack, gather, spread, spread_q


def nn(a, b):
    return jnp.dot(a, b, preferred_element_type=F32)


def nt(a, b):
    return lax.dot_general(a, b, (((1,), (1,)), ((), ())), preferred_element_type=F32)


def iota(shape, dim):
    return lax.broadcasted_iota(jnp.int32, shape, dim)


def normalize(x_ref, gain, into):
    step = 48 if x_ref.shape[0] % 48 == 0 else 16
    for first in range(0, x_ref.shape[0], step):
        here = pl.ds(first, step)
        x = x_ref[here, :].astype(F32)
        rms = lax.rsqrt(jnp.mean(x * x, axis=-1, keepdims=True) + NORM_EPS)
        into[here, :] = (x * rms * gain).astype(BF)


def each(first, last, act):
    def one(step, carry):
        act(step)
        return carry

    lax.fori_loop(first, last, one, 0)


def start(copies):
    for copy in copies:
        copy.start()


def wait(copies):
    for copy in copies:
        copy.wait()


class Links:
    def __init__(self, lats, lons, margin_sem, foot_sem, line_sem):
        self.lats, self.lons, self.n = lats, lons, lats * lons
        self.lat, self.lon = lax.axis_index("lat"), lax.axis_index("lon")
        self.margin_sem, self.foot_sem, self.line_sem = margin_sem, foot_sem, line_sem
        self.barrier = pltpu.get_barrier_semaphore()

    def around(self, up, right):
        lats, lons = self.lats, self.lons
        return lax.rem(self.lat + up + lats, lats), lax.rem(self.lon + right + lons, lons)

    def away_by(self, d):
        return self.around(d // self.lons, d % self.lons)

    def signal(self, sem, device):
        pl.semaphore_signal(sem, inc=1, device_id=device, device_id_type=MESH)

    def greet(self):
        for step in range(1, self.lats):
            self.signal(self.barrier, self.around(step, 0))
        for step in range(1, self.lons):
            self.signal(self.barrier, self.around(0, step))

    def met(self):
        pl.semaphore_wait(self.barrier, self.lats - 1 + self.lons - 1)
        for step in range(1, self.lats):
            self.signal(self.line_sem, self.around(step, 0))
        pl.semaphore_wait(self.line_sem, self.lats - 1)

    def copy(self, sems, i, src, dst, device):
        return pltpu.make_async_remote_copy(
            src_ref=src,
            dst_ref=dst,
            send_sem=sems.at[2 * i],
            recv_sem=sems.at[2 * i + 1],
            device_id=device,
            device_id_type=MESH,
        )

    def pieces(self, base, src, into, way):
        return [
            self.copy(
                self.margin_sem,
                base + i,
                src.at[pl.ds(first, rows)],
                into.at[pl.ds(first, rows)],
                self.around(way * up, way * right),
            )
            for i, (first, rows, up, right) in enumerate(PIECES)
        ]

    def arrived(self, into, i, parts):
        rest = into.at[pl.ds(1, parts - 1)]
        self.copy(self.foot_sem, i, rest, rest, self.around(1, 0)).wait()

    def to_all(self, send, into, i):
        def one(d):
            self.copy(self.foot_sem, i, send.at[d], into.at[d], self.away_by(d)).start()

        steps = (self.n - 1) // 7

        def seven(k, carry):
            for j in range(7):
                one(1 + 7 * k + j)
            return carry

        lax.fori_loop(0, steps, seven, 0)
        for d in range(1 + 7 * steps, self.n):
            one(d)
        into[0] = send[0]

    def along_lon(self, send, into, i, way):
        for step in range(1, self.lons):
            device = self.around(0, way * step)
            self.copy(self.foot_sem, i, send.at[:, step], into.at[step], device).start()
        into[0] = send[:, 0]

    def along_lat(self, send, into, i, way):
        for step in range(1, self.lats):
            device = self.around(way * step, 0)
            self.copy(self.foot_sem, i, send.at[:, step], into.at[step], device).start()
        into[0] = send[:, 0]


def footprint_places(links, tile_id, count, cap):
    lats, lons, n = links.lats, links.lons, links.n
    feet = tile_id.shape[1]
    tile_lat = jnp.floor((tile_id[...].astype(F32) + 0.5) * (1.0 / lons)).astype(jnp.int32)
    up, right = tile_lat - links.lat, tile_id[...] - tile_lat * lons - links.lon
    up, right = jnp.where(up < 0, up + lats, up), jnp.where(right < 0, right + lons, right)
    away = up * lons + right
    live = iota((1, feet), 1) < count[...]
    named = (iota((n, feet), 0) == away).astype(F32)
    before = (iota((feet, feet), 0) < iota((feet, feet), 1)).astype(F32).astype(BF)
    rank = jnp.sum(nn(named.astype(BF), before) * named, axis=0, keepdims=True).astype(jnp.int32)
    return away, rank, live, named


class Heads:
    def __init__(self, chans):
        self.even = (iota((1, 128), 1) < 64).astype(F32).astype(BF)
        self.odd = (iota((1, 128), 1) >= 64).astype(F32).astype(BF)
        self.eye = (iota((128, 128), 0) == iota((128, 128), 1)).astype(F32).astype(BF)
        late_head = iota((MAIN, chans), 0) >> 4 == iota((MAIN, chans), 1) >> 6
        self.late_head = late_head.astype(F32).astype(BF)
        head_late = iota((chans, MAIN), 0) >> 6 == iota((chans, MAIN), 1) >> 4
        self.head_late = head_late.astype(F32)

    def stacked(self, x):
        return jnp.concatenate([x * self.even, x * self.odd], axis=0)

    def late_rows(self, x):
        return jnp.concatenate([x] * HEADS, axis=0) * self.late_head

    def turned(self, qkv, w, first):
        return [
            nt(self.eye, pair_of(qkv, w, first, AREA, pair)).astype(BF)
            for pair in range(HEADS // 2)
        ]


def pair_of(ref, w, first, rows, pair):
    return ref[w, 0:rows, first + 128 * pair : first + 128 * (pair + 1)]


def gather_window(source, w, tile_ref, margin_ref):
    at = 0
    for own, first, count_rows in SOURCES[w]:
        piece = (tile_ref if own else margin_ref)[pl.ds(first, count_rows), :]
        source[w, pl.ds(at, count_rows), :] = piece
        at += count_rows


RETURNED = tuple(
    [(SIDE * row + ACROSS, HALF, LEFT + HALF * row) for row in range(ACROSS)]
    + [(REACH + SIDE * row, ACROSS, TOP + ACROSS * row) for row in range(HALF)]
    + [(REACH + SIDE * row + ACROSS, HALF, TL + HALF * row) for row in range(HALF)]
)


def to_targets(selector, per_window, which):
    first, count_rows, windows = TARGETS[which]
    total = None
    for w in windows:
        part = per_window(selector[w, pl.ds(first, count_rows), :], w)
        total = part if total is None else total + part
    return total


def kernel(
    lats,
    lons,
    cap,
    state_hbm,
    gain,
    w_in_hbm,
    w_out_hbm,
    obs_in_hbm,
    obs_out_hbm,
    observed_hbm,
    scale,
    tile_id,
    cell_id,
    count,
    pack_hbm,
    gather_hbm,
    spread_hbm,
    spread_q_hbm,
    own_part_hbm,
    back_part_hbm,
    misfit,
    state,
    observed,
    pack_m,
    w_in,
    w_out,
    obs_in,
    obs_out,
    gather_m,
    spread_m,
    spread_q_m,
    packed,
    margin,
    own_n,
    margin_n,
    source,
    win,
    qkv,
    apart,
    probs,
    att_t,
    att_send,
    att_recv,
    attended,
    block_out,
    obs_send,
    obs_recv,
    idx_send,
    idx_mid,
    idx_recv,
    mis_send,
    mis_mid,
    mis_recv,
    chosen,
    silu_grad,
    hidden,
    predicted,
    residuals,
    foot_grad,
    onehot,
    back,
    back_packed,
    state_grad,
    att_grad,
    packed_g,
    margin_g,
    dk_w,
    dv_w,
    dq_t,
    proj_grad,
    part_send,
    part_recv,
    own_part,
    margin_sem,
    foot_sem,
    fetch_sem,
    store_sem,
    line_sem,
):
    links = Links(lats, lons, margin_sem, foot_sem, line_sem)
    links.greet()
    n = links.n
    slots = n * cap
    feet = tile_id.shape[1]
    chans = state.shape[1]
    fetches = [
        pltpu.make_async_copy(src, dst, fetch_sem.at[i])
        for i, (src, dst) in enumerate(
            (
                (gather_hbm, gather_m),
                (w_in_hbm, w_in),
                (spread_q_hbm, spread_q_m),
                (w_out_hbm, w_out),
                (obs_in_hbm, obs_in),
                (obs_out_hbm, obs_out),
                (spread_hbm, spread_m),
                (state_hbm, state),
                (pack_hbm, pack_m),
                (observed_hbm, observed),
            )
        )
    ]
    start(fetches[7:])
    start(fetches[:7])
    fetches[7].wait()
    fetches[8].wait()

    packed[...] = nn(pack_m[...], state[...]).astype(BF)

    links.met()
    state_copies = links.pieces(0, packed, margin, 1)
    start(state_copies)

    away, rank, live, named = footprint_places(links, tile_id, count, cap)
    slot = jnp.where(live, away * cap + rank, -1)
    cell_value = (cell_id[...] + 1).astype(F32)
    on_lane = iota((4, cap, 128), 2) == iota((4, cap, 128), 1)
    cells = []
    for first in range(0, slots, 4 * cap):
        block = (iota((4 * cap, feet), 0) + first == slot).astype(F32)
        chosen[pl.ds(first, 4 * cap), :] = block.astype(BF)
        cell = jnp.sum(block * cell_value, axis=1, keepdims=True) - 1.0
        cell = jnp.where(on_lane, cell.reshape(4, cap, 1), 0.0)
        cells.append(jnp.sum(cell, axis=1, keepdims=True))
    idx_send[...] = jnp.concatenate(cells, axis=0).reshape(lats, lons, 1, 128)
    links.along_lon(idx_send, idx_mid, 0, 1)
    fetches[9].wait()
    rows = nn(chosen[...], observed[...])
    half = rows.shape[1] // 2
    rows = rows.reshape(n, cap, 2 * half)
    obs_send[...] = jnp.concatenate([rows[:, :, :half], rows[:, :, half:]], axis=1).astype(BF)

    links.to_all(obs_send, obs_recv, 1)

    normalize(state, gain[...], own_n)

    def place(windows):
        for w in windows:
            win[w] = nn(gather_m[w], source[w]).astype(BF)

    def project(first, last):
        cells = win[first:last].reshape((last - first) * AREA, chans)
        for part in range(3):
            cols = slice(part * chans, (part + 1) * chans)
            out = nn(cells, w_in[:, cols])
            out = (out * 0.125 if part == 0 else out).astype(BF)
            qkv[first:last, :, cols] = out.reshape(last - first, AREA, chans)

    heads = Heads(chans)

    def softmax(scores):
        e = jnp.exp(scores - jnp.max(scores, axis=0, keepdims=True))
        return e * (1.0 / jnp.sum(e, axis=0, keepdims=True))

    def forward(w):
        row = jnp.where((w == 1) | (w == 2), 0, 1)
        late = heads.late_rows(qkv[w, MAIN:AREA, 0:chans])
        values_t = heads.turned(qkv, w, 2 * chans)

        def scored(pair):
            if pair < HEADS // 2:
                queries = heads.stacked(pair_of(qkv, w, 0, MAIN, pair))
                return nt(pair_of(qkv, w, chans, AREA, pair), queries)
            return nt(qkv[w, :, chans : 2 * chans], late)

        after = scored(0)
        for pair in range(HEADS // 2):
            scores, after = after, scored(pair + 1)
            for h in range(2):
                lanes = slice(MAIN * h, MAIN * (h + 1))
                p = softmax(scores[:, lanes] + apart[row, :, lanes])
                probs[w, :, 256 * pair + MAIN * h : 256 * pair + MAIN * (h + 1)] = p
                at = 128 * pair + 64 * h
                out = nn(values_t[pair][64 * h : 64 * h + 64], p.astype(BF))
                att_t[w, at : at + 64, 0:MAIN] = out.astype(BF)
        p = softmax(after + apart[row, :, 2 * MAIN :])
        probs[w, :, MAIN * HEADS :] = p
        out = nn(jnp.concatenate(values_t, axis=0), p.astype(BF))
        att_t[w, :, MAIN : 2 * MAIN] = (out * heads.head_late).astype(BF)

    first_rows = jnp.where(links.lat == 0, AREA // 2, 0)
    lane = iota((AREA, 3 * MAIN), 1)
    query = jnp.where(lane < 2 * MAIN, lane & (MAIN - 1), MAIN)
    seen_apart = (iota((AREA, 3 * MAIN), 0) < first_rows) != (query < first_rows)
    apart[0] = jnp.where(seen_apart, -1e30, 0.0)
    apart[1] = jnp.zeros((AREA, 3 * MAIN), F32)

    def att_to(which):
        return to_targets(spread_q_m, lambda m, w: nt(m, att_t[w]), which)

    gather_window(source, 3, own_n, margin_n)
    fetches[0].wait()
    fetches[1].wait()
    place((3,))
    project(3, 4)
    wait(state_copies)
    normalize(margin, gain[...], margin_n)
    for w in range(3):
        gather_window(source, w, own_n, margin_n)
    place(range(3))
    project(0, 3)
    fetches[2].wait()
    links.arrived(idx_mid, 0, lons)
    links.along_lat(idx_mid, idx_recv, 3, 1)
    att_copies = links.pieces(3, att_send, att_recv, -1)

    def forward_step(w, carry):
        @pl.when(w == 3)
        def _():
            for which in (2, 3, 4):
                first, count_rows, _ = TARGETS[which]
                att_send[pl.ds(first - REACH, count_rows), :] = att_to(which).astype(BF)
            start(att_copies)

        forward(w)
        return carry

    lax.fori_loop(0, 4, forward_step, 0)
    for which in (0, 1):
        first, count_rows, _ = TARGETS[which]
        attended[pl.ds(first, count_rows), :] = att_to(which)

    links.arrived(idx_recv, 3, lats)
    on_lane = iota((n, cap, 128), 2) == iota((n, cap, 128), 1)
    spots = jnp.where(on_lane, idx_recv[...].reshape(n, 1, 128), 0.0)
    spots = jnp.sum(spots, axis=2, keepdims=True).reshape(slots, 1)
    pick = (iota((8, 128), 1) == 0).astype(F32)
    spots_row = lax.dot_general(
        pick,
        jnp.broadcast_to(spots, (slots, 128)),
        (((1,), (1,)), ((), ())),
        precision=lax.Precision.HIGHEST,
        preferred_element_type=F32,
    )[0:1].astype(jnp.int32)
    spots = spots.astype(jnp.int32)
    for first in range(0, slots, 32):
        block = iota((32, CELLS), 1) == spots[first : first + 32]
        onehot[pl.ds(first, 32), :] = block.astype(F32).astype(BF)
    for first in range(0, CELLS, 16):
        block = iota((16, slots), 0) + first == spots_row
        back[pl.ds(first, 16), :] = block.astype(F32).astype(BF)
    back_packed[...] = nn(pack_m[...], back[...]).astype(BF)
    chunk = slots // 2
    per_scale = 1.0 / scale[...]
    wait(fetches[3:7])
    wait(att_copies)
    returned = att_recv[...].astype(F32)
    for first, count_rows, at in RETURNED:
        attended[pl.ds(first, count_rows), :] = returned[at : at + count_rows]
    block_out[...] = (
        state[...].astype(F32) + nn(attended[...].astype(BF), w_out[...])
    ).astype(BF)

    step = min(chunk, 64)
    quarters = [slice(256 * i, 256 * (i + 1)) for i in range(obs_in.shape[1] // 256)]

    def predict(c, carry):
        base = pl.multiple_of(c * chunk, chunk)
        here = pl.ds(base, chunk)
        features = nn(onehot[here, :], block_out[...]).astype(BF)
        for cols in quarters:
            whole = nn(features, obs_in[:, cols])
            for first in range(0, chunk, step):
                pre = whole[first : first + step]
                sig = 0.5 + 0.5 * jnp.tanh(0.5 * pre)
                out = pre * sig
                some = pl.ds(base + first, step)
                hidden[some, cols] = out.astype(BF)
                silu_grad[some, cols] = sig + out * (1.0 - sig)
        predicted[here, :] = nn(hidden[here, :], obs_out[...])
        return carry

    def observe(c, carry):
        base = pl.multiple_of(c * chunk, chunk)
        here = pl.ds(base, chunk)
        lanes = iota((step // cap, cap, 128), 2) == iota((step // cap, cap, 128), 1)
        costs = []
        for first in range(0, chunk, step):
            seen = obs_recv[pl.ds(c * (n // 2) + first // cap, step // cap)].astype(F32)
            seen = jnp.concatenate(
                [seen[:, :cap].reshape(step, half), seen[:, cap:].reshape(step, half)], axis=1
            )
            some = pl.ds(base + first, step)
            residual = (predicted[some, :] - seen) * per_scale
            residuals[some, :] = (residual * per_scale).astype(BF)
            cost = 0.5 * jnp.sum(residual * residual, axis=1, keepdims=True)
            cost = jnp.where(lanes, cost.reshape(step // cap, cap, 1), 0.0)
            costs.append(jnp.sum(cost, axis=1, keepdims=True))
        blocks = pl.ds(c * (lats // 2), lats // 2)
        mis_send[blocks] = jnp.concatenate(costs, axis=0).reshape(lats // 2, lons, 1, 128)
        for cols in quarters:
            whole = nt(residuals[here, :], obs_out[cols, :])
            for first in range(0, chunk, step):
                some = pl.ds(base + first, step)
                grad = whole[first : first + step] * silu_grad[some, cols]
                hidden[some, cols] = grad.astype(BF)
        foot_grad[here, :] = nt(hidden[here, :], obs_in[...]).astype(BF)
        return carry

    lax.fori_loop(0, 2, predict, 0)
    links.arrived(obs_recv, 1, n)
    lax.fori_loop(0, 2, observe, 0)

    to_send = nn(back_packed[...], foot_grad[...]).astype(BF)
    packed_g[...] = nt(to_send, w_out[...]).astype(BF)
    grad_copies = links.pieces(6, packed_g, margin_g, 1)
    start(grad_copies)
    links.along_lon(mis_send, mis_mid, 2, -1)
    state_grad[...] = nn(back[...], foot_grad[...])
    att_grad[...] = nt(state_grad[pl.ds(0, REACH), :].astype(BF), w_out[...]).astype(BF)

    def scores_gradient(p, dp):
        inner = jnp.sum(p * dp, axis=0, keepdims=True)
        return (p * (dp - inner)).astype(BF)

    def backward(w):
        late_q = heads.late_rows(qkv[w, MAIN:AREA, 0:chans])
        late_up = heads.late_rows(win[w, MAIN:AREA, :])
        ups = [heads.stacked(pair_of(win, w, 0, MAIN, pair)) for pair in range(HEADS // 2)]

        def dp_of(pair):
            if pair == HEADS // 2:
                return None
            return nt(pair_of(qkv, w, 2 * chans, AREA, pair), ups[pair])

        after = dp_of(0)
        dp = nt(qkv[w, :, 2 * chans : 3 * chans], late_up)
        keys_t = heads.turned(qkv, w, chans)
        p = probs[w, :, MAIN * HEADS :]
        ds = scores_gradient(p, dp)
        late_dk = nn(ds, late_q)
        late_dv = nn(p.astype(BF), late_up)
        out = nn(jnp.concatenate(keys_t, axis=0), ds)
        dq_t[w, :, MAIN : 2 * MAIN] = (out * (heads.head_late * 0.125)).astype(BF)
        for pair in range(HEADS // 2):
            at = 128 * pair
            dp, after = after, dp_of(pair + 1)
            ds, rounded = [], []
            for h in range(2):
                p = probs[w, :, at * 2 + MAIN * h : at * 2 + MAIN * (h + 1)]
                ds.append(scores_gradient(p, dp[:, MAIN * h : MAIN * (h + 1)]))
                rounded.append(p.astype(BF))
                out = nn(keys_t[pair][64 * h : 64 * h + 64], ds[h])
                dq_t[w, at + 64 * h : at + 64 * h + 64, 0:MAIN] = (out * 0.125).astype(BF)
            dk = nn(
                jnp.concatenate(ds, axis=1), heads.stacked(pair_of(qkv, w, 0, MAIN, pair))
            )
            dv = nn(jnp.concatenate(rounded, axis=1), ups[pair])
            dk_w[w, :, at : at + 128] = (dk + late_dk[:, at : at + 128]).astype(BF)
            dv_w[w, :, at : at + 128] = (dv + late_dv[:, at : at + 128]).astype(BF)

    gather_window(source, 3, att_grad, margin_g)
    place((3,))

    def backward_step(step, carry):
        @pl.when(step == 1)
        def _():
            wait(grad_copies)
            for w in range(3):
                gather_window(source, w, att_grad, margin_g)
            place(range(3))

        @pl.when(step == 2)
        def _():
            links.arrived(mis_mid, 2, lons)
            links.along_lat(mis_mid, mis_recv, 4, -1)

        backward(lax.rem(step + 3, 4))
        return carry

    lax.fori_loop(0, 4, backward_step, 0)

    def project_back(targets):
        for which in targets:
            first, count_rows, _ = TARGETS[which]
            here = pl.ds(first, count_rows)
            proj_grad[here, 0:chans] = to_targets(
                spread_q_m, lambda m, w: nt(m, dq_t[w]), which
            ).astype(BF)
            proj_grad[here, chans : 2 * chans] = to_targets(
                spread_m, lambda m, w: nn(m, dk_w[w]), which
            ).astype(BF)
            proj_grad[here, 2 * chans : 3 * chans] = to_targets(
                spread_m, lambda m, w: nn(m, dv_w[w]), which
            ).astype(BF)

    def norm_part(first, rows, cells, into, more=None):
        whole = nt(proj_grad[pl.ds(first, rows), :], w_in[...])
        step = 48 if rows % 48 == 0 else 16
        for row in range(0, rows, step):
            here = pl.ds(row, step)
            g = gain[...] * whole[row : row + step]
            x = cells[here, :].astype(F32)
            rms = lax.rsqrt(jnp.mean(x * x, axis=-1, keepdims=True) + NORM_EPS)
            inner = jnp.mean(x * g, axis=-1, keepdims=True)
            out = rms * g - x * (rms * rms * rms * inner)
            into[here, :] = out.astype(BF) if more is None else more[here, :] + out

    project_back((2, 3, 4))
    norm_part(REACH, MARGIN, margin, part_send)
    part_copies = links.pieces(9, part_send, part_recv, -1)
    start(part_copies)
    project_back((0, 1))
    norm_part(0, REACH, state, own_part, state_grad)
    own_part[pl.ds(REACH, STRIP), :] = state_grad[pl.ds(REACH, STRIP), :]
    own_store = pltpu.make_async_copy(own_part, own_part_hbm, store_sem.at[0])
    own_store.start()

    links.arrived(mis_recv, 4, lats)
    costs = lax.dot_general(
        mis_recv[...].reshape(n, 128),
        named,
        (((0,), (0,)), ((), ())),
        precision=lax.Precision.HIGHEST,
        preferred_element_type=F32,
    )
    costs = jnp.where(iota((128, feet), 0) == rank, costs, 0.0)
    misfit[...] = jnp.where(live, jnp.sum(costs, axis=0, keepdims=True), 0.0)
    wait(part_copies)
    back_store = pltpu.make_async_copy(part_recv, back_part_hbm, store_sem.at[1])
    back_store.start()
    own_store.wait()
    back_store.wait()


def finish(own_part, back_part, costs, gradient, misfit):
    gradient[...] = own_part[...]
    returned = back_part[...].astype(F32)
    for first, count_rows, at in RETURNED:
        gradient[pl.ds(first, count_rows), :] += returned[at : at + count_rows]
    misfit[...] = costs[...]


def shards(
    lats,
    lons,
    initial_state,
    norm_gain,
    input_weight,
    output_weight,
    obs_in_weight,
    obs_out_weight,
    observed,
    error_scale,
    foot_tile,
    foot_cell,
    foot_count,
):
    n = lats * lons
    chans = initial_state.shape[-1]
    feet, seen = observed.shape
    cap = 2 * feet // n
    slots = n * cap
    pack, gather, spread, spread_q = (jnp.asarray(m, BF) for m in selectors())
    vmem, whole = pl.BlockSpec(memory_space=pltpu.VMEM), pl.BlockSpec(memory_space=pl.ANY)
    state = initial_state.reshape(CELLS, chans)
    gain = norm_gain.reshape(1, chans)
    tile_id = foot_tile.reshape(1, feet)
    count = foot_count.reshape(1, 1)
    limit = 60 * 1024 * 1024

    def shape(*dims, dtype=BF):
        return jax.ShapeDtypeStruct(dims, dtype)

    def room(*dims, dtype=BF):
        return pltpu.VMEM(dims, dtype)

    own_part, back_part, costs = pl.pallas_call(
        functools.partial(kernel, lats, lons, cap),
        out_shape=(
            shape(CELLS, chans, dtype=F32),
            shape(MARGIN, chans),
            shape(1, feet, dtype=F32),
        ),
        in_specs=[whole, vmem] + [whole] * 5 + [vmem] * 4 + [whole] * 4,
        out_specs=(whole, whole, vmem),
        scratch_shapes=[
            room(CELLS, chans),
            room(feet, seen),
            room(MARGIN, CELLS),
            room(*input_weight.shape),
            room(*output_weight.shape),
            room(*obs_in_weight.shape),
            room(*obs_out_weight.shape),
            room(*gather.shape),
            room(*spread.shape),
            room(*spread_q.shape),
            room(MARGIN, chans),
            room(MARGIN, chans),
            room(CELLS, chans),
            room(MARGIN, chans),
            room(4, SRC, chans),
            room(4, AREA, chans),
            room(4, AREA, 3 * chans),
            room(2, AREA, 3 * MAIN, dtype=F32),
            room(4, AREA, MAIN * (HEADS + 1), dtype=F32),
            room(4, chans, 2 * MAIN),
            room(MARGIN, chans),
            room(MARGIN, chans),
            room(CELLS, chans, dtype=F32),
            room(CELLS, chans),
            room(n, 2 * cap, seen // 2),
            room(n, 2 * cap, seen // 2),
            room(lats, lons, 1, 128, dtype=F32),
            room(lons, lats, 1, 128, dtype=F32),
            room(lats, lons, 1, 128, dtype=F32),
            room(lats, lons, 1, 128, dtype=F32),
            room(lons, lats, 1, 128, dtype=F32),
            room(lats, lons, 1, 128, dtype=F32),
            room(slots, feet),
            room(slots, obs_in_weight.shape[1], dtype=F32),
            room(slots, obs_in_weight.shape[1]),
            room(slots, seen, dtype=F32),
            room(slots, seen),
            room(slots, chans),
            room(slots, CELLS),
            room(CELLS, slots),
            room(MARGIN, slots),
            room(CELLS, chans, dtype=F32),
            room(REACH, chans),
            room(MARGIN, chans),
            room(MARGIN, chans),
            room(4, AREA, chans),
            room(4, AREA, chans),
            room(4, chans, 2 * MAIN),
            room(REACH + MARGIN, 3 * chans),
            room(MARGIN, chans),
            room(MARGIN, chans),
            room(CELLS, chans, dtype=F32),
            pltpu.SemaphoreType.DMA((24,)),
            pltpu.SemaphoreType.DMA((10,)),
            pltpu.SemaphoreType.DMA((10,)),
            pltpu.SemaphoreType.DMA((2,)),
            pltpu.SemaphoreType.REGULAR,
        ],
        compiler_params=pltpu.CompilerParams(
            collective_id=0, has_side_effects=True, vmem_limit_bytes=limit
        ),
    )(
        state,
        gain,
        input_weight,
        output_weight,
        obs_in_weight,
        obs_out_weight,
        observed,
        error_scale.reshape(1, seen),
        tile_id,
        foot_cell.reshape(1, feet),
        count,
        pack,
        gather,
        spread,
        spread_q,
    )
    gradient, misfit = pl.pallas_call(
        finish,
        out_shape=(shape(CELLS, chans, dtype=F32), shape(1, feet, dtype=F32)),
        in_specs=[vmem] * 3,
        out_specs=(vmem, vmem),
    )(own_part, back_part, costs)
    return gradient.reshape(initial_state.shape), misfit.reshape(feet)


def solution(mesh):
    both = ("lat", "lon")
    placed = (
        P("lat", "lon", None),
        P(),
        P(),
        P(),
        P(),
        P(),
        P(both, None),
        P(),
        P(both, None),
        P(both),
        P(both),
    )
    return jax.shard_map(
        functools.partial(shards, mesh.shape["lat"], mesh.shape["lon"]),
        mesh=mesh,
        in_specs=placed,
        out_specs=(P("lat", "lon", None), P(both)),
        check_vma=False,
    )
```

```python
import functools

import jax
import jax.numpy as jnp
import numpy as np
from jax import lax
from jax.experimental import pallas as pl
from jax.experimental.pallas import tpu as pltpu
from jax.sharding import PartitionSpec as P

HEADS = 8
WIN = 12
HALF = WIN // 2
SIDE = 2 * WIN
CELLS = SIDE * SIDE
AREA = WIN * WIN
STRIP = HALF * SIDE
MAIN = 128
LATE = AREA - MAIN
SRC = 384
NORM_EPS = 1e-06
MESH = pl.DeviceIdType.MESH
BF = jnp.bfloat16
F32 = jnp.float32

WINDOWS = ((0, 0), (0, 1), (1, 0), (1, 1))
REACH = 3 * STRIP
ACROSS = SIDE - HALF
SIDES, CORNER = 112, 48
LEFT, TOP, TL = 0, SIDES, 2 * SIDES
MARGIN = 2 * SIDES + CORNER
PIECES = ((LEFT, SIDES, 0, 1), (TOP, SIDES, 1, 0), (TL, CORNER, 1, 1))
SOURCES = (
    ((True, 0, 176), (False, TOP, SIDES), (False, LEFT, 48), (False, TL, CORNER)),
    ((True, 0, 272), (False, TOP, SIDES)),
    ((True, 144, 288), (False, LEFT + 32, 80), (True, 0, 16)),
    ((True, 144, 288), (True, 0, 96)),
)
TARGETS = (
    (0, STRIP, (0, 1)),
    (STRIP, 2 * STRIP, (2, 3)),
    (REACH + LEFT, SIDES, (0, 2)),
    (REACH + TOP, SIDES, (0, 1)),
    (REACH + TL, CORNER, (0,)),
)


def place_of(row, col):
    if row >= 0 and col >= 0:
        return True, row * SIDE + col
    if col >= 0:
        return False, TOP + (row + HALF) * ACROSS + col
    if row >= 0:
        return False, LEFT + row * HALF + col + HALF
    return False, TL + (row + HALF) * HALF + col + HALF


def selectors():
    pack = np.zeros((MARGIN, CELLS), np.float32)
    for a in range(HALF):
        for b in range(ACROSS):
            pack[LEFT + b * HALF + a, b * SIDE + ACROSS + a] = 1
            pack[TOP + a * ACROSS + b, (ACROSS + a) * SIDE + b] = 1
        for b in range(HALF):
            pack[TL + a * HALF + b, (ACROSS + a) * SIDE + ACROSS + b] = 1
    gather = np.zeros((4, AREA, SRC), np.float32)
    spread = np.zeros((4, REACH + MARGIN, AREA), np.float32)
    spread_q = np.zeros((4, REACH + MARGIN, 2 * MAIN), np.float32)
    for w, (i, j) in enumerate(WINDOWS):
        where = {}
        at = 0
        for own, first, rows in SOURCES[w]:
            for row in range(rows):
                where.setdefault((own, first + row), at + row)
            at += rows
        for a in range(WIN):
            for b in range(WIN):
                own, spot = place_of(WIN * i - HALF + a, WIN * j - HALF + b)
                cell = a * WIN + b
                gather[w, cell, where[own, spot]] = 1
                to = spot if own else REACH + spot
                spread[w, to, cell] = 1
                for h in range(HEADS if cell >= MAIN else 1):
                    spread_q[w, to, cell + h * LATE] = 1
    return pack, gather, spread, spread_q


def nn(a, b):
    return jnp.dot(a, b, preferred_element_type=F32)


def nt(a, b):
    return lax.dot_general(a, b, (((1,), (1,)), ((), ())), preferred_element_type=F32)


def iota(shape, dim):
    return lax.broadcasted_iota(jnp.int32, shape, dim)


def normalize(x_ref, gain, into):
    step = 48 if x_ref.shape[0] % 48 == 0 else 16
    for first in range(0, x_ref.shape[0], step):
        here = pl.ds(first, step)
        x = x_ref[here, :].astype(F32)
        rms = lax.rsqrt(jnp.mean(x * x, axis=-1, keepdims=True) + NORM_EPS)
        into[here, :] = (x * rms * gain).astype(BF)


def each(first, last, act):
    def one(step, carry):
        act(step)
        return carry

    lax.fori_loop(first, last, one, 0)


def start(copies):
    for copy in copies:
        copy.start()


def wait(copies):
    for copy in copies:
        copy.wait()


class Links:
    def __init__(self, lats, lons, margin_sem, foot_sem):
        self.lats, self.lons, self.n = lats, lons, lats * lons
        self.lat, self.lon = lax.axis_index("lat"), lax.axis_index("lon")
        self.margin_sem, self.foot_sem = margin_sem, foot_sem
        self.barrier = pltpu.get_barrier_semaphore()

    def around(self, up, right):
        lats, lons = self.lats, self.lons
        return lax.rem(self.lat + up + lats, lats), lax.rem(self.lon + right + lons, lons)

    def away_by(self, d):
        return self.around(lax.rem(d, self.lats), d // self.lats)

    def greet(self, device):
        pl.semaphore_signal(self.barrier, inc=1, device_id=device, device_id_type=MESH)

    def greet_all(self):
        each(1, self.n, lambda d: self.greet(self.away_by(d)))

    def met_all(self):
        pl.semaphore_wait(self.barrier, self.n - 1)

    def copy(self, sems, i, src, dst, device):
        return pltpu.make_async_remote_copy(
            src_ref=src,
            dst_ref=dst,
            send_sem=sems.at[2 * i],
            recv_sem=sems.at[2 * i + 1],
            device_id=device,
            device_id_type=MESH,
        )

    def pieces(self, base, src, into, way):
        return [
            self.copy(
                self.margin_sem,
                base + i,
                src.at[pl.ds(first, rows)],
                into.at[pl.ds(first, rows)],
                self.around(way * up, way * right),
            )
            for i, (first, rows, up, right) in enumerate(PIECES)
        ]

    def arrived(self, into, i, parts):
        rest = into.at[pl.ds(1, parts - 1)]
        self.copy(self.foot_sem, i, rest, rest, self.around(1, 0)).wait()

    def to_all(self, send, into, i):
        each(
            1,
            self.n,
            lambda d: self.copy(self.foot_sem, i, send.at[d], into.at[d], self.away_by(d)).start(),
        )
        into[0] = send[0]

    def back_lat(self, send, into, i):
        each(
            1,
            self.lats,
            lambda step: self.copy(
                self.foot_sem, i, send.at[:, step], into.at[step], self.around(-step, 0)
            ).start(),
        )
        into[0] = send[:, 0]

    def back_lon(self, mid, into, i):
        each(
            1,
            self.lons,
            lambda step: self.copy(
                self.foot_sem, i, mid.at[:, step], into.at[step], self.around(0, -step)
            ).start(),
        )
        into[0] = mid[:, 0]


def footprint_places(links, tile_id, count, cap):
    lats, lons, n = links.lats, links.lons, links.n
    feet = tile_id.shape[1]
    tile_lat = jnp.floor((tile_id[...].astype(F32) + 0.5) * (1.0 / lons)).astype(jnp.int32)
    up, right = tile_lat - links.lat, tile_id[...] - tile_lat * lons - links.lon
    up, right = jnp.where(up < 0, up + lats, up), jnp.where(right < 0, right + lons, right)
    away = right * lats + up
    live = iota((1, feet), 1) < count[...]
    named = (iota((n, feet), 0) == away).astype(F32)
    before = (iota((feet, feet), 0) < iota((feet, feet), 1)).astype(F32).astype(BF)
    rank = jnp.sum(nn(named.astype(BF), before) * named, axis=0, keepdims=True).astype(jnp.int32)
    return away, rank, live, named


class Heads:
    def __init__(self, chans):
        self.even = (iota((1, 128), 1) < 64).astype(F32).astype(BF)
        self.odd = (iota((1, 128), 1) >= 64).astype(F32).astype(BF)
        self.eye = (iota((128, 128), 0) == iota((128, 128), 1)).astype(F32).astype(BF)
        late_head = iota((MAIN, chans), 0) >> 4 == iota((MAIN, chans), 1) >> 6
        self.late_head = late_head.astype(F32).astype(BF)
        head_late = iota((chans, MAIN), 0) >> 6 == iota((chans, MAIN), 1) >> 4
        self.head_late = head_late.astype(F32)

    def stacked(self, x):
        return jnp.concatenate([x * self.even, x * self.odd], axis=0)

    def late_rows(self, x):
        return jnp.concatenate([x] * HEADS, axis=0) * self.late_head

    def turned(self, qkv, w, first):
        return [
            nt(self.eye, pair_of(qkv, w, first, AREA, pair)).astype(BF)
            for pair in range(HEADS // 2)
        ]


def pair_of(ref, w, first, rows, pair):
    return ref[w, 0:rows, first + 128 * pair : first + 128 * (pair + 1)]


def gather_window(source, w, tile_ref, margin_ref):
    at = 0
    for own, first, count_rows in SOURCES[w]:
        piece = (tile_ref if own else margin_ref)[pl.ds(first, count_rows), :]
        source[w, pl.ds(at, count_rows), :] = piece
        at += count_rows


RETURNED = tuple(
    [(SIDE * row + ACROSS, HALF, LEFT + HALF * row) for row in range(ACROSS)]
    + [(REACH + SIDE * row, ACROSS, TOP + ACROSS * row) for row in range(HALF)]
    + [(REACH + SIDE * row + ACROSS, HALF, TL + HALF * row) for row in range(HALF)]
)


def to_targets(selector, per_window, which):
    first, count_rows, windows = TARGETS[which]
    total = None
    for w in windows:
        part = per_window(selector[w, pl.ds(first, count_rows), :], w)
        total = part if total is None else total + part
    return total


def kernel(
    lats,
    lons,
    cap,
    state_hbm,
    gain,
    w_in_hbm,
    w_out_hbm,
    obs_in_hbm,
    obs_out_hbm,
    observed_hbm,
    scale,
    tile_id,
    cell_id,
    count,
    pack_hbm,
    gather_hbm,
    spread_hbm,
    spread_q_hbm,
    own_part_hbm,
    back_part_hbm,
    misfit,
    state,
    observed,
    pack_m,
    w_in,
    w_out,
    obs_in,
    obs_out,
    gather_m,
    spread_m,
    spread_q_m,
    packed,
    margin,
    own_n,
    margin_n,
    source,
    win,
    qkv,
    apart,
    probs,
    att_t,
    att_send,
    att_recv,
    attended,
    block_out,
    obs_send,
    obs_recv,
    idx_send,
    idx_recv,
    mis_send,
    mis_mid,
    mis_recv,
    chosen,
    silu_grad,
    hidden,
    predicted,
    residuals,
    foot_grad,
    onehot,
    back,
    back_packed,
    state_grad,
    att_grad,
    packed_g,
    margin_g,
    dk_w,
    dv_w,
    dq_t,
    proj_grad,
    part_send,
    part_recv,
    own_part,
    margin_sem,
    foot_sem,
    fetch_sem,
    store_sem,
):
    links = Links(lats, lons, margin_sem, foot_sem)
    n = links.n
    slots = n * cap
    feet = tile_id.shape[1]
    chans = state.shape[1]
    fetches = [
        pltpu.make_async_copy(src, dst, fetch_sem.at[i])
        for i, (src, dst) in enumerate(
            (
                (gather_hbm, gather_m),
                (w_in_hbm, w_in),
                (spread_q_hbm, spread_q_m),
                (w_out_hbm, w_out),
                (obs_in_hbm, obs_in),
                (obs_out_hbm, obs_out),
                (spread_hbm, spread_m),
                (state_hbm, state),
                (pack_hbm, pack_m),
                (observed_hbm, observed),
            )
        )
    ]
    start(fetches[7:])
    links.greet_all()
    start(fetches[:7])
    wait(fetches[7:9])

    packed[...] = nn(pack_m[...], state[...]).astype(BF)

    links.met_all()
    state_copies = links.pieces(0, packed, margin, 1)
    start(state_copies)

    away, rank, live, named = footprint_places(links, tile_id, count, cap)
    slot = jnp.where(live, away * cap + rank, -1)
    cell_value = (cell_id[...] + 1).astype(F32)
    on_lane = iota((4, cap, 128), 2) == iota((4, cap, 128), 1)
    cells = []
    for first in range(0, slots, 4 * cap):
        block = (iota((4 * cap, feet), 0) + first == slot).astype(F32)
        chosen[pl.ds(first, 4 * cap), :] = block.astype(BF)
        cell = jnp.sum(block * cell_value, axis=1, keepdims=True) - 1.0
        cell = jnp.where(on_lane, cell.reshape(4, cap, 1), 0.0)
        cells.append(jnp.sum(cell, axis=1, keepdims=True))
    idx_send[...] = jnp.concatenate(cells, axis=0)
    fetches[9].wait()
    rows = nn(chosen[...], observed[...])
    half = rows.shape[1] // 2
    rows = rows.reshape(n, cap, 2 * half)
    obs_send[...] = jnp.concatenate([rows[:, :, :half], rows[:, :, half:]], axis=1).astype(BF)

    links.to_all(idx_send, idx_recv, 0)
    links.to_all(obs_send, obs_recv, 1)

    normalize(state, gain[...], own_n)

    def place(windows):
        for w in windows:
            win[w] = nn(gather_m[w], source[w]).astype(BF)

    def project(first, last):
        cells = win[first:last].reshape((last - first) * AREA, chans)
        for part in range(3):
            cols = slice(part * chans, (part + 1) * chans)
            out = nn(cells, w_in[:, cols])
            out = (out * 0.125 if part == 0 else out).astype(BF)
            qkv[first:last, :, cols] = out.reshape(last - first, AREA, chans)

    heads = Heads(chans)

    def softmax(scores):
        e = jnp.exp(scores - jnp.max(scores, axis=0, keepdims=True))
        return e * (1.0 / jnp.sum(e, axis=0, keepdims=True))

    def forward(w):
        row = jnp.where(w < 2, 0, 1)
        late = heads.late_rows(qkv[w, MAIN:AREA, 0:chans])
        values_t = heads.turned(qkv, w, 2 * chans)

        def scored(pair):
            if pair < HEADS // 2:
                queries = heads.stacked(pair_of(qkv, w, 0, MAIN, pair))
                return nt(pair_of(qkv, w, chans, AREA, pair), queries)
            return nt(qkv[w, :, chans : 2 * chans], late)

        after = scored(0)
        for pair in range(HEADS // 2):
            scores, after = after, scored(pair + 1)
            for h in range(2):
                lanes = slice(MAIN * h, MAIN * (h + 1))
                p = softmax(scores[:, lanes] + apart[row, :, lanes])
                probs[w, :, 256 * pair + MAIN * h : 256 * pair + MAIN * (h + 1)] = p
                at = 128 * pair + 64 * h
                out = nn(values_t[pair][64 * h : 64 * h + 64], p.astype(BF))
                att_t[w, at : at + 64, 0:MAIN] = out.astype(BF)
        p = softmax(after + apart[row, :, 2 * MAIN :])
        probs[w, :, MAIN * HEADS :] = p
        out = nn(jnp.concatenate(values_t, axis=0), p.astype(BF))
        att_t[w, :, MAIN : 2 * MAIN] = (out * heads.head_late).astype(BF)

    first_rows = jnp.where(links.lat == 0, AREA // 2, 0)
    lane = iota((AREA, 3 * MAIN), 1)
    query = jnp.where(lane < 2 * MAIN, lane & (MAIN - 1), MAIN)
    seen_apart = (iota((AREA, 3 * MAIN), 0) < first_rows) != (query < first_rows)
    apart[0] = jnp.where(seen_apart, -1e30, 0.0)
    apart[1] = jnp.zeros((AREA, 3 * MAIN), F32)

    def att_to(which):
        return to_targets(spread_q_m, lambda m, w: nt(m, att_t[w]), which)

    gather_window(source, 3, own_n, margin_n)
    fetches[0].wait()
    fetches[1].wait()
    place((3,))
    project(3, 4)
    wait(state_copies)
    normalize(margin, gain[...], margin_n)
    for w in range(3):
        gather_window(source, w, own_n, margin_n)
    place(range(3))
    project(0, 3)
    fetches[2].wait()
    att_copies = links.pieces(3, att_send, att_recv, -1)

    def forward_step(w, carry):
        for at, targets, some in ((2, (3, 4), att_copies[1:]), (3, (2,), att_copies[:1])):

            @pl.when(w == at)
            def _():
                for which in targets:
                    first, count_rows, _ = TARGETS[which]
                    att_send[pl.ds(first - REACH, count_rows), :] = att_to(which).astype(BF)
                start(some)

        forward(w)
        return carry

    lax.fori_loop(0, 4, forward_step, 0)
    for which in (0, 1):
        first, count_rows, _ = TARGETS[which]
        attended[pl.ds(first, count_rows), :] = att_to(which)

    links.arrived(idx_recv, 0, n)
    on_lane = iota((n, cap, 128), 2) == iota((n, cap, 128), 1)
    spots = jnp.where(on_lane, idx_recv[...], 0.0)
    spots = jnp.sum(spots, axis=2, keepdims=True).reshape(slots, 1)
    pick = (iota((8, 128), 1) == 0).astype(F32)
    spots_row = lax.dot_general(
        pick,
        jnp.broadcast_to(spots, (slots, 128)),
        (((1,), (1,)), ((), ())),
        precision=lax.Precision.HIGHEST,
        preferred_element_type=F32,
    )[0:1].astype(jnp.int32)
    spots = spots.astype(jnp.int32)
    for first in range(0, slots, 32):
        block = iota((32, CELLS), 1) == spots[first : first + 32]
        onehot[pl.ds(first, 32), :] = block.astype(F32).astype(BF)
    for first in range(0, CELLS, 16):
        block = iota((16, slots), 0) + first == spots_row
        back[pl.ds(first, 16), :] = block.astype(F32).astype(BF)
    back_packed[...] = nn(pack_m[...], back[...]).astype(BF)
    chunk = slots // 2
    per_scale = 1.0 / scale[...]
    wait(fetches[3:7])
    wait(att_copies)
    returned = att_recv[...].astype(F32)
    for first, count_rows, at in RETURNED:
        attended[pl.ds(first, count_rows), :] = returned[at : at + count_rows]
    block_out[...] = (
        state[...].astype(F32) + nn(attended[...].astype(BF), w_out[...])
    ).astype(BF)

    step = min(chunk, 64)
    quarters = [slice(256 * i, 256 * (i + 1)) for i in range(obs_in.shape[1] // 256)]

    def predict(c, carry):
        base = pl.multiple_of(c * chunk, chunk)
        here = pl.ds(base, chunk)
        features = nn(onehot[here, :], block_out[...]).astype(BF)
        for cols in quarters:
            whole = nn(features, obs_in[:, cols])
            for first in range(0, chunk, step):
                pre = whole[first : first + step]
                sig = 0.5 + 0.5 * jnp.tanh(0.5 * pre)
                out = pre * sig
                some = pl.ds(base + first, step)
                hidden[some, cols] = out.astype(BF)
                silu_grad[some, cols] = sig + out * (1.0 - sig)
        predicted[here, :] = nn(hidden[here, :], obs_out[...])
        return carry

    def observe(c, carry):
        base = pl.multiple_of(c * chunk, chunk)
        here = pl.ds(base, chunk)
        lanes = iota((step // cap, cap, 128), 2) == iota((step // cap, cap, 128), 1)
        costs = []
        for first in range(0, chunk, step):
            seen = obs_recv[pl.ds(c * (n // 2) + first // cap, step // cap)].astype(F32)
            seen = jnp.concatenate(
                [seen[:, :cap].reshape(step, half), seen[:, cap:].reshape(step, half)], axis=1
            )
            some = pl.ds(base + first, step)
            residual = (predicted[some, :] - seen) * per_scale
            residuals[some, :] = (residual * per_scale).astype(BF)
            cost = 0.5 * jnp.sum(residual * residual, axis=1, keepdims=True)
            cost = jnp.where(lanes, cost.reshape(step // cap, cap, 1), 0.0)
            costs.append(jnp.sum(cost, axis=1, keepdims=True))
        blocks = pl.ds(c * (lons // 2), lons // 2)
        mis_send[blocks] = jnp.concatenate(costs, axis=0).reshape(lons // 2, lats, 1, 128)
        for cols in quarters:
            whole = nt(residuals[here, :], obs_out[cols, :])
            for first in range(0, chunk, step):
                some = pl.ds(base + first, step)
                grad = whole[first : first + step] * silu_grad[some, cols]
                hidden[some, cols] = grad.astype(BF)
        foot_grad[here, :] = nt(hidden[here, :], obs_in[...]).astype(BF)
        return carry

    lax.fori_loop(0, 2, predict, 0)
    links.arrived(obs_recv, 1, n)
    lax.fori_loop(0, 2, observe, 0)

    to_send = nn(back_packed[...], foot_grad[...]).astype(BF)
    packed_g[...] = nt(to_send, w_out[...]).astype(BF)
    grad_copies = links.pieces(6, packed_g, margin_g, 1)
    start(grad_copies)
    links.back_lat(mis_send, mis_mid, 2)
    state_grad[...] = nn(back[...], foot_grad[...])
    att_grad[...] = nt(state_grad[pl.ds(0, REACH), :].astype(BF), w_out[...]).astype(BF)

    def scores_gradient(p, dp):
        inner = jnp.sum(p * dp, axis=0, keepdims=True)
        return (p * (dp - inner)).astype(BF)

    def backward(w):
        late_q = heads.late_rows(qkv[w, MAIN:AREA, 0:chans])
        late_up = heads.late_rows(win[w, MAIN:AREA, :])
        ups = [heads.stacked(pair_of(win, w, 0, MAIN, pair)) for pair in range(HEADS // 2)]

        def dp_of(pair):
            if pair == HEADS // 2:
                return None
            return nt(pair_of(qkv, w, 2 * chans, AREA, pair), ups[pair])

        after = dp_of(0)
        dp = nt(qkv[w, :, 2 * chans : 3 * chans], late_up)
        keys_t = heads.turned(qkv, w, chans)
        p = probs[w, :, MAIN * HEADS :]
        ds = scores_gradient(p, dp)
        late_dk = nn(ds, late_q)
        late_dv = nn(p.astype(BF), late_up)
        out = nn(jnp.concatenate(keys_t, axis=0), ds)
        dq_t[w, :, MAIN : 2 * MAIN] = (out * (heads.head_late * 0.125)).astype(BF)
        for pair in range(HEADS // 2):
            at = 128 * pair
            dp, after = after, dp_of(pair + 1)
            ds, rounded = [], []
            for h in range(2):
                p = probs[w, :, at * 2 + MAIN * h : at * 2 + MAIN * (h + 1)]
                ds.append(scores_gradient(p, dp[:, MAIN * h : MAIN * (h + 1)]))
                rounded.append(p.astype(BF))
                out = nn(keys_t[pair][64 * h : 64 * h + 64], ds[h])
                dq_t[w, at + 64 * h : at + 64 * h + 64, 0:MAIN] = (out * 0.125).astype(BF)
            dk = nn(
                jnp.concatenate(ds, axis=1), heads.stacked(pair_of(qkv, w, 0, MAIN, pair))
            )
            dv = nn(jnp.concatenate(rounded, axis=1), ups[pair])
            dk_w[w, :, at : at + 128] = (dk + late_dk[:, at : at + 128]).astype(BF)
            dv_w[w, :, at : at + 128] = (dv + late_dv[:, at : at + 128]).astype(BF)

    def project_back(targets):
        for which in targets:
            first, count_rows, _ = TARGETS[which]
            here = pl.ds(first, count_rows)
            proj_grad[here, 0:chans] = to_targets(
                spread_q_m, lambda m, w: nt(m, dq_t[w]), which
            ).astype(BF)
            proj_grad[here, chans : 2 * chans] = to_targets(
                spread_m, lambda m, w: nn(m, dk_w[w]), which
            ).astype(BF)
            proj_grad[here, 2 * chans : 3 * chans] = to_targets(
                spread_m, lambda m, w: nn(m, dv_w[w]), which
            ).astype(BF)

    def norm_part(first, rows, cells, at, into, more=None):
        whole = nt(proj_grad[pl.ds(first, rows), :], w_in[...])
        step = 48 if rows % 48 == 0 else 16
        for row in range(0, rows, step):
            here = pl.ds(at + row, step)
            g = gain[...] * whole[row : row + step]
            x = cells[here, :].astype(F32)
            rms = lax.rsqrt(jnp.mean(x * x, axis=-1, keepdims=True) + NORM_EPS)
            inner = jnp.mean(x * g, axis=-1, keepdims=True)
            out = rms * g - x * (rms * rms * rms * inner)
            into[here, :] = out.astype(BF) if more is None else more[here, :] + out

    part_copies = links.pieces(9, part_send, part_recv, -1)
    gather_window(source, 3, att_grad, margin_g)
    place((3,))

    def backward_step(step, carry):
        @pl.when(step == 1)
        def _():
            wait(grad_copies)
            for w in range(3):
                gather_window(source, w, att_grad, margin_g)
            place(range(3))

        @pl.when(step == 2)
        def _():
            links.arrived(mis_mid, 2, lats)
            links.back_lon(mis_mid, mis_recv, 3)

        @pl.when(step == 3)
        def _():
            project_back((3, 4))
            norm_part(REACH + TOP, MARGIN - TOP, margin, TOP, part_send)
            start(part_copies[1:])

        backward(lax.rem(step + 3, 4))
        return carry

    lax.fori_loop(0, 4, backward_step, 0)

    project_back((2,))
    norm_part(REACH + LEFT, SIDES, margin, LEFT, part_send)
    start(part_copies[:1])
    project_back((0, 1))
    norm_part(0, REACH, state, 0, own_part, state_grad)
    own_part[pl.ds(REACH, STRIP), :] = state_grad[pl.ds(REACH, STRIP), :]
    own_store = pltpu.make_async_copy(own_part, own_part_hbm, store_sem.at[0])
    own_store.start()

    links.arrived(mis_recv, 3, lons)
    costs = lax.dot_general(
        mis_recv[...].reshape(n, 128),
        named,
        (((0,), (0,)), ((), ())),
        precision=lax.Precision.HIGHEST,
        preferred_element_type=F32,
    )
    costs = jnp.where(iota((128, feet), 0) == rank, costs, 0.0)
    misfit[...] = jnp.where(live, jnp.sum(costs, axis=0, keepdims=True), 0.0)
    wait(part_copies)
    back_store = pltpu.make_async_copy(part_recv, back_part_hbm, store_sem.at[1])
    back_store.start()
    own_store.wait()
    back_store.wait()


def finish(own_part, back_part, costs, gradient, misfit):
    gradient[...] = own_part[...]
    returned = back_part[...].astype(F32)
    for first, count_rows, at in RETURNED:
        gradient[pl.ds(first, count_rows), :] += returned[at : at + count_rows]
    misfit[...] = costs[...]


def shards(
    lats,
    lons,
    initial_state,
    norm_gain,
    input_weight,
    output_weight,
    obs_in_weight,
    obs_out_weight,
    observed,
    error_scale,
    foot_tile,
    foot_cell,
    foot_count,
):
    n = lats * lons
    chans = initial_state.shape[-1]
    feet, seen = observed.shape
    cap = 2 * feet // n
    slots = n * cap
    pack, gather, spread, spread_q = (jnp.asarray(m, BF) for m in selectors())
    vmem, whole = pl.BlockSpec(memory_space=pltpu.VMEM), pl.BlockSpec(memory_space=pl.ANY)
    state = initial_state.reshape(CELLS, chans)
    gain = norm_gain.reshape(1, chans)
    tile_id = foot_tile.reshape(1, feet)
    count = foot_count.reshape(1, 1)
    limit = 60 * 1024 * 1024

    def shape(*dims, dtype=BF):
        return jax.ShapeDtypeStruct(dims, dtype)

    def room(*dims, dtype=BF):
        return pltpu.VMEM(dims, dtype)

    own_part, back_part, costs = pl.pallas_call(
        functools.partial(kernel, lats, lons, cap),
        out_shape=(
            shape(CELLS, chans, dtype=F32),
            shape(MARGIN, chans),
            shape(1, feet, dtype=F32),
        ),
        in_specs=[whole, vmem] + [whole] * 5 + [vmem] * 4 + [whole] * 4,
        out_specs=(whole, whole, vmem),
        scratch_shapes=[
            room(CELLS, chans),
            room(feet, seen),
            room(MARGIN, CELLS),
            room(*input_weight.shape),
            room(*output_weight.shape),
            room(*obs_in_weight.shape),
            room(*obs_out_weight.shape),
            room(*gather.shape),
            room(*spread.shape),
            room(*spread_q.shape),
            room(MARGIN, chans),
            room(MARGIN, chans),
            room(CELLS, chans),
            room(MARGIN, chans),
            room(4, SRC, chans),
            room(4, AREA, chans),
            room(4, AREA, 3 * chans),
            room(2, AREA, 3 * MAIN, dtype=F32),
            room(4, AREA, MAIN * (HEADS + 1), dtype=F32),
            room(4, chans, 2 * MAIN),
            room(MARGIN, chans),
            room(MARGIN, chans),
            room(CELLS, chans, dtype=F32),
            room(CELLS, chans),
            room(n, 2 * cap, seen // 2),
            room(n, 2 * cap, seen // 2),
            room(n, 1, 128, dtype=F32),
            room(n, 1, 128, dtype=F32),
            room(lons, lats, 1, 128, dtype=F32),
            room(lats, lons, 1, 128, dtype=F32),
            room(lons, lats, 1, 128, dtype=F32),
            room(slots, feet),
            room(slots, obs_in_weight.shape[1], dtype=F32),
            room(slots, obs_in_weight.shape[1]),
            room(slots, seen, dtype=F32),
            room(slots, seen),
            room(slots, chans),
            room(slots, CELLS),
            room(CELLS, slots),
            room(MARGIN, slots),
            room(CELLS, chans, dtype=F32),
            room(REACH, chans),
            room(MARGIN, chans),
            room(MARGIN, chans),
            room(4, AREA, chans),
            room(4, AREA, chans),
            room(4, chans, 2 * MAIN),
            room(REACH + MARGIN, 3 * chans),
            room(MARGIN, chans),
            room(MARGIN, chans),
            room(CELLS, chans, dtype=F32),
            pltpu.SemaphoreType.DMA((24,)),
            pltpu.SemaphoreType.DMA((8,)),
            pltpu.SemaphoreType.DMA((10,)),
            pltpu.SemaphoreType.DMA((2,)),
        ],
        compiler_params=pltpu.CompilerParams(
            collective_id=0, has_side_effects=True, vmem_limit_bytes=limit
        ),
    )(
        state,
        gain,
        input_weight,
        output_weight,
        obs_in_weight,
        obs_out_weight,
        observed,
        error_scale.reshape(1, seen),
        tile_id,
        foot_cell.reshape(1, feet),
        count,
        pack,
        gather,
        spread,
        spread_q,
    )
    gradient, misfit = pl.pallas_call(
        finish,
        out_shape=(shape(CELLS, chans, dtype=F32), shape(1, feet, dtype=F32)),
        in_specs=[vmem] * 3,
        out_specs=(vmem, vmem),
    )(own_part, back_part, costs)
    return gradient.reshape(initial_state.shape), misfit.reshape(feet)


def solution(mesh):
    both = ("lat", "lon")
    placed = (
        P("lat", "lon", None),
        P(),
        P(),
        P(),
        P(),
        P(),
        P(both, None),
        P(),
        P(both, None),
        P(both),
        P(both),
    )
    return jax.shard_map(
        functools.partial(shards, mesh.shape["lat"], mesh.shape["lon"]),
        mesh=mesh,
        in_specs=placed,
        out_specs=(P("lat", "lon", None), P(both)),
        check_vma=False,
    )
```

```python
import functools

import jax
import jax.numpy as jnp
import numpy as np
from jax import lax
from jax.experimental import pallas as pl
from jax.experimental.pallas import tpu as pltpu
from jax.sharding import PartitionSpec as P

HEADS = 8
WIN = 12
HALF = WIN // 2
SIDE = 2 * WIN
CELLS = SIDE * SIDE
AREA = WIN * WIN
STRIP = HALF * SIDE
MAIN = 128
LATE = AREA - MAIN
SRC = 384
NORM_EPS = 1e-06
MESH = pl.DeviceIdType.MESH
BF = jnp.bfloat16
F32 = jnp.float32

WINDOWS = ((0, 0), (0, 1), (1, 0), (1, 1))
REACH = 3 * STRIP
ACROSS = SIDE - HALF
SIDES, CORNER = 112, 48
LEFT, TOP, TL = 0, SIDES, 2 * SIDES
MARGIN = 2 * SIDES + CORNER
PIECES = ((LEFT, SIDES, 0, 1), (TOP, SIDES, 1, 0), (TL, CORNER, 1, 1))
SOURCES = (
    ((True, 0, 176), (False, TOP, SIDES), (False, LEFT, 48), (False, TL, CORNER)),
    ((True, 0, 272), (False, TOP, SIDES)),
    ((True, 144, 288), (False, LEFT + 32, 80), (True, 0, 16)),
    ((True, 144, 288), (True, 0, 96)),
)
TARGETS = (
    (0, STRIP, (0, 1)),
    (STRIP, 2 * STRIP, (2, 3)),
    (REACH + LEFT, SIDES, (0, 2)),
    (REACH + TOP, SIDES, (0, 1)),
    (REACH + TL, CORNER, (0,)),
)


def place_of(row, col):
    if row >= 0 and col >= 0:
        return True, row * SIDE + col
    if col >= 0:
        return False, TOP + (row + HALF) * ACROSS + col
    if row >= 0:
        return False, LEFT + row * HALF + col + HALF
    return False, TL + (row + HALF) * HALF + col + HALF


def selectors():
    pack = np.zeros((MARGIN, CELLS), np.float32)
    for a in range(HALF):
        for b in range(ACROSS):
            pack[LEFT + b * HALF + a, b * SIDE + ACROSS + a] = 1
            pack[TOP + a * ACROSS + b, (ACROSS + a) * SIDE + b] = 1
        for b in range(HALF):
            pack[TL + a * HALF + b, (ACROSS + a) * SIDE + ACROSS + b] = 1
    gather = np.zeros((4, AREA, SRC), np.float32)
    spread = np.zeros((4, REACH + MARGIN, AREA), np.float32)
    spread_q = np.zeros((4, REACH + MARGIN, 2 * MAIN), np.float32)
    for w, (i, j) in enumerate(WINDOWS):
        where = {}
        at = 0
        for own, first, rows in SOURCES[w]:
            for row in range(rows):
                where.setdefault((own, first + row), at + row)
            at += rows
        for a in range(WIN):
            for b in range(WIN):
                own, spot = place_of(WIN * i - HALF + a, WIN * j - HALF + b)
                cell = a * WIN + b
                gather[w, cell, where[own, spot]] = 1
                to = spot if own else REACH + spot
                spread[w, to, cell] = 1
                for h in range(HEADS if cell >= MAIN else 1):
                    spread_q[w, to, cell + h * LATE] = 1
    return pack, gather, spread, spread_q


def nn(a, b):
    return jnp.dot(a, b, preferred_element_type=F32)


def nt(a, b):
    return lax.dot_general(a, b, (((1,), (1,)), ((), ())), preferred_element_type=F32)


def iota(shape, dim):
    return lax.broadcasted_iota(jnp.int32, shape, dim)


def normalize(x_ref, gain, into):
    step = 48 if x_ref.shape[0] % 48 == 0 else 16
    for first in range(0, x_ref.shape[0], step):
        here = pl.ds(first, step)
        x = x_ref[here, :].astype(F32)
        rms = lax.rsqrt(jnp.mean(x * x, axis=-1, keepdims=True) + NORM_EPS)
        into[here, :] = (x * rms * gain).astype(BF)


def each(first, last, act):
    def one(step, carry):
        act(step)
        return carry

    lax.fori_loop(first, last, one, 0)


def start(copies):
    for copy in copies:
        copy.start()


def wait(copies):
    for copy in copies:
        copy.wait()


class Links:
    def __init__(self, lats, lons, margin_sem, foot_sem):
        self.lats, self.lons, self.n = lats, lons, lats * lons
        self.lat, self.lon = lax.axis_index("lat"), lax.axis_index("lon")
        self.margin_sem, self.foot_sem = margin_sem, foot_sem
        self.barrier = pltpu.get_barrier_semaphore()

    def around(self, up, right):
        lats, lons = self.lats, self.lons
        return lax.rem(self.lat + up + lats, lats), lax.rem(self.lon + right + lons, lons)

    def away_by(self, d):
        return self.around(lax.rem(d, self.lats), d // self.lats)

    def greet(self, device):
        pl.semaphore_signal(self.barrier, inc=1, device_id=device, device_id_type=MESH)

    def greet_all(self):
        each(1, self.n, lambda d: self.greet(self.away_by(d)))

    def met_all(self):
        pl.semaphore_wait(self.barrier, self.n - 1)

    def copy(self, sems, i, src, dst, device):
        return pltpu.make_async_remote_copy(
            src_ref=src,
            dst_ref=dst,
            send_sem=sems.at[2 * i],
            recv_sem=sems.at[2 * i + 1],
            device_id=device,
            device_id_type=MESH,
        )

    def pieces(self, base, src, into, way):
        return [
            self.copy(
                self.margin_sem,
                base + i,
                src.at[pl.ds(first, rows)],
                into.at[pl.ds(first, rows)],
                self.around(way * up, way * right),
            )
            for i, (first, rows, up, right) in enumerate(PIECES)
        ]

    def arrived(self, into, i, parts):
        rest = into.at[pl.ds(1, parts - 1)]
        self.copy(self.foot_sem, i, rest, rest, self.around(1, 0)).wait()

    def to_all(self, send, into, i):
        each(
            1,
            self.n,
            lambda d: self.copy(self.foot_sem, i, send.at[d], into.at[d], self.away_by(d)).start(),
        )
        into[0] = send[0]

    def back_lat(self, send, into, i):
        each(
            1,
            self.lats,
            lambda step: self.copy(
                self.foot_sem, i, send.at[:, step], into.at[step], self.around(-step, 0)
            ).start(),
        )
        into[0] = send[:, 0]

    def back_lon(self, mid, into, i):
        each(
            1,
            self.lons,
            lambda step: self.copy(
                self.foot_sem, i, mid.at[:, step], into.at[step], self.around(0, -step)
            ).start(),
        )
        into[0] = mid[:, 0]


def footprint_places(links, tile_id, count, cap):
    lats, lons, n = links.lats, links.lons, links.n
    feet = tile_id.shape[1]
    tile_lat = jnp.floor((tile_id[...].astype(F32) + 0.5) * (1.0 / lons)).astype(jnp.int32)
    up, right = tile_lat - links.lat, tile_id[...] - tile_lat * lons - links.lon
    up, right = jnp.where(up < 0, up + lats, up), jnp.where(right < 0, right + lons, right)
    away = right * lats + up
    live = iota((1, feet), 1) < count[...]
    named = (iota((n, feet), 0) == away).astype(F32)
    before = (iota((feet, feet), 0) < iota((feet, feet), 1)).astype(F32).astype(BF)
    rank = jnp.sum(nn(named.astype(BF), before) * named, axis=0, keepdims=True).astype(jnp.int32)
    return away, rank, live, named


class Heads:
    def __init__(self, chans):
        self.even = (iota((1, 128), 1) < 64).astype(F32).astype(BF)
        self.odd = (iota((1, 128), 1) >= 64).astype(F32).astype(BF)
        self.eye = (iota((128, 128), 0) == iota((128, 128), 1)).astype(F32).astype(BF)
        late_head = iota((MAIN, chans), 0) >> 4 == iota((MAIN, chans), 1) >> 6
        self.late_head = late_head.astype(F32).astype(BF)
        head_late = iota((chans, MAIN), 0) >> 6 == iota((chans, MAIN), 1) >> 4
        self.head_late = head_late.astype(F32)

    def stacked(self, x):
        return jnp.concatenate([x * self.even, x * self.odd], axis=0)

    def late_rows(self, x):
        return jnp.concatenate([x] * HEADS, axis=0) * self.late_head

    def turned(self, qkv, w, first):
        return [
            nt(self.eye, pair_of(qkv, w, first, AREA, pair)).astype(BF)
            for pair in range(HEADS // 2)
        ]


def pair_of(ref, w, first, rows, pair):
    return ref[w, 0:rows, first + 128 * pair : first + 128 * (pair + 1)]


def gather_window(source, w, tile_ref, margin_ref):
    at = 0
    for own, first, count_rows in SOURCES[w]:
        piece = (tile_ref if own else margin_ref)[pl.ds(first, count_rows), :]
        source[w, pl.ds(at, count_rows), :] = piece
        at += count_rows


RETURNED = tuple(
    [(SIDE * row + ACROSS, HALF, LEFT + HALF * row) for row in range(ACROSS)]
    + [(REACH + SIDE * row, ACROSS, TOP + ACROSS * row) for row in range(HALF)]
    + [(REACH + SIDE * row + ACROSS, HALF, TL + HALF * row) for row in range(HALF)]
)


def to_targets(selector, per_window, which):
    first, count_rows, windows = TARGETS[which]
    total = None
    for w in windows:
        part = per_window(selector[w, pl.ds(first, count_rows), :], w)
        total = part if total is None else total + part
    return total


def kernel(
    lats,
    lons,
    cap,
    state_hbm,
    gain_hbm,
    w_in_hbm,
    w_out_hbm,
    obs_in_hbm,
    obs_out_hbm,
    observed_hbm,
    scale_hbm,
    tile_id_hbm,
    cell_id_hbm,
    count_hbm,
    pack_hbm,
    gather_hbm,
    spread_hbm,
    spread_q_hbm,
    own_part_hbm,
    back_part_hbm,
    misfit_hbm,
    state,
    observed,
    pack_m,
    gain,
    scale,
    tile_id,
    cell_id,
    count,
    misfit,
    w_in,
    w_out,
    obs_in,
    obs_out,
    gather_m,
    spread_m,
    spread_q_m,
    packed,
    margin,
    own_n,
    margin_n,
    source,
    win,
    qkv,
    apart,
    probs,
    att_t,
    att_send,
    att_recv,
    attended,
    block_out,
    obs_send,
    obs_recv,
    idx_send,
    idx_recv,
    mis_send,
    mis_mid,
    mis_recv,
    chosen,
    silu_grad,
    hidden,
    predicted,
    residuals,
    foot_grad,
    onehot,
    back,
    back_packed,
    state_grad,
    att_grad,
    packed_g,
    margin_g,
    dk_w,
    dv_w,
    dq_t,
    keys_t,
    proj_grad,
    part_send,
    part_recv,
    own_part,
    margin_sem,
    foot_sem,
    fetch_sem,
    store_sem,
):
    links = Links(lats, lons, margin_sem, foot_sem)
    n = links.n
    slots = n * cap
    feet = tile_id.shape[1]
    chans = state.shape[1]
    fetches = [
        pltpu.make_async_copy(src, dst, fetch_sem.at[i])
        for i, (src, dst) in enumerate(
            (
                (gather_hbm, gather_m),
                (w_in_hbm, w_in),
                (spread_q_hbm, spread_q_m),
                (w_out_hbm, w_out),
                (obs_in_hbm, obs_in),
                (obs_out_hbm, obs_out),
                (spread_hbm, spread_m),
                (state_hbm, state),
                (pack_hbm, pack_m),
                (observed_hbm, observed),
                (gain_hbm, gain),
                (scale_hbm, scale),
                (tile_id_hbm, tile_id),
                (cell_id_hbm, cell_id),
                (count_hbm, count),
            )
        )
    ]
    start(fetches[7:9])
    links.greet_all()
    start(fetches[9:])
    start(fetches[:7])
    wait(fetches[7:9])

    packed[...] = nn(pack_m[...], state[...]).astype(BF)

    links.met_all()
    state_copies = links.pieces(0, packed, margin, 1)
    start(state_copies)

    wait(fetches[10:])
    away, rank, live, named = footprint_places(links, tile_id, count, cap)
    slot = jnp.where(live, away * cap + rank, -1)
    cell_value = (cell_id[...] + 1).astype(F32)
    on_lane = iota((4, cap, 128), 2) == iota((4, cap, 128), 1)
    cells = []
    for first in range(0, slots, 4 * cap):
        block = (iota((4 * cap, feet), 0) + first == slot).astype(F32)
        chosen[pl.ds(first, 4 * cap), :] = block.astype(BF)
        cell = jnp.sum(block * cell_value, axis=1, keepdims=True) - 1.0
        cell = jnp.where(on_lane, cell.reshape(4, cap, 1), 0.0)
        cells.append(jnp.sum(cell, axis=1, keepdims=True))
    idx_send[...] = jnp.concatenate(cells, axis=0)
    fetches[9].wait()
    rows = nn(chosen[...], observed[...])
    half = rows.shape[1] // 2
    rows = rows.reshape(n, cap, 2 * half)
    obs_send[...] = jnp.concatenate([rows[:, :, :half], rows[:, :, half:]], axis=1).astype(BF)

    links.to_all(idx_send, idx_recv, 0)
    links.to_all(obs_send, obs_recv, 1)

    normalize(state, gain[...], own_n)

    def place(windows):
        for w in windows:
            win[w] = nn(gather_m[w], source[w]).astype(BF)

    def project(first, last):
        cells = win[first:last].reshape((last - first) * AREA, chans)
        for part in range(3):
            cols = slice(part * chans, (part + 1) * chans)
            out = nn(cells, w_in[:, cols])
            out = (out * 0.125 if part == 0 else out).astype(BF)
            qkv[first:last, :, cols] = out.reshape(last - first, AREA, chans)

    heads = Heads(chans)

    def softmax(scores):
        e = jnp.exp(scores - jnp.max(scores, axis=0, keepdims=True))
        return e * (1.0 / jnp.sum(e, axis=0, keepdims=True))

    def forward(w):
        row = jnp.where(w < 2, 0, 1)
        late = heads.late_rows(qkv[w, MAIN:AREA, 0:chans])
        values_t = heads.turned(qkv, w, 2 * chans)

        def scored(pair):
            if pair < HEADS // 2:
                queries = heads.stacked(pair_of(qkv, w, 0, MAIN, pair))
                return nt(pair_of(qkv, w, chans, AREA, pair), queries)
            return nt(qkv[w, :, chans : 2 * chans], late)

        after = scored(0)
        for pair in range(HEADS // 2):
            scores, after = after, scored(pair + 1)
            for h in range(2):
                lanes = slice(MAIN * h, MAIN * (h + 1))
                p = softmax(scores[:, lanes] + apart[row, :, lanes])
                probs[w, :, 256 * pair + MAIN * h : 256 * pair + MAIN * (h + 1)] = p
                at = 128 * pair + 64 * h
                out = nn(values_t[pair][64 * h : 64 * h + 64], p.astype(BF))
                att_t[w, at : at + 64, 0:MAIN] = out.astype(BF)
        p = softmax(after + apart[row, :, 2 * MAIN :])
        probs[w, :, MAIN * HEADS :] = p
        out = nn(jnp.concatenate(values_t, axis=0), p.astype(BF))
        att_t[w, :, MAIN : 2 * MAIN] = (out * heads.head_late).astype(BF)

    first_rows = jnp.where(links.lat == 0, AREA // 2, 0)
    lane = iota((AREA, 3 * MAIN), 1)
    query = jnp.where(lane < 2 * MAIN, lane & (MAIN - 1), MAIN)
    seen_apart = (iota((AREA, 3 * MAIN), 0) < first_rows) != (query < first_rows)
    apart[0] = jnp.where(seen_apart, -1e30, 0.0)
    apart[1] = jnp.zeros((AREA, 3 * MAIN), F32)

    def att_to(which):
        return to_targets(spread_q_m, lambda m, w: nt(m, att_t[w]), which)

    gather_window(source, 3, own_n, margin_n)
    fetches[0].wait()
    fetches[1].wait()
    place((3,))
    project(3, 4)
    wait(state_copies)
    normalize(margin, gain[...], margin_n)
    for w in range(3):
        gather_window(source, w, own_n, margin_n)
    place(range(3))
    project(0, 3)
    fetches[2].wait()
    att_copies = links.pieces(3, att_send, att_recv, -1)

    def forward_step(w, carry):
        for at, targets, some in ((2, (3, 4), att_copies[1:]), (3, (2,), att_copies[:1])):

            @pl.when(w == at)
            def _():
                for which in targets:
                    first, count_rows, _ = TARGETS[which]
                    att_send[pl.ds(first - REACH, count_rows), :] = att_to(which).astype(BF)
                start(some)

        forward(w)
        return carry

    lax.fori_loop(0, 4, forward_step, 0)
    for which in (0, 1):
        first, count_rows, _ = TARGETS[which]
        attended[pl.ds(first, count_rows), :] = att_to(which)

    links.arrived(idx_recv, 0, n)
    on_lane = iota((n, cap, 128), 2) == iota((n, cap, 128), 1)
    spots = jnp.where(on_lane, idx_recv[...], 0.0)
    spots = jnp.sum(spots, axis=2, keepdims=True).reshape(slots, 1)
    pick = (iota((8, 128), 1) == 0).astype(F32)
    spots_row = lax.dot_general(
        pick,
        jnp.broadcast_to(spots, (slots, 128)),
        (((1,), (1,)), ((), ())),
        precision=lax.Precision.HIGHEST,
        preferred_element_type=F32,
    )[0:1].astype(jnp.int32)
    spots = spots.astype(jnp.int32)
    for first in range(0, slots, 32):
        block = iota((32, CELLS), 1) == spots[first : first + 32]
        onehot[pl.ds(first, 32), :] = block.astype(F32).astype(BF)
    for first in range(0, CELLS, 16):
        block = iota((16, slots), 0) + first == spots_row
        back[pl.ds(first, 16), :] = block.astype(F32).astype(BF)
    back_packed[...] = nn(pack_m[...], back[...]).astype(BF)
    chunk = slots // 2
    per_scale = 1.0 / scale[...]
    wait(fetches[3:7])
    wait(att_copies)
    returned = att_recv[...].astype(F32)
    for first, count_rows, at in RETURNED:
        attended[pl.ds(first, count_rows), :] = returned[at : at + count_rows]
    block_out[...] = (
        state[...].astype(F32) + nn(attended[...].astype(BF), w_out[...])
    ).astype(BF)

    step = min(chunk, 64)
    quarters = [slice(256 * i, 256 * (i + 1)) for i in range(obs_in.shape[1] // 256)]

    def predict(c, carry):
        base = pl.multiple_of(c * chunk, chunk)
        here = pl.ds(base, chunk)
        features = nn(onehot[here, :], block_out[...]).astype(BF)
        for cols in quarters:
            whole = nn(features, obs_in[:, cols])
            for first in range(0, chunk, step):
                pre = whole[first : first + step]
                sig = 0.5 + 0.5 * jnp.tanh(0.5 * pre)
                out = pre * sig
                some = pl.ds(base + first, step)
                hidden[some, cols] = out.astype(BF)
                silu_grad[some, cols] = sig + out * (1.0 - sig)
        predicted[here, :] = nn(hidden[here, :], obs_out[...])
        return carry

    def observe(c, carry):
        base = pl.multiple_of(c * chunk, chunk)
        here = pl.ds(base, chunk)
        lanes = iota((step // cap, cap, 128), 2) == iota((step // cap, cap, 128), 1)
        costs = []
        for first in range(0, chunk, step):
            seen = obs_recv[pl.ds(c * (n // 2) + first // cap, step // cap)].astype(F32)
            seen = jnp.concatenate(
                [seen[:, :cap].reshape(step, half), seen[:, cap:].reshape(step, half)], axis=1
            )
            some = pl.ds(base + first, step)
            residual = (predicted[some, :] - seen) * per_scale
            residuals[some, :] = (residual * per_scale).astype(BF)
            cost = 0.5 * jnp.sum(residual * residual, axis=1, keepdims=True)
            cost = jnp.where(lanes, cost.reshape(step // cap, cap, 1), 0.0)
            costs.append(jnp.sum(cost, axis=1, keepdims=True))
        blocks = pl.ds(c * (lons // 2), lons // 2)
        mis_send[blocks] = jnp.concatenate(costs, axis=0).reshape(lons // 2, lats, 1, 128)
        for cols in quarters:
            whole = nt(residuals[here, :], obs_out[cols, :])
            for first in range(0, chunk, step):
                some = pl.ds(base + first, step)
                grad = whole[first : first + step] * silu_grad[some, cols]
                hidden[some, cols] = grad.astype(BF)
        foot_grad[here, :] = nt(hidden[here, :], obs_in[...]).astype(BF)
        return carry

    lax.fori_loop(0, 2, predict, 0)
    links.arrived(obs_recv, 1, n)
    lax.fori_loop(0, 2, observe, 0)

    to_send = nn(back_packed[...], foot_grad[...]).astype(BF)
    packed_g[...] = nt(to_send, w_out[...]).astype(BF)
    grad_copies = links.pieces(6, packed_g, margin_g, 1)
    start(grad_copies)
    links.back_lat(mis_send, mis_mid, 2)
    state_grad[...] = nn(back[...], foot_grad[...])
    att_grad[...] = nt(state_grad[pl.ds(0, REACH), :].astype(BF), w_out[...]).astype(BF)

    def turn_keys(w, carry):
        keys_t[w] = jnp.concatenate(heads.turned(qkv, w, chans), axis=0)
        return carry

    lax.fori_loop(0, 4, turn_keys, 0)

    def scores_gradient(p, dp):
        inner = jnp.sum(p * dp, axis=0, keepdims=True)
        return (p * (dp - inner)).astype(BF)

    def backward(w):
        late_q = heads.late_rows(qkv[w, MAIN:AREA, 0:chans])
        late_up = heads.late_rows(win[w, MAIN:AREA, :])
        ups = [heads.stacked(pair_of(win, w, 0, MAIN, pair)) for pair in range(HEADS // 2)]

        def dp_of(pair):
            if pair == HEADS // 2:
                return None
            return nt(pair_of(qkv, w, 2 * chans, AREA, pair), ups[pair])

        after = dp_of(0)
        dp = nt(qkv[w, :, 2 * chans : 3 * chans], late_up)
        p = probs[w, :, MAIN * HEADS :]
        ds = scores_gradient(p, dp)
        late_dk = nn(ds, late_q)
        late_dv = nn(p.astype(BF), late_up)
        out = nn(keys_t[w], ds)
        dq_t[w, :, MAIN : 2 * MAIN] = (out * (heads.head_late * 0.125)).astype(BF)
        for pair in range(HEADS // 2):
            at = 128 * pair
            dp, after = after, dp_of(pair + 1)
            ds, rounded = [], []
            for h in range(2):
                p = probs[w, :, at * 2 + MAIN * h : at * 2 + MAIN * (h + 1)]
                ds.append(scores_gradient(p, dp[:, MAIN * h : MAIN * (h + 1)]))
                rounded.append(p.astype(BF))
                rows = slice(at + 64 * h, at + 64 * h + 64)
                dq_t[w, rows, 0:MAIN] = (nn(keys_t[w, rows, :], ds[h]) * 0.125).astype(BF)
            dk = nn(
                jnp.concatenate(ds, axis=1), heads.stacked(pair_of(qkv, w, 0, MAIN, pair))
            )
            dv = nn(jnp.concatenate(rounded, axis=1), ups[pair])
            dk_w[w, :, at : at + 128] = (dk + late_dk[:, at : at + 128]).astype(BF)
            dv_w[w, :, at : at + 128] = (dv + late_dv[:, at : at + 128]).astype(BF)

    def project_back(targets):
        for which in targets:
            first, count_rows, _ = TARGETS[which]
            here = pl.ds(first, count_rows)
            proj_grad[here, 0:chans] = to_targets(
                spread_q_m, lambda m, w: nt(m, dq_t[w]), which
            ).astype(BF)
            proj_grad[here, chans : 2 * chans] = to_targets(
                spread_m, lambda m, w: nn(m, dk_w[w]), which
            ).astype(BF)
            proj_grad[here, 2 * chans : 3 * chans] = to_targets(
                spread_m, lambda m, w: nn(m, dv_w[w]), which
            ).astype(BF)

    def norm_part(first, rows, cells, at, into, more=None):
        whole = nt(proj_grad[pl.ds(first, rows), :], w_in[...])
        step = 48 if rows % 48 == 0 else 16
        for row in range(0, rows, step):
            here = pl.ds(at + row, step)
            g = gain[...] * whole[row : row + step]
            x = cells[here, :].astype(F32)
            rms = lax.rsqrt(jnp.mean(x * x, axis=-1, keepdims=True) + NORM_EPS)
            inner = jnp.mean(x * g, axis=-1, keepdims=True)
            out = rms * g - x * (rms * rms * rms * inner)
            into[here, :] = out.astype(BF) if more is None else more[here, :] + out

    part_copies = links.pieces(9, part_send, part_recv, -1)
    gather_window(source, 3, att_grad, margin_g)
    place((3,))

    def backward_step(step, carry):
        @pl.when(step == 1)
        def _():
            wait(grad_copies)
            for w in range(3):
                gather_window(source, w, att_grad, margin_g)
            place(range(3))

        @pl.when(step == 2)
        def _():
            links.arrived(mis_mid, 2, lats)
            links.back_lon(mis_mid, mis_recv, 3)

        @pl.when(step == 3)
        def _():
            project_back((3, 4))
            norm_part(REACH + TOP, MARGIN - TOP, margin, TOP, part_send)
            start(part_copies[1:])

        backward(lax.rem(step + 3, 4))
        return carry

    lax.fori_loop(0, 4, backward_step, 0)

    project_back((2,))
    norm_part(REACH + LEFT, SIDES, margin, LEFT, part_send)
    start(part_copies[:1])
    project_back((0, 1))
    norm_part(0, REACH, state, 0, own_part, state_grad)
    own_part[pl.ds(REACH, STRIP), :] = state_grad[pl.ds(REACH, STRIP), :]
    own_store = pltpu.make_async_copy(own_part, own_part_hbm, store_sem.at[0])
    own_store.start()

    links.arrived(mis_recv, 3, lons)
    costs = lax.dot_general(
        mis_recv[...].reshape(n, 128),
        named,
        (((0,), (0,)), ((), ())),
        precision=lax.Precision.HIGHEST,
        preferred_element_type=F32,
    )
    costs = jnp.where(iota((128, feet), 0) == rank, costs, 0.0)
    misfit[...] = jnp.where(live, jnp.sum(costs, axis=0, keepdims=True), 0.0)
    misfit_store = pltpu.make_async_copy(misfit, misfit_hbm, store_sem.at[2])
    misfit_store.start()
    wait(part_copies)
    back_store = pltpu.make_async_copy(part_recv, back_part_hbm, store_sem.at[1])
    back_store.start()
    wait([own_store, misfit_store, back_store])


def finish(own_part, back_part, costs, gradient, misfit):
    gradient[...] = own_part[...]
    returned = back_part[...].astype(F32)
    for first, count_rows, at in RETURNED:
        gradient[pl.ds(first, count_rows), :] += returned[at : at + count_rows]
    misfit[...] = costs[...]


def shards(
    lats,
    lons,
    initial_state,
    norm_gain,
    input_weight,
    output_weight,
    obs_in_weight,
    obs_out_weight,
    observed,
    error_scale,
    foot_tile,
    foot_cell,
    foot_count,
):
    n = lats * lons
    chans = initial_state.shape[-1]
    feet, seen = observed.shape
    cap = 2 * feet // n
    slots = n * cap
    pack, gather, spread, spread_q = (jnp.asarray(m, BF) for m in selectors())
    vmem, whole = pl.BlockSpec(memory_space=pltpu.VMEM), pl.BlockSpec(memory_space=pl.ANY)
    state = initial_state.reshape(CELLS, chans)
    gain = norm_gain.reshape(1, chans)
    tile_id = foot_tile.reshape(1, feet)
    count = foot_count.reshape(1, 1)
    limit = 60 * 1024 * 1024

    def shape(*dims, dtype=BF):
        return jax.ShapeDtypeStruct(dims, dtype)

    def room(*dims, dtype=BF):
        return pltpu.VMEM(dims, dtype)

    own_part, back_part, costs = pl.pallas_call(
        functools.partial(kernel, lats, lons, cap),
        out_shape=(
            shape(CELLS, chans, dtype=F32),
            shape(MARGIN, chans),
            shape(1, feet, dtype=F32),
        ),
        in_specs=[whole] * 15,
        out_specs=(whole,) * 3,
        scratch_shapes=[
            room(CELLS, chans),
            room(feet, seen),
            room(MARGIN, CELLS),
            room(1, chans, dtype=F32),
            room(1, seen, dtype=F32),
            room(1, feet, dtype=jnp.int32),
            room(1, feet, dtype=jnp.int32),
            room(1, 1, dtype=jnp.int32),
            room(1, feet, dtype=F32),
            room(*input_weight.shape),
            room(*output_weight.shape),
            room(*obs_in_weight.shape),
            room(*obs_out_weight.shape),
            room(*gather.shape),
            room(*spread.shape),
            room(*spread_q.shape),
            room(MARGIN, chans),
            room(MARGIN, chans),
            room(CELLS, chans),
            room(MARGIN, chans),
            room(4, SRC, chans),
            room(4, AREA, chans),
            room(4, AREA, 3 * chans),
            room(2, AREA, 3 * MAIN, dtype=F32),
            room(4, AREA, MAIN * (HEADS + 1), dtype=F32),
            room(4, chans, 2 * MAIN),
            room(MARGIN, chans),
            room(MARGIN, chans),
            room(CELLS, chans, dtype=F32),
            room(CELLS, chans),
            room(n, 2 * cap, seen // 2),
            room(n, 2 * cap, seen // 2),
            room(n, 1, 128, dtype=F32),
            room(n, 1, 128, dtype=F32),
            room(lons, lats, 1, 128, dtype=F32),
            room(lats, lons, 1, 128, dtype=F32),
            room(lons, lats, 1, 128, dtype=F32),
            room(slots, feet),
            room(slots, obs_in_weight.shape[1], dtype=F32),
            room(slots, obs_in_weight.shape[1]),
            room(slots, seen, dtype=F32),
            room(slots, seen),
            room(slots, chans),
            room(slots, CELLS),
            room(CELLS, slots),
            room(MARGIN, slots),
            room(CELLS, chans, dtype=F32),
            room(REACH, chans),
            room(MARGIN, chans),
            room(MARGIN, chans),
            room(4, AREA, chans),
            room(4, AREA, chans),
            room(4, chans, 2 * MAIN),
            room(4, chans, AREA),
            room(REACH + MARGIN, 3 * chans),
            room(MARGIN, chans),
            room(MARGIN, chans),
            room(CELLS, chans, dtype=F32),
            pltpu.SemaphoreType.DMA((24,)),
            pltpu.SemaphoreType.DMA((8,)),
            pltpu.SemaphoreType.DMA((15,)),
            pltpu.SemaphoreType.DMA((3,)),
        ],
        compiler_params=pltpu.CompilerParams(
            collective_id=0, has_side_effects=True, vmem_limit_bytes=limit
        ),
    )(
        state,
        gain,
        input_weight,
        output_weight,
        obs_in_weight,
        obs_out_weight,
        observed,
        error_scale.reshape(1, seen),
        tile_id,
        foot_cell.reshape(1, feet),
        count,
        pack,
        gather,
        spread,
        spread_q,
    )
    gradient, misfit = pl.pallas_call(
        finish,
        out_shape=(shape(CELLS, chans, dtype=F32), shape(1, feet, dtype=F32)),
        in_specs=[vmem] * 3,
        out_specs=(vmem, vmem),
    )(own_part, back_part, costs)
    return gradient.reshape(initial_state.shape), misfit.reshape(feet)


def solution(mesh):
    both = ("lat", "lon")
    placed = (
        P("lat", "lon", None),
        P(),
        P(),
        P(),
        P(),
        P(),
        P(both, None),
        P(),
        P(both, None),
        P(both),
        P(both),
    )
    return jax.shard_map(
        functools.partial(shards, mesh.shape["lat"], mesh.shape["lon"]),
        mesh=mesh,
        in_specs=placed,
        out_specs=(P("lat", "lon", None), P(both)),
        check_vma=False,
    )
```

```python
import functools

import jax
import jax.numpy as jnp
import numpy as np
from jax import lax
from jax.experimental import pallas as pl
from jax.experimental.pallas import tpu as pltpu
from jax.sharding import PartitionSpec as P

HEADS = 8
WIN = 12
HALF = WIN // 2
SIDE = 2 * WIN
CELLS = SIDE * SIDE
AREA = WIN * WIN
STRIP = HALF * SIDE
MAIN = 128
LATE = AREA - MAIN
SRC = 384
NORM_EPS = 1e-06
MESH = pl.DeviceIdType.MESH
BF = jnp.bfloat16
F32 = jnp.float32

WINDOWS = ((0, 0), (0, 1), (1, 0), (1, 1))
REACH = 3 * STRIP
ACROSS = SIDE - HALF
SIDES, CORNER = 112, 48
LEFT, TOP, TL = 0, SIDES, 2 * SIDES
MARGIN = 2 * SIDES + CORNER
PIECES = ((LEFT, SIDES, 0, 1), (TOP, SIDES, 1, 0), (TL, CORNER, 1, 1))
SOURCES = (
    ((True, 0, 176), (False, TOP, SIDES), (False, LEFT, 48), (False, TL, CORNER)),
    ((True, 0, 272), (False, TOP, SIDES)),
    ((True, 144, 288), (False, LEFT + 32, 80), (True, 0, 16)),
    ((True, 144, 288), (True, 0, 96)),
)
TARGETS = (
    (0, STRIP, (0, 1)),
    (STRIP, 2 * STRIP, (2, 3)),
    (REACH + LEFT, SIDES, (0, 2)),
    (REACH + TOP, SIDES, (0, 1)),
    (REACH + TL, CORNER, (0,)),
)


def place_of(row, col):
    if row >= 0 and col >= 0:
        return True, row * SIDE + col
    if col >= 0:
        return False, TOP + (row + HALF) * ACROSS + col
    if row >= 0:
        return False, LEFT + row * HALF + col + HALF
    return False, TL + (row + HALF) * HALF + col + HALF


def selectors():
    pack = np.zeros((MARGIN, CELLS), np.float32)
    for a in range(HALF):
        for b in range(ACROSS):
            pack[LEFT + b * HALF + a, b * SIDE + ACROSS + a] = 1
            pack[TOP + a * ACROSS + b, (ACROSS + a) * SIDE + b] = 1
        for b in range(HALF):
            pack[TL + a * HALF + b, (ACROSS + a) * SIDE + ACROSS + b] = 1
    gather = np.zeros((4, AREA, SRC), np.float32)
    spread = np.zeros((4, REACH + MARGIN, AREA), np.float32)
    spread_q = np.zeros((4, REACH + MARGIN, 2 * MAIN), np.float32)
    for w, (i, j) in enumerate(WINDOWS):
        where = {}
        at = 0
        for own, first, rows in SOURCES[w]:
            for row in range(rows):
                where.setdefault((own, first + row), at + row)
            at += rows
        for a in range(WIN):
            for b in range(WIN):
                own, spot = place_of(WIN * i - HALF + a, WIN * j - HALF + b)
                cell = a * WIN + b
                gather[w, cell, where[own, spot]] = 1
                to = spot if own else REACH + spot
                spread[w, to, cell] = 1
                for h in range(HEADS if cell >= MAIN else 1):
                    spread_q[w, to, cell + h * LATE] = 1
    return pack, gather, spread, spread_q


def nn(a, b):
    return jnp.dot(a, b, preferred_element_type=F32)


def nt(a, b):
    return lax.dot_general(a, b, (((1,), (1,)), ((), ())), preferred_element_type=F32)


def iota(shape, dim):
    return lax.broadcasted_iota(jnp.int32, shape, dim)


def normalize(x_ref, gain, into):
    step = 48 if x_ref.shape[0] % 48 == 0 else 16
    for first in range(0, x_ref.shape[0], step):
        here = pl.ds(first, step)
        x = x_ref[here, :].astype(F32)
        rms = lax.rsqrt(jnp.mean(x * x, axis=-1, keepdims=True) + NORM_EPS)
        into[here, :] = (x * rms * gain).astype(BF)


def each(first, last, act):
    def one(step, carry):
        act(step)
        return carry

    lax.fori_loop(first, last, one, 0)


def start(copies):
    for copy in copies:
        copy.start()


def wait(copies):
    for copy in copies:
        copy.wait()


class Links:
    def __init__(self, lats, lons, margin_sem, foot_sem):
        self.lats, self.lons, self.n = lats, lons, lats * lons
        self.lat, self.lon = lax.axis_index("lat"), lax.axis_index("lon")
        self.margin_sem, self.foot_sem = margin_sem, foot_sem
        self.barrier = pltpu.get_barrier_semaphore()

    def around(self, up, right):
        lats, lons = self.lats, self.lons
        return lax.rem(self.lat + up + lats, lats), lax.rem(self.lon + right + lons, lons)

    def away_by(self, d):
        return self.around(lax.rem(d, self.lats), d // self.lats)

    def greet(self, device):
        pl.semaphore_signal(self.barrier, inc=1, device_id=device, device_id_type=MESH)

    def greet_all(self):
        each(1, self.n, lambda d: self.greet(self.away_by(d)))

    def met_all(self):
        pl.semaphore_wait(self.barrier, self.n - 1)

    def copy(self, sems, i, src, dst, device):
        return pltpu.make_async_remote_copy(
            src_ref=src,
            dst_ref=dst,
            send_sem=sems.at[2 * i],
            recv_sem=sems.at[2 * i + 1],
            device_id=device,
            device_id_type=MESH,
        )

    def pieces(self, base, src, into, way):
        return [
            self.copy(
                self.margin_sem,
                base + i,
                src.at[pl.ds(first, rows)],
                into.at[pl.ds(first, rows)],
                self.around(way * up, way * right),
            )
            for i, (first, rows, up, right) in enumerate(PIECES)
        ]

    def arrived(self, into, i, parts):
        rest = into.at[pl.ds(1, parts - 1)]
        self.copy(self.foot_sem, i, rest, rest, self.around(1, 0)).wait()

    def to_all(self, send, into, i):
        each(
            1,
            self.n,
            lambda d: self.copy(self.foot_sem, i, send.at[d], into.at[d], self.away_by(d)).start(),
        )
        into[0] = send[0]

    def back_lat(self, send, into, i):
        each(
            1,
            self.lats,
            lambda step: self.copy(
                self.foot_sem, i, send.at[:, step], into.at[step], self.around(-step, 0)
            ).start(),
        )
        into[0] = send[:, 0]

    def back_lon(self, mid, into, i):
        each(
            1,
            self.lons,
            lambda step: self.copy(
                self.foot_sem, i, mid.at[:, step], into.at[step], self.around(0, -step)
            ).start(),
        )
        into[0] = mid[:, 0]


def footprint_places(links, tile_id, count, cap):
    lats, lons, n = links.lats, links.lons, links.n
    feet = tile_id.shape[1]
    tile_lat = jnp.floor((tile_id[...].astype(F32) + 0.5) * (1.0 / lons)).astype(jnp.int32)
    up, right = tile_lat - links.lat, tile_id[...] - tile_lat * lons - links.lon
    up, right = jnp.where(up < 0, up + lats, up), jnp.where(right < 0, right + lons, right)
    away = right * lats + up
    live = iota((1, feet), 1) < count[...]
    named = (iota((n, feet), 0) == away).astype(F32)
    before = (iota((feet, feet), 0) < iota((feet, feet), 1)).astype(F32).astype(BF)
    rank = jnp.sum(nn(named.astype(BF), before) * named, axis=0, keepdims=True).astype(jnp.int32)
    return away, rank, live, named


class Heads:
    def __init__(self, chans):
        self.even = (iota((1, 128), 1) < 64).astype(F32).astype(BF)
        self.odd = (iota((1, 128), 1) >= 64).astype(F32).astype(BF)
        late_head = iota((MAIN, chans), 0) >> 4 == iota((MAIN, chans), 1) >> 6
        self.late_head = late_head.astype(F32).astype(BF)

    def stacked(self, x):
        return jnp.concatenate([x * self.even, x * self.odd], axis=0)

    def late_rows(self, x):
        return jnp.concatenate([x] * HEADS, axis=0) * self.late_head

    def turned(self, qkv, w, first):
        return [pair_of(qkv, w, first, AREA, pair).T for pair in range(HEADS // 2)]

    def late_out(self, x, held):
        return nn(x.T, held).astype(BF) * self.late_head


def pair_of(ref, w, first, rows, pair):
    return ref[w, 0:rows, first + 128 * pair : first + 128 * (pair + 1)]


def gather_window(source, w, tile_ref, margin_ref):
    at = 0
    for own, first, count_rows in SOURCES[w]:
        piece = (tile_ref if own else margin_ref)[pl.ds(first, count_rows), :]
        source[w, pl.ds(at, count_rows), :] = piece
        at += count_rows


RETURNED = tuple(
    [(SIDE * row + ACROSS, HALF, LEFT + HALF * row) for row in range(ACROSS)]
    + [(REACH + SIDE * row, ACROSS, TOP + ACROSS * row) for row in range(HALF)]
    + [(REACH + SIDE * row + ACROSS, HALF, TL + HALF * row) for row in range(HALF)]
)


def to_targets(selector, per_window, which):
    first, count_rows, windows = TARGETS[which]
    total = None
    for w in windows:
        part = per_window(selector[w, pl.ds(first, count_rows), :], w)
        total = part if total is None else total + part
    return total


def kernel(
    lats,
    lons,
    cap,
    state_hbm,
    gain_hbm,
    w_in_hbm,
    w_out_hbm,
    obs_in_hbm,
    obs_out_hbm,
    observed_hbm,
    scale_hbm,
    tile_id_hbm,
    cell_id_hbm,
    count_hbm,
    pack_hbm,
    gather_hbm,
    spread_hbm,
    spread_q_hbm,
    own_part_hbm,
    back_part_hbm,
    misfit_hbm,
    state,
    observed,
    pack_m,
    gain,
    scale,
    tile_id,
    cell_id,
    count,
    misfit,
    w_in,
    w_out,
    obs_in,
    obs_out,
    gather_m,
    spread_m,
    spread_q_m,
    packed,
    margin,
    own_n,
    margin_n,
    source,
    win,
    qkv,
    apart,
    probs,
    att_w,
    att_send,
    att_recv,
    attended,
    block_out,
    obs_send,
    obs_recv,
    idx_send,
    idx_recv,
    mis_send,
    mis_mid,
    mis_recv,
    chosen,
    silu_grad,
    hidden,
    predicted,
    residuals,
    foot_grad,
    onehot,
    back,
    back_packed,
    state_grad,
    att_grad,
    packed_g,
    margin_g,
    dk_w,
    dv_w,
    dq_w,
    keys_t,
    proj_grad,
    part_send,
    part_recv,
    own_part,
    margin_sem,
    foot_sem,
    fetch_sem,
    store_sem,
):
    links = Links(lats, lons, margin_sem, foot_sem)
    n = links.n
    slots = n * cap
    feet = tile_id.shape[1]
    chans = state.shape[1]
    fetches = [
        pltpu.make_async_copy(src, dst, fetch_sem.at[i])
        for i, (src, dst) in enumerate(
            (
                (gather_hbm, gather_m),
                (w_in_hbm, w_in),
                (spread_q_hbm, spread_q_m),
                (w_out_hbm, w_out),
                (obs_in_hbm, obs_in),
                (obs_out_hbm, obs_out),
                (spread_hbm, spread_m),
                (state_hbm, state),
                (pack_hbm, pack_m),
                (observed_hbm, observed),
                (gain_hbm, gain),
                (scale_hbm, scale),
                (tile_id_hbm, tile_id),
                (cell_id_hbm, cell_id),
                (count_hbm, count),
            )
        )
    ]
    start(fetches[7:9])
    links.greet_all()
    start(fetches[9:])
    start(fetches[:7])
    wait(fetches[7:9])

    packed[...] = nn(pack_m[...], state[...]).astype(BF)

    links.met_all()
    state_copies = links.pieces(0, packed, margin, 1)
    start(state_copies)

    wait(fetches[10:])
    away, rank, live, named = footprint_places(links, tile_id, count, cap)
    slot = jnp.where(live, away * cap + rank, -1)
    cell_value = (cell_id[...] + 1).astype(F32)
    on_lane = iota((4, cap, 128), 2) == iota((4, cap, 128), 1)
    cells = []
    for first in range(0, slots, 4 * cap):
        block = (iota((4 * cap, feet), 0) + first == slot).astype(F32)
        chosen[pl.ds(first, 4 * cap), :] = block.astype(BF)
        cell = jnp.sum(block * cell_value, axis=1, keepdims=True) - 1.0
        cell = jnp.where(on_lane, cell.reshape(4, cap, 1), 0.0)
        cells.append(jnp.sum(cell, axis=1, keepdims=True))
    idx_send[...] = jnp.concatenate(cells, axis=0)
    fetches[9].wait()
    rows = nn(chosen[...], observed[...])
    half = rows.shape[1] // 2
    rows = rows.reshape(n, cap, 2 * half)
    obs_send[...] = jnp.concatenate([rows[:, :, :half], rows[:, :, half:]], axis=1).astype(BF)

    links.to_all(idx_send, idx_recv, 0)
    links.to_all(obs_send, obs_recv, 1)

    normalize(state, gain[...], own_n)

    def place(windows):
        for w in windows:
            win[w] = nn(gather_m[w], source[w]).astype(BF)

    def project(first, last):
        cells = win[first:last].reshape((last - first) * AREA, chans)
        for part in range(3):
            cols = slice(part * chans, (part + 1) * chans)
            out = nn(cells, w_in[:, cols])
            out = (out * 0.125 if part == 0 else out).astype(BF)
            qkv[first:last, :, cols] = out.reshape(last - first, AREA, chans)

    heads = Heads(chans)

    def softmax(scores):
        e = jnp.exp(scores - jnp.max(scores, axis=0, keepdims=True))
        return e * (1.0 / jnp.sum(e, axis=0, keepdims=True))

    def forward(w):
        row = jnp.where(w < 2, 0, 1)
        late = heads.late_rows(qkv[w, MAIN:AREA, 0:chans])
        values_t = heads.turned(qkv, w, 2 * chans)

        def scored(pair):
            if pair < HEADS // 2:
                queries = heads.stacked(pair_of(qkv, w, 0, MAIN, pair))
                return nt(pair_of(qkv, w, chans, AREA, pair), queries)
            return nt(qkv[w, :, chans : 2 * chans], late)

        after = scored(0)
        for pair in range(HEADS // 2):
            scores, after = after, scored(pair + 1)
            out = []
            for h in range(2):
                lanes = slice(MAIN * h, MAIN * (h + 1))
                p = softmax(scores[:, lanes] + apart[row, :, lanes])
                probs[w, :, 256 * pair + MAIN * h : 256 * pair + MAIN * (h + 1)] = p
                out.append(nn(values_t[pair][64 * h : 64 * h + 64], p.astype(BF)))
            out = jnp.concatenate(out, axis=0).astype(BF)
            att_w[w, 0:MAIN, 128 * pair : 128 * (pair + 1)] = out.T
        p = softmax(after + apart[row, :, 2 * MAIN :])
        probs[w, :, MAIN * HEADS :] = p
        att_w[w, MAIN : 2 * MAIN, :] = heads.late_out(p.astype(BF), qkv[w, :, 2 * chans :])

    first_rows = jnp.where(links.lat == 0, AREA // 2, 0)
    lane = iota((AREA, 3 * MAIN), 1)
    query = jnp.where(lane < 2 * MAIN, lane & (MAIN - 1), MAIN)
    seen_apart = (iota((AREA, 3 * MAIN), 0) < first_rows) != (query < first_rows)
    apart[0] = jnp.where(seen_apart, -1e30, 0.0)
    apart[1] = jnp.zeros((AREA, 3 * MAIN), F32)

    def att_wo(which):
        return to_targets(spread_q_m, lambda m, w: nn(m, att_w[w]), which)

    gather_window(source, 3, own_n, margin_n)
    fetches[0].wait()
    fetches[1].wait()
    place((3,))
    project(3, 4)
    wait(state_copies)
    normalize(margin, gain[...], margin_n)
    for w in range(3):
        gather_window(source, w, own_n, margin_n)
    place(range(3))
    project(0, 3)
    fetches[2].wait()
    att_copies = links.pieces(3, att_send, att_recv, -1)

    def forward_step(w, carry):
        for at, targets, some in ((2, (3, 4), att_copies[1:]), (3, (2,), att_copies[:1])):

            @pl.when(w == at)
            def _():
                for which in targets:
                    first, count_rows, _ = TARGETS[which]
                    att_send[pl.ds(first - REACH, count_rows), :] = att_wo(which).astype(BF)
                start(some)

        forward(w)
        return carry

    lax.fori_loop(0, 4, forward_step, 0)
    for which in (0, 1):
        first, count_rows, _ = TARGETS[which]
        attended[pl.ds(first, count_rows), :] = att_wo(which)

    links.arrived(idx_recv, 0, n)
    on_lane = iota((n, cap, 128), 2) == iota((n, cap, 128), 1)
    spots = jnp.where(on_lane, idx_recv[...], 0.0)
    spots = jnp.sum(spots, axis=2, keepdims=True).reshape(slots, 1)
    pick = (iota((8, 128), 1) == 0).astype(F32)
    spots_row = lax.dot_general(
        pick,
        jnp.broadcast_to(spots, (slots, 128)),
        (((1,), (1,)), ((), ())),
        precision=lax.Precision.HIGHEST,
        preferred_element_type=F32,
    )[0:1].astype(jnp.int32)
    spots = spots.astype(jnp.int32)
    for first in range(0, slots, 32):
        block = iota((32, CELLS), 1) == spots[first : first + 32]
        onehot[pl.ds(first, 32), :] = block.astype(F32).astype(BF)
    for first in range(0, CELLS, 16):
        block = iota((16, slots), 0) + first == spots_row
        back[pl.ds(first, 16), :] = block.astype(F32).astype(BF)
    back_packed[...] = nn(pack_m[...], back[...]).astype(BF)
    chunk = slots // 2
    per_scale = 1.0 / scale[...]
    wait(fetches[3:7])
    wait(att_copies)
    returned = att_recv[...].astype(F32)
    for first, count_rows, at in RETURNED:
        attended[pl.ds(first, count_rows), :] = returned[at : at + count_rows]
    block_out[...] = (
        state[...].astype(F32) + nn(attended[...].astype(BF), w_out[...])
    ).astype(BF)

    step = min(chunk, 64)
    quarters = [slice(256 * i, 256 * (i + 1)) for i in range(obs_in.shape[1] // 256)]

    def predict(c, carry):
        base = pl.multiple_of(c * chunk, chunk)
        here = pl.ds(base, chunk)
        features = nn(onehot[here, :], block_out[...]).astype(BF)
        for cols in quarters:
            whole = nn(features, obs_in[:, cols])
            for first in range(0, chunk, step):
                pre = whole[first : first + step]
                sig = 0.5 + 0.5 * jnp.tanh(0.5 * pre)
                out = pre * sig
                some = pl.ds(base + first, step)
                hidden[some, cols] = out.astype(BF)
                silu_grad[some, cols] = sig + out * (1.0 - sig)
        predicted[here, :] = nn(hidden[here, :], obs_out[...])
        return carry

    def observe(c, carry):
        base = pl.multiple_of(c * chunk, chunk)
        here = pl.ds(base, chunk)
        lanes = iota((step // cap, cap, 128), 2) == iota((step // cap, cap, 128), 1)
        costs = []
        for first in range(0, chunk, step):
            seen = obs_recv[pl.ds(c * (n // 2) + first // cap, step // cap)].astype(F32)
            seen = jnp.concatenate(
                [seen[:, :cap].reshape(step, half), seen[:, cap:].reshape(step, half)], axis=1
            )
            some = pl.ds(base + first, step)
            residual = (predicted[some, :] - seen) * per_scale
            residuals[some, :] = (residual * per_scale).astype(BF)
            cost = 0.5 * jnp.sum(residual * residual, axis=1, keepdims=True)
            cost = jnp.where(lanes, cost.reshape(step // cap, cap, 1), 0.0)
            costs.append(jnp.sum(cost, axis=1, keepdims=True))
        blocks = pl.ds(c * (lons // 2), lons // 2)
        mis_send[blocks] = jnp.concatenate(costs, axis=0).reshape(lons // 2, lats, 1, 128)
        for cols in quarters:
            whole = nt(residuals[here, :], obs_out[cols, :])
            for first in range(0, chunk, step):
                some = pl.ds(base + first, step)
                grad = whole[first : first + step] * silu_grad[some, cols]
                hidden[some, cols] = grad.astype(BF)
        foot_grad[here, :] = nt(hidden[here, :], obs_in[...]).astype(BF)
        return carry

    lax.fori_loop(0, 2, predict, 0)
    links.arrived(obs_recv, 1, n)
    lax.fori_loop(0, 2, observe, 0)

    to_send = nn(back_packed[...], foot_grad[...]).astype(BF)
    packed_g[...] = nt(to_send, w_out[...]).astype(BF)
    grad_copies = links.pieces(6, packed_g, margin_g, 1)
    start(grad_copies)
    links.back_lat(mis_send, mis_mid, 2)
    state_grad[...] = nn(back[...], foot_grad[...])
    att_grad[...] = nt(state_grad[pl.ds(0, REACH), :].astype(BF), w_out[...]).astype(BF)

    def turn_keys(w, carry):
        keys_t[w] = jnp.concatenate(heads.turned(qkv, w, chans), axis=0)
        return carry

    lax.fori_loop(0, 4, turn_keys, 0)

    def scores_gradient(p, dp):
        inner = jnp.sum(p * dp, axis=0, keepdims=True)
        return (p * (dp - inner)).astype(BF)

    def backward(w):
        late_q = heads.late_rows(qkv[w, MAIN:AREA, 0:chans])
        late_up = heads.late_rows(win[w, MAIN:AREA, :])
        ups = [heads.stacked(pair_of(win, w, 0, MAIN, pair)) for pair in range(HEADS // 2)]

        def dp_of(pair):
            if pair == HEADS // 2:
                return None
            return nt(pair_of(qkv, w, 2 * chans, AREA, pair), ups[pair])

        after = dp_of(0)
        dp = nt(qkv[w, :, 2 * chans : 3 * chans], late_up)
        p = probs[w, :, MAIN * HEADS :]
        ds = scores_gradient(p, dp)
        late_dk = nn(ds, late_q)
        late_dv = nn(p.astype(BF), late_up)
        late_dq = heads.late_out(ds, qkv[w, :, chans : 2 * chans])
        dq_w[w, MAIN : 2 * MAIN, :] = late_dq * jnp.bfloat16(0.125)
        for pair in range(HEADS // 2):
            at = 128 * pair
            dp, after = after, dp_of(pair + 1)
            ds, rounded, out = [], [], []
            for h in range(2):
                p = probs[w, :, at * 2 + MAIN * h : at * 2 + MAIN * (h + 1)]
                ds.append(scores_gradient(p, dp[:, MAIN * h : MAIN * (h + 1)]))
                rounded.append(p.astype(BF))
                out.append(nn(keys_t[w, at + 64 * h : at + 64 * h + 64, :], ds[h]))
            out = (jnp.concatenate(out, axis=0) * 0.125).astype(BF)
            dq_w[w, 0:MAIN, at : at + 128] = out.T
            dk = nn(
                jnp.concatenate(ds, axis=1), heads.stacked(pair_of(qkv, w, 0, MAIN, pair))
            )
            dv = nn(jnp.concatenate(rounded, axis=1), ups[pair])
            dk_w[w, :, at : at + 128] = (dk + late_dk[:, at : at + 128]).astype(BF)
            dv_w[w, :, at : at + 128] = (dv + late_dv[:, at : at + 128]).astype(BF)

    def project_back(targets):
        for which in targets:
            first, count_rows, _ = TARGETS[which]
            here = pl.ds(first, count_rows)
            proj_grad[here, 0:chans] = to_targets(
                spread_q_m, lambda m, w: nn(m, dq_w[w]), which
            ).astype(BF)
            proj_grad[here, chans : 2 * chans] = to_targets(
                spread_m, lambda m, w: nn(m, dk_w[w]), which
            ).astype(BF)
            proj_grad[here, 2 * chans : 3 * chans] = to_targets(
                spread_m, lambda m, w: nn(m, dv_w[w]), which
            ).astype(BF)

    def norm_part(first, rows, cells, at, into, more=None):
        whole = nt(proj_grad[pl.ds(first, rows), :], w_in[...])
        step = 48 if rows % 48 == 0 else 16
        for row in range(0, rows, step):
            here = pl.ds(at + row, step)
            g = gain[...] * whole[row : row + step]
            x = cells[here, :].astype(F32)
            rms = lax.rsqrt(jnp.mean(x * x, axis=-1, keepdims=True) + NORM_EPS)
            inner = jnp.mean(x * g, axis=-1, keepdims=True)
            out = rms * g - x * (rms * rms * rms * inner)
            into[here, :] = out.astype(BF) if more is None else more[here, :] + out

    part_copies = links.pieces(9, part_send, part_recv, -1)
    gather_window(source, 3, att_grad, margin_g)
    place((3,))

    def backward_step(step, carry):
        @pl.when(step == 1)
        def _():
            wait(grad_copies)
            for w in range(3):
                gather_window(source, w, att_grad, margin_g)
            place(range(3))

        @pl.when(step == 2)
        def _():
            links.arrived(mis_mid, 2, lats)
            links.back_lon(mis_mid, mis_recv, 3)

        @pl.when(step == 3)
        def _():
            project_back((3, 4))
            norm_part(REACH + TOP, MARGIN - TOP, margin, TOP, part_send)
            start(part_copies[1:])

        backward(lax.rem(step + 3, 4))
        return carry

    lax.fori_loop(0, 4, backward_step, 0)

    project_back((2,))
    norm_part(REACH + LEFT, SIDES, margin, LEFT, part_send)
    start(part_copies[:1])
    project_back((0, 1))
    norm_part(0, REACH, state, 0, own_part, state_grad)
    own_part[pl.ds(REACH, STRIP), :] = state_grad[pl.ds(REACH, STRIP), :]
    own_store = pltpu.make_async_copy(own_part, own_part_hbm, store_sem.at[0])
    own_store.start()

    links.arrived(mis_recv, 3, lons)
    costs = lax.dot_general(
        mis_recv[...].reshape(n, 128),
        named,
        (((0,), (0,)), ((), ())),
        precision=lax.Precision.HIGHEST,
        preferred_element_type=F32,
    )
    costs = jnp.where(iota((128, feet), 0) == rank, costs, 0.0)
    misfit[...] = jnp.where(live, jnp.sum(costs, axis=0, keepdims=True), 0.0)
    misfit_store = pltpu.make_async_copy(misfit, misfit_hbm, store_sem.at[2])
    misfit_store.start()
    wait(part_copies)
    back_store = pltpu.make_async_copy(part_recv, back_part_hbm, store_sem.at[1])
    back_store.start()
    wait([own_store, misfit_store, back_store])


def finish(own_hbm, back_hbm, costs_hbm, gradient, misfit, whole, back, costs, sems):
    rows = CELLS // 6
    parts = [pl.ds(first, rows) for first in range(0, CELLS, rows)]
    ins = [pltpu.make_async_copy(own_hbm.at[p], whole.at[p], sems.at[i]) for i, p in enumerate(parts)]
    outs = [
        pltpu.make_async_copy(whole.at[p], gradient.at[p], sems.at[6 + i]) for i, p in enumerate(parts)
    ]
    more = [
        pltpu.make_async_copy(back_hbm, back, sems.at[12]),
        pltpu.make_async_copy(costs_hbm, costs, sems.at[13]),
    ]
    out = pltpu.make_async_copy(costs, misfit, sems.at[14])
    start(more)
    start(ins)
    wait(more)
    out.start()
    returned = back[...].astype(F32)
    for i in range(6):
        ins[i].wait()
        for first, count_rows, at in RETURNED:
            if first // rows == i:
                whole[pl.ds(first, count_rows), :] += returned[at : at + count_rows]
        outs[i].start()
    wait(outs)
    out.wait()


def shards(
    lats,
    lons,
    initial_state,
    norm_gain,
    input_weight,
    output_weight,
    obs_in_weight,
    obs_out_weight,
    observed,
    error_scale,
    foot_tile,
    foot_cell,
    foot_count,
):
    n = lats * lons
    chans = initial_state.shape[-1]
    feet, seen = observed.shape
    cap = 2 * feet // n
    slots = n * cap
    pack, gather, spread, spread_q = (jnp.asarray(m, BF) for m in selectors())
    whole = pl.BlockSpec(memory_space=pl.ANY)
    state = initial_state.reshape(CELLS, chans)
    gain = norm_gain.reshape(1, chans)
    tile_id = foot_tile.reshape(1, feet)
    count = foot_count.reshape(1, 1)
    limit = 60 * 1024 * 1024

    def shape(*dims, dtype=BF):
        return jax.ShapeDtypeStruct(dims, dtype)

    def room(*dims, dtype=BF):
        return pltpu.VMEM(dims, dtype)

    own_part, back_part, costs = pl.pallas_call(
        functools.partial(kernel, lats, lons, cap),
        out_shape=(
            shape(CELLS, chans, dtype=F32),
            shape(MARGIN, chans),
            shape(1, feet, dtype=F32),
        ),
        in_specs=[whole] * 15,
        out_specs=(whole,) * 3,
        scratch_shapes=[
            room(CELLS, chans),
            room(feet, seen),
            room(MARGIN, CELLS),
            room(1, chans, dtype=F32),
            room(1, seen, dtype=F32),
            room(1, feet, dtype=jnp.int32),
            room(1, feet, dtype=jnp.int32),
            room(1, 1, dtype=jnp.int32),
            room(1, feet, dtype=F32),
            room(*input_weight.shape),
            room(*output_weight.shape),
            room(*obs_in_weight.shape),
            room(*obs_out_weight.shape),
            room(*gather.shape),
            room(*spread.shape),
            room(*spread_q.shape),
            room(MARGIN, chans),
            room(MARGIN, chans),
            room(CELLS, chans),
            room(MARGIN, chans),
            room(4, SRC, chans),
            room(4, AREA, chans),
            room(4, AREA, 3 * chans),
            room(2, AREA, 3 * MAIN, dtype=F32),
            room(4, AREA, MAIN * (HEADS + 1), dtype=F32),
            room(4, 2 * MAIN, chans),
            room(MARGIN, chans),
            room(MARGIN, chans),
            room(CELLS, chans, dtype=F32),
            room(CELLS, chans),
            room(n, 2 * cap, seen // 2),
            room(n, 2 * cap, seen // 2),
            room(n, 1, 128, dtype=F32),
            room(n, 1, 128, dtype=F32),
            room(lons, lats, 1, 128, dtype=F32),
            room(lats, lons, 1, 128, dtype=F32),
            room(lons, lats, 1, 128, dtype=F32),
            room(slots, feet),
            room(slots, obs_in_weight.shape[1], dtype=F32),
            room(slots, obs_in_weight.shape[1]),
            room(slots, seen, dtype=F32),
            room(slots, seen),
            room(slots, chans),
            room(slots, CELLS),
            room(CELLS, slots),
            room(MARGIN, slots),
            room(CELLS, chans, dtype=F32),
            room(REACH, chans),
            room(MARGIN, chans),
            room(MARGIN, chans),
            room(4, AREA, chans),
            room(4, AREA, chans),
            room(4, 2 * MAIN, chans),
            room(4, chans, AREA),
            room(REACH + MARGIN, 3 * chans),
            room(MARGIN, chans),
            room(MARGIN, chans),
            room(CELLS, chans, dtype=F32),
            pltpu.SemaphoreType.DMA((24,)),
            pltpu.SemaphoreType.DMA((8,)),
            pltpu.SemaphoreType.DMA((15,)),
            pltpu.SemaphoreType.DMA((3,)),
        ],
        compiler_params=pltpu.CompilerParams(
            collective_id=0, has_side_effects=True, vmem_limit_bytes=limit
        ),
    )(
        state,
        gain,
        input_weight,
        output_weight,
        obs_in_weight,
        obs_out_weight,
        observed,
        error_scale.reshape(1, seen),
        tile_id,
        foot_cell.reshape(1, feet),
        count,
        pack,
        gather,
        spread,
        spread_q,
    )
    gradient, misfit = pl.pallas_call(
        finish,
        out_shape=(shape(CELLS, chans, dtype=F32), shape(1, feet, dtype=F32)),
        in_specs=[whole] * 3,
        out_specs=(whole, whole),
        scratch_shapes=[
            room(CELLS, chans, dtype=F32),
            room(MARGIN, chans),
            room(1, feet, dtype=F32),
            pltpu.SemaphoreType.DMA((15,)),
        ],
    )(own_part, back_part, costs)
    return gradient.reshape(initial_state.shape), misfit.reshape(feet)


def solution(mesh):
    both = ("lat", "lon")
    placed = (
        P("lat", "lon", None),
        P(),
        P(),
        P(),
        P(),
        P(),
        P(both, None),
        P(),
        P(both, None),
        P(both),
        P(both),
    )
    return jax.shard_map(
        functools.partial(shards, mesh.shape["lat"], mesh.shape["lon"]),
        mesh=mesh,
        in_specs=placed,
        out_specs=(P("lat", "lon", None), P(both)),
        check_vma=False,
    )
```

```python
import functools

import jax
import jax.numpy as jnp
import numpy as np
from jax import lax
from jax.experimental import pallas as pl
from jax.experimental.pallas import tpu as pltpu
from jax.sharding import PartitionSpec as P

HEADS = 8
WIN = 12
HALF = WIN // 2
SIDE = 2 * WIN
CELLS = SIDE * SIDE
AREA = WIN * WIN
STRIP = HALF * SIDE
MAIN = 128
LATE = AREA - MAIN
SRC = 384
NORM_EPS = 1e-06
MESH = pl.DeviceIdType.MESH
BF = jnp.bfloat16
F32 = jnp.float32

WINDOWS = ((0, 0), (0, 1), (1, 0), (1, 1))
REACH = 3 * STRIP
ACROSS = SIDE - HALF
SIDES, CORNER = 112, 48
LEFT, TOP, TL = 0, SIDES, 2 * SIDES
MARGIN = 2 * SIDES + CORNER
PIECES = ((LEFT, SIDES, 0, 1), (TOP, SIDES, 1, 0), (TL, CORNER, 1, 1))
SOURCES = (
    ((True, 0, 176), (False, TOP, SIDES), (False, LEFT, 48), (False, TL, CORNER)),
    ((True, 0, 272), (False, TOP, SIDES)),
    ((True, 144, 288), (False, LEFT + 32, 80), (True, 0, 16)),
    ((True, 144, 288), (True, 0, 96)),
)
TARGETS = (
    (0, STRIP, (0, 1)),
    (STRIP, 2 * STRIP, (2, 3)),
    (REACH + LEFT, SIDES, (0, 2)),
    (REACH + TOP, SIDES, (0, 1)),
    (REACH + TL, CORNER, (0,)),
)


def place_of(row, col):
    if row >= 0 and col >= 0:
        return True, row * SIDE + col
    if col >= 0:
        return False, TOP + (row + HALF) * ACROSS + col
    if row >= 0:
        return False, LEFT + row * HALF + col + HALF
    return False, TL + (row + HALF) * HALF + col + HALF


def selectors():
    pack = np.zeros((MARGIN, CELLS), np.float32)
    for a in range(HALF):
        for b in range(ACROSS):
            pack[LEFT + b * HALF + a, b * SIDE + ACROSS + a] = 1
            pack[TOP + a * ACROSS + b, (ACROSS + a) * SIDE + b] = 1
        for b in range(HALF):
            pack[TL + a * HALF + b, (ACROSS + a) * SIDE + ACROSS + b] = 1
    gather = np.zeros((4, AREA, SRC), np.float32)
    spread = np.zeros((4, REACH + MARGIN, AREA), np.float32)
    spread_q = np.zeros((4, REACH + MARGIN, 2 * MAIN), np.float32)
    for w, (i, j) in enumerate(WINDOWS):
        where = {}
        at = 0
        for own, first, rows in SOURCES[w]:
            for row in range(rows):
                where.setdefault((own, first + row), at + row)
            at += rows
        for a in range(WIN):
            for b in range(WIN):
                own, spot = place_of(WIN * i - HALF + a, WIN * j - HALF + b)
                cell = a * WIN + b
                gather[w, cell, where[own, spot]] = 1
                to = spot if own else REACH + spot
                spread[w, to, cell] = 1
                for h in range(HEADS if cell >= MAIN else 1):
                    spread_q[w, to, cell + h * LATE] = 1
    return pack, gather, spread, spread_q


def nn(a, b):
    return jnp.dot(a, b, preferred_element_type=F32)


def nt(a, b):
    return lax.dot_general(a, b, (((1,), (1,)), ((), ())), preferred_element_type=F32)


def iota(shape, dim):
    return lax.broadcasted_iota(jnp.int32, shape, dim)


def normalize(x_ref, gain, into):
    step = 48 if x_ref.shape[0] % 48 == 0 else 16
    for first in range(0, x_ref.shape[0], step):
        here = pl.ds(first, step)
        x = x_ref[here, :].astype(F32)
        rms = lax.rsqrt(jnp.mean(x * x, axis=-1, keepdims=True) + NORM_EPS)
        into[here, :] = (x * rms * gain).astype(BF)


def each(first, last, act):
    def one(step, carry):
        act(step)
        return carry

    lax.fori_loop(first, last, one, 0)


def start(copies):
    for copy in copies:
        copy.start()


def wait(copies):
    for copy in copies:
        copy.wait()


class Links:
    def __init__(self, lats, lons, margin_sem, foot_sem):
        self.lats, self.lons, self.n = lats, lons, lats * lons
        self.lat, self.lon = lax.axis_index("lat"), lax.axis_index("lon")
        self.margin_sem, self.foot_sem = margin_sem, foot_sem
        self.barrier = pltpu.get_barrier_semaphore()

    def around(self, up, right):
        lats, lons = self.lats, self.lons
        return lax.rem(self.lat + up + lats, lats), lax.rem(self.lon + right + lons, lons)

    def away_by(self, d):
        return self.around(d // self.lons, d % self.lons)

    def greet(self, device):
        pl.semaphore_signal(self.barrier, inc=1, device_id=device, device_id_type=MESH)

    def others(self, act):
        steps = (self.n - 1) // 7

        def seven(k, carry):
            for j in range(7):
                act(1 + 7 * k + j)
            return carry

        lax.fori_loop(0, steps, seven, 0)
        for d in range(1 + 7 * steps, self.n):
            act(d)

    def greet_all(self):
        self.others(lambda d: self.greet(self.away_by(d)))

    def met_all(self):
        pl.semaphore_wait(self.barrier, self.n - 1)

    def copy(self, sems, i, src, dst, device):
        return pltpu.make_async_remote_copy(
            src_ref=src,
            dst_ref=dst,
            send_sem=sems.at[2 * i],
            recv_sem=sems.at[2 * i + 1],
            device_id=device,
            device_id_type=MESH,
        )

    def pieces(self, base, src, into, way):
        return [
            self.copy(
                self.margin_sem,
                base + i,
                src.at[pl.ds(first, rows)],
                into.at[pl.ds(first, rows)],
                self.around(way * up, way * right),
            )
            for i, (first, rows, up, right) in enumerate(PIECES)
        ]

    def arrived(self, into, i, parts):
        rest = into.at[pl.ds(1, parts - 1)]
        self.copy(self.foot_sem, i, rest, rest, self.around(1, 0)).wait()

    def to_all(self, send, into, i):
        self.others(
            lambda d: self.copy(self.foot_sem, i, send.at[d], into.at[d], self.away_by(d)).start()
        )
        into[0] = send[0]

    def along_lon(self, send, into, i, way):
        for step in range(1, self.lons):
            device = self.around(0, way * step)
            self.copy(self.foot_sem, i, send.at[:, step], into.at[step], device).start()
        into[0] = send[:, 0]

    def along_lat(self, send, into, i, way):
        for step in range(1, self.lats):
            device = self.around(way * step, 0)
            self.copy(self.foot_sem, i, send.at[:, step], into.at[step], device).start()
        into[0] = send[:, 0]


def footprint_places(links, tile_id, count, cap):
    lats, lons, n = links.lats, links.lons, links.n
    feet = tile_id.shape[1]
    tile_lat = jnp.floor((tile_id[...].astype(F32) + 0.5) * (1.0 / lons)).astype(jnp.int32)
    up, right = tile_lat - links.lat, tile_id[...] - tile_lat * lons - links.lon
    up, right = jnp.where(up < 0, up + lats, up), jnp.where(right < 0, right + lons, right)
    away = up * lons + right
    live = iota((1, feet), 1) < count[...]
    named = (iota((n, feet), 0) == away).astype(F32)
    before = (iota((feet, feet), 0) < iota((feet, feet), 1)).astype(F32).astype(BF)
    rank = jnp.sum(nn(named.astype(BF), before) * named, axis=0, keepdims=True).astype(jnp.int32)
    return away, rank, live, named


class Heads:
    def __init__(self, chans):
        self.even = (iota((1, 128), 1) < 64).astype(F32).astype(BF)
        self.odd = (iota((1, 128), 1) >= 64).astype(F32).astype(BF)
        late_head = iota((MAIN, chans), 0) >> 4 == iota((MAIN, chans), 1) >> 6
        self.late_head = late_head.astype(F32).astype(BF)

    def stacked(self, x):
        return jnp.concatenate([x * self.even, x * self.odd], axis=0)

    def late_rows(self, x):
        return jnp.concatenate([x] * HEADS, axis=0) * self.late_head

    def turned(self, qkv, w, first):
        return [pair_of(qkv, w, first, AREA, pair).T for pair in range(HEADS // 2)]

    def late_out(self, x, held):
        return nn(x.T, held).astype(BF) * self.late_head


def pair_of(ref, w, first, rows, pair):
    return ref[w, 0:rows, first + 128 * pair : first + 128 * (pair + 1)]


def gather_window(source, w, tile_ref, margin_ref):
    at = 0
    for own, first, count_rows in SOURCES[w]:
        piece = (tile_ref if own else margin_ref)[pl.ds(first, count_rows), :]
        source[w, pl.ds(at, count_rows), :] = piece
        at += count_rows


RETURNED = tuple(
    [(SIDE * row + ACROSS, HALF, LEFT + HALF * row) for row in range(ACROSS)]
    + [(REACH + SIDE * row, ACROSS, TOP + ACROSS * row) for row in range(HALF)]
    + [(REACH + SIDE * row + ACROSS, HALF, TL + HALF * row) for row in range(HALF)]
)


def to_targets(selector, per_window, which):
    first, count_rows, windows = TARGETS[which]
    total = None
    for w in windows:
        part = per_window(selector[w, pl.ds(first, count_rows), :], w)
        total = part if total is None else total + part
    return total


def kernel(
    lats,
    lons,
    cap,
    state_hbm,
    gain_hbm,
    w_in_hbm,
    w_out_hbm,
    obs_in_hbm,
    obs_out_hbm,
    observed_hbm,
    scale_hbm,
    tile_id_hbm,
    cell_id_hbm,
    count_hbm,
    pack_hbm,
    gather_hbm,
    spread_hbm,
    spread_q_hbm,
    own_part_hbm,
    back_part_hbm,
    misfit_hbm,
    state,
    observed,
    pack_m,
    gain,
    scale,
    tile_id,
    cell_id,
    count,
    misfit,
    w_in,
    w_out,
    obs_in,
    obs_out,
    gather_m,
    spread_m,
    spread_q_m,
    packed,
    margin,
    own_n,
    margin_n,
    source,
    win,
    qkv,
    apart,
    probs,
    att_w,
    att_send,
    att_recv,
    attended,
    block_out,
    obs_send,
    obs_recv,
    idx_send,
    idx_mid,
    idx_recv,
    mis_send,
    mis_mid,
    mis_recv,
    chosen,
    silu_grad,
    hidden,
    predicted,
    residuals,
    foot_grad,
    onehot,
    back,
    back_packed,
    state_grad,
    att_grad,
    packed_g,
    margin_g,
    dk_w,
    dv_w,
    dq_w,
    keys_t,
    proj_grad,
    part_send,
    part_recv,
    own_part,
    margin_sem,
    foot_sem,
    fetch_sem,
    store_sem,
):
    links = Links(lats, lons, margin_sem, foot_sem)
    n = links.n
    slots = n * cap
    feet = tile_id.shape[1]
    chans = state.shape[1]
    fetches = [
        pltpu.make_async_copy(src, dst, fetch_sem.at[i])
        for i, (src, dst) in enumerate(
            (
                (gather_hbm, gather_m),
                (w_in_hbm, w_in),
                (spread_q_hbm, spread_q_m),
                (w_out_hbm, w_out),
                (obs_in_hbm, obs_in),
                (obs_out_hbm, obs_out),
                (spread_hbm, spread_m),
                (state_hbm, state),
                (pack_hbm, pack_m),
                (observed_hbm, observed),
                (gain_hbm, gain),
                (scale_hbm, scale),
                (tile_id_hbm, tile_id),
                (cell_id_hbm, cell_id),
                (count_hbm, count),
            )
        )
    ]
    start(fetches[7:9])
    links.greet_all()
    start(fetches[9:])
    start(fetches[:7])
    wait(fetches[7:9])

    packed[...] = nn(pack_m[...], state[...]).astype(BF)

    links.met_all()
    state_copies = links.pieces(0, packed, margin, 1)
    start(state_copies)

    wait(fetches[10:])
    away, rank, live, named = footprint_places(links, tile_id, count, cap)
    slot = jnp.where(live, away * cap + rank, -1)
    cell_value = (cell_id[...] + 1).astype(F32)
    on_lane = iota((4, cap, 128), 2) == iota((4, cap, 128), 1)
    cells = []
    for first in range(0, slots, 4 * cap):
        block = (iota((4 * cap, feet), 0) + first == slot).astype(F32)
        chosen[pl.ds(first, 4 * cap), :] = block.astype(BF)
        cell = jnp.sum(block * cell_value, axis=1, keepdims=True) - 1.0
        cell = jnp.where(on_lane, cell.reshape(4, cap, 1), 0.0)
        cells.append(jnp.sum(cell, axis=1, keepdims=True))
    idx_send[...] = jnp.concatenate(cells, axis=0).reshape(lats, lons, 1, 128)
    links.along_lon(idx_send, idx_mid, 0, 1)
    fetches[9].wait()
    rows = nn(chosen[...], observed[...])
    half = rows.shape[1] // 2
    rows = rows.reshape(n, cap, 2 * half)
    obs_send[...] = jnp.concatenate([rows[:, :, :half], rows[:, :, half:]], axis=1).astype(BF)

    links.to_all(obs_send, obs_recv, 1)

    normalize(state, gain[...], own_n)

    def place(windows):
        for w in windows:
            win[w] = nn(gather_m[w], source[w]).astype(BF)

    def project(first, last):
        cells = win[first:last].reshape((last - first) * AREA, chans)
        for part in range(3):
            cols = slice(part * chans, (part + 1) * chans)
            out = nn(cells, w_in[:, cols])
            out = (out * 0.125 if part == 0 else out).astype(BF)
            qkv[first:last, :, cols] = out.reshape(last - first, AREA, chans)

    heads = Heads(chans)

    def softmax(scores):
        e = jnp.exp(scores - jnp.max(scores, axis=0, keepdims=True))
        return e * (1.0 / jnp.sum(e, axis=0, keepdims=True))

    def forward(w):
        row = jnp.where(w < 2, 0, 1)
        late = heads.late_rows(qkv[w, MAIN:AREA, 0:chans])
        values_t = heads.turned(qkv, w, 2 * chans)

        def scored(pair):
            if pair < HEADS // 2:
                queries = heads.stacked(pair_of(qkv, w, 0, MAIN, pair))
                return nt(pair_of(qkv, w, chans, AREA, pair), queries)
            return nt(qkv[w, :, chans : 2 * chans], late)

        after = scored(0)
        for pair in range(HEADS // 2):
            scores, after = after, scored(pair + 1)
            out = []
            for h in range(2):
                lanes = slice(MAIN * h, MAIN * (h + 1))
                p = softmax(scores[:, lanes] + apart[row, :, lanes])
                probs[w, :, 256 * pair + MAIN * h : 256 * pair + MAIN * (h + 1)] = p
                out.append(nn(values_t[pair][64 * h : 64 * h + 64], p.astype(BF)))
            out = jnp.concatenate(out, axis=0).astype(BF)
            att_w[w, 0:MAIN, 128 * pair : 128 * (pair + 1)] = out.T
        p = softmax(after + apart[row, :, 2 * MAIN :])
        probs[w, :, MAIN * HEADS :] = p
        att_w[w, MAIN : 2 * MAIN, :] = heads.late_out(p.astype(BF), qkv[w, :, 2 * chans :])

    first_rows = jnp.where(links.lat == 0, AREA // 2, 0)
    lane = iota((AREA, 3 * MAIN), 1)
    query = jnp.where(lane < 2 * MAIN, lane & (MAIN - 1), MAIN)
    seen_apart = (iota((AREA, 3 * MAIN), 0) < first_rows) != (query < first_rows)
    apart[0] = jnp.where(seen_apart, -1e30, 0.0)
    apart[1] = jnp.zeros((AREA, 3 * MAIN), F32)

    def att_wo(which):
        return to_targets(spread_q_m, lambda m, w: nn(m, att_w[w]), which)

    gather_window(source, 3, own_n, margin_n)
    fetches[0].wait()
    fetches[1].wait()
    place((3,))
    project(3, 4)
    wait(state_copies)
    normalize(margin, gain[...], margin_n)
    for w in range(3):
        gather_window(source, w, own_n, margin_n)
    place(range(3))
    project(0, 3)
    fetches[2].wait()
    links.arrived(idx_mid, 0, lons)
    links.along_lat(idx_mid, idx_recv, 3, 1)
    att_copies = links.pieces(3, att_send, att_recv, -1)

    def forward_step(w, carry):
        for at, targets, some in ((2, (3, 4), att_copies[1:]), (3, (2,), att_copies[:1])):

            @pl.when(w == at)
            def _():
                for which in targets:
                    first, count_rows, _ = TARGETS[which]
                    att_send[pl.ds(first - REACH, count_rows), :] = att_wo(which).astype(BF)
                start(some)

        forward(w)
        return carry

    lax.fori_loop(0, 4, forward_step, 0)
    for which in (0, 1):
        first, count_rows, _ = TARGETS[which]
        attended[pl.ds(first, count_rows), :] = att_wo(which)

    links.arrived(idx_recv, 3, lats)
    on_lane = iota((n, cap, 128), 2) == iota((n, cap, 128), 1)
    spots = jnp.where(on_lane, idx_recv[...].reshape(n, 1, 128), 0.0)
    spots = jnp.sum(spots, axis=2, keepdims=True).reshape(slots, 1)
    pick = (iota((8, 128), 1) == 0).astype(F32)
    spots_row = lax.dot_general(
        pick,
        jnp.broadcast_to(spots, (slots, 128)),
        (((1,), (1,)), ((), ())),
        precision=lax.Precision.HIGHEST,
        preferred_element_type=F32,
    )[0:1].astype(jnp.int32)
    spots = spots.astype(jnp.int32)
    for first in range(0, slots, 32):
        block = iota((32, CELLS), 1) == spots[first : first + 32]
        onehot[pl.ds(first, 32), :] = block.astype(F32).astype(BF)
    for first in range(0, CELLS, 16):
        block = iota((16, slots), 0) + first == spots_row
        back[pl.ds(first, 16), :] = block.astype(F32).astype(BF)
    back_packed[...] = nn(pack_m[...], back[...]).astype(BF)
    chunk = slots // 2
    per_scale = 1.0 / scale[...]
    wait(fetches[3:7])
    wait(att_copies)
    returned = att_recv[...].astype(F32)
    for first, count_rows, at in RETURNED:
        attended[pl.ds(first, count_rows), :] = returned[at : at + count_rows]
    block_out[...] = (
        state[...].astype(F32) + nn(attended[...].astype(BF), w_out[...])
    ).astype(BF)

    step = min(chunk, 64)
    quarters = [slice(256 * i, 256 * (i + 1)) for i in range(obs_in.shape[1] // 256)]

    def predict(c, carry):
        base = pl.multiple_of(c * chunk, chunk)
        here = pl.ds(base, chunk)
        features = nn(onehot[here, :], block_out[...]).astype(BF)
        for cols in quarters:
            whole = nn(features, obs_in[:, cols])
            for first in range(0, chunk, step):
                pre = whole[first : first + step]
                sig = 0.5 + 0.5 * jnp.tanh(0.5 * pre)
                out = pre * sig
                some = pl.ds(base + first, step)
                hidden[some, cols] = out.astype(BF)
                silu_grad[some, cols] = sig + out * (1.0 - sig)
        predicted[here, :] = nn(hidden[here, :], obs_out[...])
        return carry

    def observe(c, carry):
        base = pl.multiple_of(c * chunk, chunk)
        here = pl.ds(base, chunk)
        lanes = iota((step // cap, cap, 128), 2) == iota((step // cap, cap, 128), 1)
        costs = []
        for first in range(0, chunk, step):
            seen = obs_recv[pl.ds(c * (n // 2) + first // cap, step // cap)].astype(F32)
            seen = jnp.concatenate(
                [seen[:, :cap].reshape(step, half), seen[:, cap:].reshape(step, half)], axis=1
            )
            some = pl.ds(base + first, step)
            residual = (predicted[some, :] - seen) * per_scale
            residuals[some, :] = (residual * per_scale).astype(BF)
            cost = 0.5 * jnp.sum(residual * residual, axis=1, keepdims=True)
            cost = jnp.where(lanes, cost.reshape(step // cap, cap, 1), 0.0)
            costs.append(jnp.sum(cost, axis=1, keepdims=True))
        blocks = pl.ds(c * (lats // 2), lats // 2)
        mis_send[blocks] = jnp.concatenate(costs, axis=0).reshape(lats // 2, lons, 1, 128)
        for cols in quarters:
            whole = nt(residuals[here, :], obs_out[cols, :])
            for first in range(0, chunk, step):
                some = pl.ds(base + first, step)
                grad = whole[first : first + step] * silu_grad[some, cols]
                hidden[some, cols] = grad.astype(BF)
        foot_grad[here, :] = nt(hidden[here, :], obs_in[...]).astype(BF)
        return carry

    lax.fori_loop(0, 2, predict, 0)
    links.arrived(obs_recv, 1, n)
    lax.fori_loop(0, 2, observe, 0)

    to_send = nn(back_packed[...], foot_grad[...]).astype(BF)
    packed_g[...] = nt(to_send, w_out[...]).astype(BF)
    grad_copies = links.pieces(6, packed_g, margin_g, 1)
    start(grad_copies)
    links.along_lon(mis_send, mis_mid, 2, -1)
    state_grad[...] = nn(back[...], foot_grad[...])
    att_grad[...] = nt(state_grad[pl.ds(0, REACH), :].astype(BF), w_out[...]).astype(BF)

    def turn_keys(w, carry):
        keys_t[w] = jnp.concatenate(heads.turned(qkv, w, chans), axis=0)
        return carry

    lax.fori_loop(0, 4, turn_keys, 0)

    def scores_gradient(p, dp):
        inner = jnp.sum(p * dp, axis=0, keepdims=True)
        return (p * (dp - inner)).astype(BF)

    def backward(w):
        late_q = heads.late_rows(qkv[w, MAIN:AREA, 0:chans])
        late_up = heads.late_rows(win[w, MAIN:AREA, :])
        ups = [heads.stacked(pair_of(win, w, 0, MAIN, pair)) for pair in range(HEADS // 2)]

        def dp_of(pair):
            if pair == HEADS // 2:
                return None
            return nt(pair_of(qkv, w, 2 * chans, AREA, pair), ups[pair])

        after = dp_of(0)
        dp = nt(qkv[w, :, 2 * chans : 3 * chans], late_up)
        p = probs[w, :, MAIN * HEADS :]
        ds = scores_gradient(p, dp)
        late_dk = nn(ds, late_q)
        late_dv = nn(p.astype(BF), late_up)
        late_dq = heads.late_out(ds, qkv[w, :, chans : 2 * chans])
        dq_w[w, MAIN : 2 * MAIN, :] = late_dq * jnp.bfloat16(0.125)
        for pair in range(HEADS // 2):
            at = 128 * pair
            dp, after = after, dp_of(pair + 1)
            ds, rounded, out = [], [], []
            for h in range(2):
                p = probs[w, :, at * 2 + MAIN * h : at * 2 + MAIN * (h + 1)]
                ds.append(scores_gradient(p, dp[:, MAIN * h : MAIN * (h + 1)]))
                rounded.append(p.astype(BF))
                out.append(nn(keys_t[w, at + 64 * h : at + 64 * h + 64, :], ds[h]))
            out = (jnp.concatenate(out, axis=0) * 0.125).astype(BF)
            dq_w[w, 0:MAIN, at : at + 128] = out.T
            dk = nn(
                jnp.concatenate(ds, axis=1), heads.stacked(pair_of(qkv, w, 0, MAIN, pair))
            )
            dv = nn(jnp.concatenate(rounded, axis=1), ups[pair])
            dk_w[w, :, at : at + 128] = (dk + late_dk[:, at : at + 128]).astype(BF)
            dv_w[w, :, at : at + 128] = (dv + late_dv[:, at : at + 128]).astype(BF)

    def project_back(targets):
        for which in targets:
            first, count_rows, _ = TARGETS[which]
            here = pl.ds(first, count_rows)
            proj_grad[here, 0:chans] = to_targets(
                spread_q_m, lambda m, w: nn(m, dq_w[w]), which
            ).astype(BF)
            proj_grad[here, chans : 2 * chans] = to_targets(
                spread_m, lambda m, w: nn(m, dk_w[w]), which
            ).astype(BF)
            proj_grad[here, 2 * chans : 3 * chans] = to_targets(
                spread_m, lambda m, w: nn(m, dv_w[w]), which
            ).astype(BF)

    def norm_part(first, rows, cells, at, into, more=None):
        whole = nt(proj_grad[pl.ds(first, rows), :], w_in[...])
        step = 48 if rows % 48 == 0 else 16
        for row in range(0, rows, step):
            here = pl.ds(at + row, step)
            g = gain[...] * whole[row : row + step]
            x = cells[here, :].astype(F32)
            rms = lax.rsqrt(jnp.mean(x * x, axis=-1, keepdims=True) + NORM_EPS)
            inner = jnp.mean(x * g, axis=-1, keepdims=True)
            out = rms * g - x * (rms * rms * rms * inner)
            into[here, :] = out.astype(BF) if more is None else more[here, :] + out

    part_copies = links.pieces(9, part_send, part_recv, -1)
    gather_window(source, 3, att_grad, margin_g)
    place((3,))

    def backward_step(step, carry):
        @pl.when(step == 1)
        def _():
            wait(grad_copies)
            for w in range(3):
                gather_window(source, w, att_grad, margin_g)
            place(range(3))

        @pl.when(step == 2)
        def _():
            links.arrived(mis_mid, 2, lons)
            links.along_lat(mis_mid, mis_recv, 4, -1)

        @pl.when(step == 3)
        def _():
            project_back((3, 4))
            norm_part(REACH + TOP, MARGIN - TOP, margin, TOP, part_send)
            start(part_copies[1:])

        backward(lax.rem(step + 3, 4))
        return carry

    lax.fori_loop(0, 4, backward_step, 0)

    project_back((2,))
    norm_part(REACH + LEFT, SIDES, margin, LEFT, part_send)
    start(part_copies[:1])
    project_back((0, 1))
    norm_part(0, REACH, state, 0, own_part, state_grad)
    own_part[pl.ds(REACH, STRIP), :] = state_grad[pl.ds(REACH, STRIP), :]
    own_store = pltpu.make_async_copy(own_part, own_part_hbm, store_sem.at[0])
    own_store.start()

    links.arrived(mis_recv, 4, lats)
    costs = lax.dot_general(
        mis_recv[...].reshape(n, 128),
        named,
        (((0,), (0,)), ((), ())),
        precision=lax.Precision.HIGHEST,
        preferred_element_type=F32,
    )
    costs = jnp.where(iota((128, feet), 0) == rank, costs, 0.0)
    misfit[...] = jnp.where(live, jnp.sum(costs, axis=0, keepdims=True), 0.0)
    misfit_store = pltpu.make_async_copy(misfit, misfit_hbm, store_sem.at[2])
    misfit_store.start()
    wait(part_copies)
    back_store = pltpu.make_async_copy(part_recv, back_part_hbm, store_sem.at[1])
    back_store.start()
    wait([own_store, misfit_store, back_store])


def finish(own_hbm, back_hbm, costs_hbm, gradient, misfit, whole, back, costs, sems):
    rows = CELLS // 6
    parts = [pl.ds(first, rows) for first in range(0, CELLS, rows)]
    ins = [pltpu.make_async_copy(own_hbm.at[p], whole.at[p], sems.at[i]) for i, p in enumerate(parts)]
    outs = [
        pltpu.make_async_copy(whole.at[p], gradient.at[p], sems.at[6 + i]) for i, p in enumerate(parts)
    ]
    more = [
        pltpu.make_async_copy(back_hbm, back, sems.at[12]),
        pltpu.make_async_copy(costs_hbm, costs, sems.at[13]),
    ]
    out = pltpu.make_async_copy(costs, misfit, sems.at[14])
    start(more)
    start(ins)
    wait(more)
    out.start()
    returned = back[...].astype(F32)
    for i in range(6):
        ins[i].wait()
        for first, count_rows, at in RETURNED:
            if first // rows == i:
                whole[pl.ds(first, count_rows), :] += returned[at : at + count_rows]
        outs[i].start()
    wait(outs)
    out.wait()


def shards(
    lats,
    lons,
    initial_state,
    norm_gain,
    input_weight,
    output_weight,
    obs_in_weight,
    obs_out_weight,
    observed,
    error_scale,
    foot_tile,
    foot_cell,
    foot_count,
):
    n = lats * lons
    chans = initial_state.shape[-1]
    feet, seen = observed.shape
    cap = 2 * feet // n
    slots = n * cap
    pack, gather, spread, spread_q = (jnp.asarray(m, BF) for m in selectors())
    whole = pl.BlockSpec(memory_space=pl.ANY)
    state = initial_state.reshape(CELLS, chans)
    gain = norm_gain.reshape(1, chans)
    tile_id = foot_tile.reshape(1, feet)
    count = foot_count.reshape(1, 1)
    limit = 60 * 1024 * 1024

    def shape(*dims, dtype=BF):
        return jax.ShapeDtypeStruct(dims, dtype)

    def room(*dims, dtype=BF):
        return pltpu.VMEM(dims, dtype)

    own_part, back_part, costs = pl.pallas_call(
        functools.partial(kernel, lats, lons, cap),
        out_shape=(
            shape(CELLS, chans, dtype=F32),
            shape(MARGIN, chans),
            shape(1, feet, dtype=F32),
        ),
        in_specs=[whole] * 15,
        out_specs=(whole,) * 3,
        scratch_shapes=[
            room(CELLS, chans),
            room(feet, seen),
            room(MARGIN, CELLS),
            room(1, chans, dtype=F32),
            room(1, seen, dtype=F32),
            room(1, feet, dtype=jnp.int32),
            room(1, feet, dtype=jnp.int32),
            room(1, 1, dtype=jnp.int32),
            room(1, feet, dtype=F32),
            room(*input_weight.shape),
            room(*output_weight.shape),
            room(*obs_in_weight.shape),
            room(*obs_out_weight.shape),
            room(*gather.shape),
            room(*spread.shape),
            room(*spread_q.shape),
            room(MARGIN, chans),
            room(MARGIN, chans),
            room(CELLS, chans),
            room(MARGIN, chans),
            room(4, SRC, chans),
            room(4, AREA, chans),
            room(4, AREA, 3 * chans),
            room(2, AREA, 3 * MAIN, dtype=F32),
            room(4, AREA, MAIN * (HEADS + 1), dtype=F32),
            room(4, 2 * MAIN, chans),
            room(MARGIN, chans),
            room(MARGIN, chans),
            room(CELLS, chans, dtype=F32),
            room(CELLS, chans),
            room(n, 2 * cap, seen // 2),
            room(n, 2 * cap, seen // 2),
            room(lats, lons, 1, 128, dtype=F32),
            room(lons, lats, 1, 128, dtype=F32),
            room(lats, lons, 1, 128, dtype=F32),
            room(lats, lons, 1, 128, dtype=F32),
            room(lons, lats, 1, 128, dtype=F32),
            room(lats, lons, 1, 128, dtype=F32),
            room(slots, feet),
            room(slots, obs_in_weight.shape[1], dtype=F32),
            room(slots, obs_in_weight.shape[1]),
            room(slots, seen, dtype=F32),
            room(slots, seen),
            room(slots, chans),
            room(slots, CELLS),
            room(CELLS, slots),
            room(MARGIN, slots),
            room(CELLS, chans, dtype=F32),
            room(REACH, chans),
            room(MARGIN, chans),
            room(MARGIN, chans),
            room(4, AREA, chans),
            room(4, AREA, chans),
            room(4, 2 * MAIN, chans),
            room(4, chans, AREA),
            room(REACH + MARGIN, 3 * chans),
            room(MARGIN, chans),
            room(MARGIN, chans),
            room(CELLS, chans, dtype=F32),
            pltpu.SemaphoreType.DMA((24,)),
            pltpu.SemaphoreType.DMA((10,)),
            pltpu.SemaphoreType.DMA((15,)),
            pltpu.SemaphoreType.DMA((3,)),
        ],
        compiler_params=pltpu.CompilerParams(
            collective_id=0, has_side_effects=True, vmem_limit_bytes=limit
        ),
    )(
        state,
        gain,
        input_weight,
        output_weight,
        obs_in_weight,
        obs_out_weight,
        observed,
        error_scale.reshape(1, seen),
        tile_id,
        foot_cell.reshape(1, feet),
        count,
        pack,
        gather,
        spread,
        spread_q,
    )
    gradient, misfit = pl.pallas_call(
        finish,
        out_shape=(shape(CELLS, chans, dtype=F32), shape(1, feet, dtype=F32)),
        in_specs=[whole] * 3,
        out_specs=(whole, whole),
        scratch_shapes=[
            room(CELLS, chans, dtype=F32),
            room(MARGIN, chans),
            room(1, feet, dtype=F32),
            pltpu.SemaphoreType.DMA((15,)),
        ],
    )(own_part, back_part, costs)
    return gradient.reshape(initial_state.shape), misfit.reshape(feet)


def solution(mesh):
    both = ("lat", "lon")
    placed = (
        P("lat", "lon", None),
        P(),
        P(),
        P(),
        P(),
        P(),
        P(both, None),
        P(),
        P(both, None),
        P(both),
        P(both),
    )
    return jax.shard_map(
        functools.partial(shards, mesh.shape["lat"], mesh.shape["lon"]),
        mesh=mesh,
        in_specs=placed,
        out_specs=(P("lat", "lon", None), P(both)),
        check_vma=False,
    )
```

```python
import functools
import math

import jax
import jax.numpy as jnp
import numpy as np
from jax import lax
from jax.experimental import pallas as pl
from jax.experimental.pallas import tpu as pltpu
from jax.sharding import PartitionSpec as P

HEADS = 8
WIN = 12
HALF = WIN // 2
SIDE = 2 * WIN
CELLS = SIDE * SIDE
AREA = WIN * WIN
STRIP = HALF * SIDE
MAIN = 128
LATE = AREA - MAIN
SRC = 384
NORM_EPS = 1e-06
MESH = pl.DeviceIdType.MESH
BF = jnp.bfloat16
F32 = jnp.float32

WINDOWS = ((0, 0), (0, 1), (1, 0), (1, 1))
REACH = 3 * STRIP
ACROSS = SIDE - HALF
SIDES, CORNER = 112, 48
LEFT, TOP, TL = 0, SIDES, 2 * SIDES
MARGIN = 2 * SIDES + CORNER
PIECES = ((LEFT, SIDES, 0, 1), (TOP, SIDES, 1, 0), (TL, CORNER, 1, 1))
SOURCES = (
    ((True, 0, 176), (False, TOP, SIDES), (False, LEFT, 48), (False, TL, CORNER)),
    ((True, 0, 272), (False, TOP, SIDES)),
    ((True, 144, 288), (False, LEFT + 32, 80), (True, 0, 16)),
    ((True, 144, 288), (True, 0, 96)),
)
TARGETS = (
    (0, STRIP, (0, 1)),
    (STRIP, 2 * STRIP, (2, 3)),
    (REACH + LEFT, SIDES, (0, 2)),
    (REACH + TOP, SIDES, (0, 1)),
    (REACH + TL, CORNER, (0,)),
)


def place_of(row, col):
    if row >= 0 and col >= 0:
        return True, row * SIDE + col
    if col >= 0:
        return False, TOP + (row + HALF) * ACROSS + col
    if row >= 0:
        return False, LEFT + row * HALF + col + HALF
    return False, TL + (row + HALF) * HALF + col + HALF


def selectors():
    pack = np.zeros((MARGIN, CELLS), np.float32)
    for a in range(HALF):
        for b in range(ACROSS):
            pack[LEFT + b * HALF + a, b * SIDE + ACROSS + a] = 1
            pack[TOP + a * ACROSS + b, (ACROSS + a) * SIDE + b] = 1
        for b in range(HALF):
            pack[TL + a * HALF + b, (ACROSS + a) * SIDE + ACROSS + b] = 1
    gather = np.zeros((4, AREA, SRC), np.float32)
    spread = np.zeros((4, REACH + MARGIN, AREA), np.float32)
    spread_q = np.zeros((4, REACH + MARGIN, 2 * MAIN), np.float32)
    for w, (i, j) in enumerate(WINDOWS):
        where = {}
        at = 0
        for own, first, rows in SOURCES[w]:
            for row in range(rows):
                where.setdefault((own, first + row), at + row)
            at += rows
        for a in range(WIN):
            for b in range(WIN):
                own, spot = place_of(WIN * i - HALF + a, WIN * j - HALF + b)
                cell = a * WIN + b
                gather[w, cell, where[own, spot]] = 1
                to = spot if own else REACH + spot
                spread[w, to, cell] = 1
                for h in range(HEADS if cell >= MAIN else 1):
                    spread_q[w, to, cell + h * LATE] = 1
    return pack, gather, spread, spread_q


def nn(a, b):
    return jnp.dot(a, b, preferred_element_type=F32)


def nt(a, b):
    return lax.dot_general(a, b, (((1,), (1,)), ((), ())), preferred_element_type=F32)


def iota(shape, dim):
    return lax.broadcasted_iota(jnp.int32, shape, dim)


def normalize(x_ref, gain, into):
    step = 48 if x_ref.shape[0] % 48 == 0 else 16
    for first in range(0, x_ref.shape[0], step):
        here = pl.ds(first, step)
        x = x_ref[here, :].astype(F32)
        rms = lax.rsqrt(jnp.mean(x * x, axis=-1, keepdims=True) + NORM_EPS)
        into[here, :] = (x * rms * gain).astype(BF)


def each(first, last, act):
    def one(step, carry):
        act(step)
        return carry

    lax.fori_loop(first, last, one, 0)


def start(copies):
    for copy in copies:
        copy.start()


def wait(copies):
    for copy in copies:
        copy.wait()


class Links:
    def __init__(self, lats, lons, margin_sem, foot_sem):
        self.lats, self.lons, self.n = lats, lons, lats * lons
        self.lat, self.lon = lax.axis_index("lat"), lax.axis_index("lon")
        self.margin_sem, self.foot_sem = margin_sem, foot_sem
        self.barrier = pltpu.get_barrier_semaphore()

    def around(self, up, right):
        lats, lons = self.lats, self.lons
        return lax.rem(self.lat + up + lats, lats), lax.rem(self.lon + right + lons, lons)

    def away_by(self, d):
        return self.around(lax.rem(d, self.lats), d // self.lats)

    def greet(self, device):
        pl.semaphore_signal(self.barrier, inc=1, device_id=device, device_id_type=MESH)

    def greet_all(self):
        each(1, self.n, lambda d: self.greet(self.away_by(d)))

    def met_all(self):
        pl.semaphore_wait(self.barrier, self.n - 1)

    def copy(self, sems, i, src, dst, device):
        return pltpu.make_async_remote_copy(
            src_ref=src,
            dst_ref=dst,
            send_sem=sems.at[2 * i],
            recv_sem=sems.at[2 * i + 1],
            device_id=device,
            device_id_type=MESH,
        )

    def pieces(self, base, src, into, way):
        return [
            self.copy(
                self.margin_sem,
                base + i,
                src.at[pl.ds(first, rows)],
                into.at[pl.ds(first, rows)],
                self.around(way * up, way * right),
            )
            for i, (first, rows, up, right) in enumerate(PIECES)
        ]

    def arrived(self, into, i, parts):
        rest = into.at[pl.ds(1, parts - 1)]
        self.copy(self.foot_sem, i, rest, rest, self.around(1, 0)).wait()

    def to_all(self, send, into, i):
        stride = 45 if math.gcd(45, self.n) == 1 else 1

        def one(k):
            d = lax.rem(k * stride, self.n)
            self.copy(self.foot_sem, i, send.at[d], into.at[d], self.away_by(d)).start()

        each(1, self.n, one)
        into[0] = send[0]

    def back_lat(self, send, into, i):
        each(
            1,
            self.lats,
            lambda step: self.copy(
                self.foot_sem, i, send.at[:, step], into.at[step], self.around(-step, 0)
            ).start(),
        )
        into[0] = send[:, 0]

    def back_lon(self, mid, into, i):
        each(
            1,
            self.lons,
            lambda step: self.copy(
                self.foot_sem, i, mid.at[:, step], into.at[step], self.around(0, -step)
            ).start(),
        )
        into[0] = mid[:, 0]


def footprint_places(links, tile_id, count, cap):
    lats, lons, n = links.lats, links.lons, links.n
    feet = tile_id.shape[1]
    tile_lat = jnp.floor((tile_id[...].astype(F32) + 0.5) * (1.0 / lons)).astype(jnp.int32)
    up, right = tile_lat - links.lat, tile_id[...] - tile_lat * lons - links.lon
    up, right = jnp.where(up < 0, up + lats, up), jnp.where(right < 0, right + lons, right)
    away = right * lats + up
    live = iota((1, feet), 1) < count[...]
    named = (iota((n, feet), 0) == away).astype(F32)
    before = (iota((feet, feet), 0) < iota((feet, feet), 1)).astype(F32).astype(BF)
    rank = jnp.sum(nn(named.astype(BF), before) * named, axis=0, keepdims=True).astype(jnp.int32)
    return away, rank, live, named


class Heads:
    def __init__(self, chans):
        self.even = (iota((1, 128), 1) < 64).astype(F32).astype(BF)
        self.odd = (iota((1, 128), 1) >= 64).astype(F32).astype(BF)
        late_head = iota((MAIN, chans), 0) >> 4 == iota((MAIN, chans), 1) >> 6
        self.late_head = late_head.astype(F32).astype(BF)

    def stacked(self, x):
        return jnp.concatenate([x * self.even, x * self.odd], axis=0)

    def late_rows(self, x):
        return jnp.concatenate([x] * HEADS, axis=0) * self.late_head

    def turned(self, qkv, w, first):
        return [pair_of(qkv, w, first, AREA, pair).T for pair in range(HEADS // 2)]

    def late_out(self, x, held):
        return nn(x.T, held).astype(BF) * self.late_head


def pair_of(ref, w, first, rows, pair):
    return ref[w, 0:rows, first + 128 * pair : first + 128 * (pair + 1)]


def gather_window(source, w, tile_ref, margin_ref):
    at = 0
    for own, first, count_rows in SOURCES[w]:
        piece = (tile_ref if own else margin_ref)[pl.ds(first, count_rows), :]
        source[w, pl.ds(at, count_rows), :] = piece
        at += count_rows


RETURNED = tuple(
    [(SIDE * row + ACROSS, HALF, LEFT + HALF * row) for row in range(ACROSS)]
    + [(REACH + SIDE * row, ACROSS, TOP + ACROSS * row) for row in range(HALF)]
    + [(REACH + SIDE * row + ACROSS, HALF, TL + HALF * row) for row in range(HALF)]
)


def to_targets(selector, per_window, which):
    first, count_rows, windows = TARGETS[which]
    total = None
    for w in windows:
        part = per_window(selector[w, pl.ds(first, count_rows), :], w)
        total = part if total is None else total + part
    return total


def kernel(
    lats,
    lons,
    cap,
    state_hbm,
    gain_hbm,
    w_in_hbm,
    w_out_hbm,
    obs_in_hbm,
    obs_out_hbm,
    observed_hbm,
    scale_hbm,
    tile_id_hbm,
    cell_id_hbm,
    count_hbm,
    pack_hbm,
    gather_hbm,
    spread_hbm,
    spread_q_hbm,
    own_part_hbm,
    back_part_hbm,
    misfit_hbm,
    state,
    observed,
    pack_m,
    gain,
    scale,
    tile_id,
    cell_id,
    count,
    misfit,
    w_in,
    w_out,
    obs_in,
    obs_out,
    gather_m,
    spread_m,
    spread_q_m,
    packed,
    margin,
    own_n,
    margin_n,
    source,
    win,
    qkv,
    apart,
    probs,
    att_w,
    att_send,
    att_recv,
    attended,
    block_out,
    obs_send,
    obs_recv,
    idx_send,
    idx_recv,
    mis_send,
    mis_mid,
    mis_recv,
    chosen,
    silu_grad,
    hidden,
    predicted,
    residuals,
    foot_grad,
    onehot,
    back,
    back_packed,
    state_grad,
    att_grad,
    packed_g,
    margin_g,
    dk_w,
    dv_w,
    dq_w,
    keys_t,
    proj_grad,
    part_send,
    part_recv,
    own_part,
    margin_sem,
    foot_sem,
    fetch_sem,
    store_sem,
):
    links = Links(lats, lons, margin_sem, foot_sem)
    n = links.n
    slots = n * cap
    feet = tile_id.shape[1]
    chans = state.shape[1]
    fetches = [
        pltpu.make_async_copy(src, dst, fetch_sem.at[i])
        for i, (src, dst) in enumerate(
            (
                (gather_hbm, gather_m),
                (w_in_hbm, w_in),
                (spread_q_hbm, spread_q_m),
                (w_out_hbm, w_out),
                (obs_in_hbm, obs_in),
                (obs_out_hbm, obs_out),
                (spread_hbm, spread_m),
                (state_hbm, state),
                (pack_hbm, pack_m),
                (observed_hbm, observed),
                (gain_hbm, gain),
                (scale_hbm, scale),
                (tile_id_hbm, tile_id),
                (cell_id_hbm, cell_id),
                (count_hbm, count),
            )
        )
    ]
    start(fetches[7:9])
    links.greet_all()
    start(fetches[9:])
    start(fetches[:7])
    wait(fetches[7:9])

    packed[...] = nn(pack_m[...], state[...]).astype(BF)

    links.met_all()
    state_copies = links.pieces(0, packed, margin, 1)
    start(state_copies)

    wait(fetches[10:])
    away, rank, live, named = footprint_places(links, tile_id, count, cap)
    slot = jnp.where(live, away * cap + rank, -1)
    cell_value = (cell_id[...] + 1).astype(F32)
    on_lane = iota((4, cap, 128), 2) == iota((4, cap, 128), 1)
    cells = []
    for first in range(0, slots, 4 * cap):
        block = (iota((4 * cap, feet), 0) + first == slot).astype(F32)
        chosen[pl.ds(first, 4 * cap), :] = block.astype(BF)
        cell = jnp.sum(block * cell_value, axis=1, keepdims=True) - 1.0
        cell = jnp.where(on_lane, cell.reshape(4, cap, 1), 0.0)
        cells.append(jnp.sum(cell, axis=1, keepdims=True))
    idx_send[...] = jnp.concatenate(cells, axis=0)
    fetches[9].wait()
    rows = nn(chosen[...], observed[...])
    half = rows.shape[1] // 2
    rows = rows.reshape(n, cap, 2 * half)
    obs_send[...] = jnp.concatenate([rows[:, :, :half], rows[:, :, half:]], axis=1).astype(BF)

    links.to_all(idx_send, idx_recv, 0)
    links.to_all(obs_send, obs_recv, 1)

    normalize(state, gain[...], own_n)

    def place(windows):
        for w in windows:
            win[w] = nn(gather_m[w], source[w]).astype(BF)

    def project(first, last):
        cells = win[first:last].reshape((last - first) * AREA, chans)
        for part in range(3):
            cols = slice(part * chans, (part + 1) * chans)
            out = nn(cells, w_in[:, cols])
            out = (out * 0.125 if part == 0 else out).astype(BF)
            qkv[first:last, :, cols] = out.reshape(last - first, AREA, chans)

    heads = Heads(chans)

    def softmax(scores):
        e = jnp.exp(scores - jnp.max(scores, axis=0, keepdims=True))
        return e * (1.0 / jnp.sum(e, axis=0, keepdims=True))

    def forward(w):
        row = jnp.where(w < 2, 0, 1)
        late = heads.late_rows(qkv[w, MAIN:AREA, 0:chans])
        values_t = heads.turned(qkv, w, 2 * chans)

        def scored(pair):
            if pair < HEADS // 2:
                queries = heads.stacked(pair_of(qkv, w, 0, MAIN, pair))
                return nt(pair_of(qkv, w, chans, AREA, pair), queries)
            return nt(qkv[w, :, chans : 2 * chans], late)

        after = scored(0)
        for pair in range(HEADS // 2):
            scores, after = after, scored(pair + 1)
            out = []
            for h in range(2):
                lanes = slice(MAIN * h, MAIN * (h + 1))
                p = softmax(scores[:, lanes] + apart[row, :, lanes])
                probs[w, :, 256 * pair + MAIN * h : 256 * pair + MAIN * (h + 1)] = p
                out.append(nn(values_t[pair][64 * h : 64 * h + 64], p.astype(BF)))
            out = jnp.concatenate(out, axis=0).astype(BF)
            att_w[w, 0:MAIN, 128 * pair : 128 * (pair + 1)] = out.T
        p = softmax(after + apart[row, :, 2 * MAIN :])
        probs[w, :, MAIN * HEADS :] = p
        att_w[w, MAIN : 2 * MAIN, :] = heads.late_out(p.astype(BF), qkv[w, :, 2 * chans :])

    first_rows = jnp.where(links.lat == 0, AREA // 2, 0)
    lane = iota((AREA, 3 * MAIN), 1)
    query = jnp.where(lane < 2 * MAIN, lane & (MAIN - 1), MAIN)
    seen_apart = (iota((AREA, 3 * MAIN), 0) < first_rows) != (query < first_rows)
    apart[0] = jnp.where(seen_apart, -1e30, 0.0)
    apart[1] = jnp.zeros((AREA, 3 * MAIN), F32)

    def att_wo(which):
        return to_targets(spread_q_m, lambda m, w: nn(m, att_w[w]), which)

    gather_window(source, 3, own_n, margin_n)
    fetches[0].wait()
    fetches[1].wait()
    place((3,))
    project(3, 4)
    wait(state_copies)
    normalize(margin, gain[...], margin_n)
    for w in range(3):
        gather_window(source, w, own_n, margin_n)
    place(range(3))
    project(0, 3)
    fetches[2].wait()
    att_copies = links.pieces(3, att_send, att_recv, -1)

    def forward_step(w, carry):
        for at, targets, some in ((2, (3, 4), att_copies[1:]), (3, (2,), att_copies[:1])):

            @pl.when(w == at)
            def _():
                for which in targets:
                    first, count_rows, _ = TARGETS[which]
                    att_send[pl.ds(first - REACH, count_rows), :] = att_wo(which).astype(BF)
                start(some)

        forward(w)
        return carry

    lax.fori_loop(0, 4, forward_step, 0)
    for which in (0, 1):
        first, count_rows, _ = TARGETS[which]
        attended[pl.ds(first, count_rows), :] = att_wo(which)

    links.arrived(idx_recv, 0, n)
    on_lane = iota((n, cap, 128), 2) == iota((n, cap, 128), 1)
    spots = jnp.where(on_lane, idx_recv[...], 0.0)
    spots = jnp.sum(spots, axis=2, keepdims=True).reshape(slots, 1)
    pick = (iota((8, 128), 1) == 0).astype(F32)
    spots_row = lax.dot_general(
        pick,
        jnp.broadcast_to(spots, (slots, 128)),
        (((1,), (1,)), ((), ())),
        precision=lax.Precision.HIGHEST,
        preferred_element_type=F32,
    )[0:1].astype(jnp.int32)
    spots = spots.astype(jnp.int32)
    for first in range(0, slots, 32):
        block = iota((32, CELLS), 1) == spots[first : first + 32]
        onehot[pl.ds(first, 32), :] = block.astype(F32).astype(BF)
    for first in range(0, CELLS, 16):
        block = iota((16, slots), 0) + first == spots_row
        back[pl.ds(first, 16), :] = block.astype(F32).astype(BF)
    back_packed[...] = nn(pack_m[...], back[...]).astype(BF)
    chunk = slots // 2
    per_scale = 1.0 / scale[...]
    wait(fetches[3:7])
    wait(att_copies)
    returned = att_recv[...].astype(F32)
    for first, count_rows, at in RETURNED:
        attended[pl.ds(first, count_rows), :] = returned[at : at + count_rows]
    block_out[...] = (
        state[...].astype(F32) + nn(attended[...].astype(BF), w_out[...])
    ).astype(BF)

    step = min(chunk, 64)
    quarters = [slice(256 * i, 256 * (i + 1)) for i in range(obs_in.shape[1] // 256)]

    def predict(c, carry):
        base = pl.multiple_of(c * chunk, chunk)
        here = pl.ds(base, chunk)
        features = nn(onehot[here, :], block_out[...]).astype(BF)
        for cols in quarters:
            whole = nn(features, obs_in[:, cols])
            for first in range(0, chunk, step):
                pre = whole[first : first + step]
                sig = 0.5 + 0.5 * jnp.tanh(0.5 * pre)
                out = pre * sig
                some = pl.ds(base + first, step)
                hidden[some, cols] = out.astype(BF)
                silu_grad[some, cols] = sig + out * (1.0 - sig)
        predicted[here, :] = nn(hidden[here, :], obs_out[...])
        return carry

    def observe(c, carry):
        base = pl.multiple_of(c * chunk, chunk)
        here = pl.ds(base, chunk)
        lanes = iota((step // cap, cap, 128), 2) == iota((step // cap, cap, 128), 1)
        costs = []
        for first in range(0, chunk, step):
            seen = obs_recv[pl.ds(c * (n // 2) + first // cap, step // cap)].astype(F32)
            seen = jnp.concatenate(
                [seen[:, :cap].reshape(step, half), seen[:, cap:].reshape(step, half)], axis=1
            )
            some = pl.ds(base + first, step)
            residual = (predicted[some, :] - seen) * per_scale
            residuals[some, :] = (residual * per_scale).astype(BF)
            cost = 0.5 * jnp.sum(residual * residual, axis=1, keepdims=True)
            cost = jnp.where(lanes, cost.reshape(step // cap, cap, 1), 0.0)
            costs.append(jnp.sum(cost, axis=1, keepdims=True))
        blocks = pl.ds(c * (lons // 2), lons // 2)
        mis_send[blocks] = jnp.concatenate(costs, axis=0).reshape(lons // 2, lats, 1, 128)
        for cols in quarters:
            whole = nt(residuals[here, :], obs_out[cols, :])
            for first in range(0, chunk, step):
                some = pl.ds(base + first, step)
                grad = whole[first : first + step] * silu_grad[some, cols]
                hidden[some, cols] = grad.astype(BF)
        foot_grad[here, :] = nt(hidden[here, :], obs_in[...]).astype(BF)
        return carry

    lax.fori_loop(0, 2, predict, 0)
    links.arrived(obs_recv, 1, n)
    lax.fori_loop(0, 2, observe, 0)

    to_send = nn(back_packed[...], foot_grad[...]).astype(BF)
    packed_g[...] = nt(to_send, w_out[...]).astype(BF)
    grad_copies = links.pieces(6, packed_g, margin_g, 1)
    start(grad_copies)
    links.back_lat(mis_send, mis_mid, 2)
    state_grad[...] = nn(back[...], foot_grad[...])
    att_grad[...] = nt(state_grad[pl.ds(0, REACH), :].astype(BF), w_out[...]).astype(BF)

    def turn_keys(w, carry):
        keys_t[w] = jnp.concatenate(heads.turned(qkv, w, chans), axis=0)
        return carry

    lax.fori_loop(0, 4, turn_keys, 0)

    def scores_gradient(p, dp):
        inner = jnp.sum(p * dp, axis=0, keepdims=True)
        return (p * (dp - inner)).astype(BF)

    def backward(w):
        late_q = heads.late_rows(qkv[w, MAIN:AREA, 0:chans])
        late_up = heads.late_rows(win[w, MAIN:AREA, :])
        ups = [heads.stacked(pair_of(win, w, 0, MAIN, pair)) for pair in range(HEADS // 2)]

        def dp_of(pair):
            if pair == HEADS // 2:
                return None
            return nt(pair_of(qkv, w, 2 * chans, AREA, pair), ups[pair])

        after = dp_of(0)
        dp = nt(qkv[w, :, 2 * chans : 3 * chans], late_up)
        p = probs[w, :, MAIN * HEADS :]
        ds = scores_gradient(p, dp)
        late_dk = nn(ds, late_q)
        late_dv = nn(p.astype(BF), late_up)
        late_dq = heads.late_out(ds, qkv[w, :, chans : 2 * chans])
        dq_w[w, MAIN : 2 * MAIN, :] = late_dq * jnp.bfloat16(0.125)
        for pair in range(HEADS // 2):
            at = 128 * pair
            dp, after = after, dp_of(pair + 1)
            ds, rounded, out = [], [], []
            for h in range(2):
                p = probs[w, :, at * 2 + MAIN * h : at * 2 + MAIN * (h + 1)]
                ds.append(scores_gradient(p, dp[:, MAIN * h : MAIN * (h + 1)]))
                rounded.append(p.astype(BF))
                out.append(nn(keys_t[w, at + 64 * h : at + 64 * h + 64, :], ds[h]))
            out = (jnp.concatenate(out, axis=0) * 0.125).astype(BF)
            dq_w[w, 0:MAIN, at : at + 128] = out.T
            dk = nn(
                jnp.concatenate(ds, axis=1), heads.stacked(pair_of(qkv, w, 0, MAIN, pair))
            )
            dv = nn(jnp.concatenate(rounded, axis=1), ups[pair])
            dk_w[w, :, at : at + 128] = (dk + late_dk[:, at : at + 128]).astype(BF)
            dv_w[w, :, at : at + 128] = (dv + late_dv[:, at : at + 128]).astype(BF)

    def project_back(targets):
        for which in targets:
            first, count_rows, _ = TARGETS[which]
            here = pl.ds(first, count_rows)
            proj_grad[here, 0:chans] = to_targets(
                spread_q_m, lambda m, w: nn(m, dq_w[w]), which
            ).astype(BF)
            proj_grad[here, chans : 2 * chans] = to_targets(
                spread_m, lambda m, w: nn(m, dk_w[w]), which
            ).astype(BF)
            proj_grad[here, 2 * chans : 3 * chans] = to_targets(
                spread_m, lambda m, w: nn(m, dv_w[w]), which
            ).astype(BF)

    def norm_part(first, rows, cells, at, into, more=None):
        whole = nt(proj_grad[pl.ds(first, rows), :], w_in[...])
        step = 48 if rows % 48 == 0 else 16
        for row in range(0, rows, step):
            here = pl.ds(at + row, step)
            g = gain[...] * whole[row : row + step]
            x = cells[here, :].astype(F32)
            rms = lax.rsqrt(jnp.mean(x * x, axis=-1, keepdims=True) + NORM_EPS)
            inner = jnp.mean(x * g, axis=-1, keepdims=True)
            out = rms * g - x * (rms * rms * rms * inner)
            into[here, :] = out.astype(BF) if more is None else more[here, :] + out

    part_copies = links.pieces(9, part_send, part_recv, -1)
    gather_window(source, 3, att_grad, margin_g)
    place((3,))

    def backward_step(step, carry):
        @pl.when(step == 1)
        def _():
            wait(grad_copies)
            for w in range(3):
                gather_window(source, w, att_grad, margin_g)
            place(range(3))

        @pl.when(step == 2)
        def _():
            links.arrived(mis_mid, 2, lats)
            links.back_lon(mis_mid, mis_recv, 3)

        @pl.when(step == 3)
        def _():
            project_back((3, 4))
            norm_part(REACH + TOP, MARGIN - TOP, margin, TOP, part_send)
            start(part_copies[1:])

        backward(lax.rem(step + 3, 4))
        return carry

    lax.fori_loop(0, 4, backward_step, 0)

    project_back((2,))
    norm_part(REACH + LEFT, SIDES, margin, LEFT, part_send)
    start(part_copies[:1])
    project_back((0, 1))
    norm_part(0, REACH, state, 0, own_part, state_grad)
    own_part[pl.ds(REACH, STRIP), :] = state_grad[pl.ds(REACH, STRIP), :]
    own_store = pltpu.make_async_copy(own_part, own_part_hbm, store_sem.at[0])
    own_store.start()

    links.arrived(mis_recv, 3, lons)
    costs = lax.dot_general(
        mis_recv[...].reshape(n, 128),
        named,
        (((0,), (0,)), ((), ())),
        precision=lax.Precision.HIGHEST,
        preferred_element_type=F32,
    )
    costs = jnp.where(iota((128, feet), 0) == rank, costs, 0.0)
    misfit[...] = jnp.where(live, jnp.sum(costs, axis=0, keepdims=True), 0.0)
    misfit_store = pltpu.make_async_copy(misfit, misfit_hbm, store_sem.at[2])
    misfit_store.start()
    wait(part_copies)
    back_store = pltpu.make_async_copy(part_recv, back_part_hbm, store_sem.at[1])
    back_store.start()
    wait([own_store, misfit_store, back_store])


def finish(own_hbm, back_hbm, costs_hbm, gradient, misfit, whole, back, costs, sems):
    rows = CELLS // 6
    parts = [pl.ds(first, rows) for first in range(0, CELLS, rows)]
    ins = [pltpu.make_async_copy(own_hbm.at[p], whole.at[p], sems.at[i]) for i, p in enumerate(parts)]
    outs = [
        pltpu.make_async_copy(whole.at[p], gradient.at[p], sems.at[6 + i]) for i, p in enumerate(parts)
    ]
    more = [
        pltpu.make_async_copy(back_hbm, back, sems.at[12]),
        pltpu.make_async_copy(costs_hbm, costs, sems.at[13]),
    ]
    out = pltpu.make_async_copy(costs, misfit, sems.at[14])
    start(more)
    start(ins)
    wait(more)
    out.start()
    returned = back[...].astype(F32)
    for i in range(6):
        ins[i].wait()
        for first, count_rows, at in RETURNED:
            if first // rows == i:
                whole[pl.ds(first, count_rows), :] += returned[at : at + count_rows]
        outs[i].start()
    wait(outs)
    out.wait()


def shards(
    lats,
    lons,
    initial_state,
    norm_gain,
    input_weight,
    output_weight,
    obs_in_weight,
    obs_out_weight,
    observed,
    error_scale,
    foot_tile,
    foot_cell,
    foot_count,
):
    n = lats * lons
    chans = initial_state.shape[-1]
    feet, seen = observed.shape
    cap = 2 * feet // n
    slots = n * cap
    pack, gather, spread, spread_q = (jnp.asarray(m, BF) for m in selectors())
    whole = pl.BlockSpec(memory_space=pl.ANY)
    state = initial_state.reshape(CELLS, chans)
    gain = norm_gain.reshape(1, chans)
    tile_id = foot_tile.reshape(1, feet)
    count = foot_count.reshape(1, 1)
    limit = 60 * 1024 * 1024

    def shape(*dims, dtype=BF):
        return jax.ShapeDtypeStruct(dims, dtype)

    def room(*dims, dtype=BF):
        return pltpu.VMEM(dims, dtype)

    own_part, back_part, costs = pl.pallas_call(
        functools.partial(kernel, lats, lons, cap),
        out_shape=(
            shape(CELLS, chans, dtype=F32),
            shape(MARGIN, chans),
            shape(1, feet, dtype=F32),
        ),
        in_specs=[whole] * 15,
        out_specs=(whole,) * 3,
        scratch_shapes=[
            room(CELLS, chans),
            room(feet, seen),
            room(MARGIN, CELLS),
            room(1, chans, dtype=F32),
            room(1, seen, dtype=F32),
            room(1, feet, dtype=jnp.int32),
            room(1, feet, dtype=jnp.int32),
            room(1, 1, dtype=jnp.int32),
            room(1, feet, dtype=F32),
            room(*input_weight.shape),
            room(*output_weight.shape),
            room(*obs_in_weight.shape),
            room(*obs_out_weight.shape),
            room(*gather.shape),
            room(*spread.shape),
            room(*spread_q.shape),
            room(MARGIN, chans),
            room(MARGIN, chans),
            room(CELLS, chans),
            room(MARGIN, chans),
            room(4, SRC, chans),
            room(4, AREA, chans),
            room(4, AREA, 3 * chans),
            room(2, AREA, 3 * MAIN, dtype=F32),
            room(4, AREA, MAIN * (HEADS + 1), dtype=F32),
            room(4, 2 * MAIN, chans),
            room(MARGIN, chans),
            room(MARGIN, chans),
            room(CELLS, chans, dtype=F32),
            room(CELLS, chans),
            room(n, 2 * cap, seen // 2),
            room(n, 2 * cap, seen // 2),
            room(n, 1, 128, dtype=F32),
            room(n, 1, 128, dtype=F32),
            room(lons, lats, 1, 128, dtype=F32),
            room(lats, lons, 1, 128, dtype=F32),
            room(lons, lats, 1, 128, dtype=F32),
            room(slots, feet),
            room(slots, obs_in_weight.shape[1], dtype=F32),
            room(slots, obs_in_weight.shape[1]),
            room(slots, seen, dtype=F32),
            room(slots, seen),
            room(slots, chans),
            room(slots, CELLS),
            room(CELLS, slots),
            room(MARGIN, slots),
            room(CELLS, chans, dtype=F32),
            room(REACH, chans),
            room(MARGIN, chans),
            room(MARGIN, chans),
            room(4, AREA, chans),
            room(4, AREA, chans),
            room(4, 2 * MAIN, chans),
            room(4, chans, AREA),
            room(REACH + MARGIN, 3 * chans),
            room(MARGIN, chans),
            room(MARGIN, chans),
            room(CELLS, chans, dtype=F32),
            pltpu.SemaphoreType.DMA((24,)),
            pltpu.SemaphoreType.DMA((8,)),
            pltpu.SemaphoreType.DMA((15,)),
            pltpu.SemaphoreType.DMA((3,)),
        ],
        compiler_params=pltpu.CompilerParams(
            collective_id=0, has_side_effects=True, vmem_limit_bytes=limit
        ),
    )(
        state,
        gain,
        input_weight,
        output_weight,
        obs_in_weight,
        obs_out_weight,
        observed,
        error_scale.reshape(1, seen),
        tile_id,
        foot_cell.reshape(1, feet),
        count,
        pack,
        gather,
        spread,
        spread_q,
    )
    gradient, misfit = pl.pallas_call(
        finish,
        out_shape=(shape(CELLS, chans, dtype=F32), shape(1, feet, dtype=F32)),
        in_specs=[whole] * 3,
        out_specs=(whole, whole),
        scratch_shapes=[
            room(CELLS, chans, dtype=F32),
            room(MARGIN, chans),
            room(1, feet, dtype=F32),
            pltpu.SemaphoreType.DMA((15,)),
        ],
    )(own_part, back_part, costs)
    return gradient.reshape(initial_state.shape), misfit.reshape(feet)


def solution(mesh):
    both = ("lat", "lon")
    placed = (
        P("lat", "lon", None),
        P(),
        P(),
        P(),
        P(),
        P(),
        P(both, None),
        P(),
        P(both, None),
        P(both),
        P(both),
    )
    return jax.shard_map(
        functools.partial(shards, mesh.shape["lat"], mesh.shape["lon"]),
        mesh=mesh,
        in_specs=placed,
        out_specs=(P("lat", "lon", None), P(both)),
        check_vma=False,
    )
```
